32 devices in a mesh: ctx: 8 (over z, x), tp: 4 (over y, core).
Axes of the slice: x: 2, y: 2, z: 4, core: 2. Of those that a mesh axis runs over, the one named last changes fastest.
Arguments:
- tokens: bfloat16 [6144, 4096], P('ctx'), may hold values from -6 to 6
- qkv_weight: bfloat16 [3, 4096, 4096], P(None, 'ctx', 'tp'), may hold values from -0.09375 to 0.09375
- short_filter: float32 [3, 7, 4096], P(None, None, 'tp'), may hold values from -2.4 to 2.4
- long_filter: float32 [256, 128], P('tp'), may hold values from -0.9 to 0.9
- decay_rate: float32 [256], P('tp'), may hold values from 0.004 to 0.2
- skip_gain: float32 [4096], P('tp'), may hold values from -3 to 3
- out_weight: bfloat16 [4096, 4096], P('tp', 'ctx'), may hold values from -0.09375 to 0.09375
Outputs:
- block_out: bfloat16 [6144, 4096], P(('ctx', 'tp'))
The draws below stay inside these ranges and needn't reach their ends.
All inputs are finite; a program needn't handle non-finite values.
Results may differ from the reference program's by a relative error of at most 0.008.
Values may be sent and summed in bfloat16 or wider, within the bound.
No kernel may reach another device: no remote copies, remote signals or barrier semaphores. Data moves between devices by JAX's collectives and lax.ppermute only.
A program may use at most 128 MiB of HBM per device.

```python
import math
import jax
import jax.numpy as jnp
from jax import lax

D = 4096
C = 4096
G = 16
TAPS = 128
SHORT = 7
TOKENS = 6144
GROUPS = 256


def steps_of(rng, dims, split, low, top_value):
    level, own = 1.0, jax.random.fold_in(rng, 6)
    for dim, shards_of in split:
        heights = jnp.exp(jax.random.uniform(jax.random.fold_in(own, dim), (shards_of,), jnp.float32, low / len(split), top_value / len(split)))
        level = level * jnp.repeat(heights, dims[dim] // shards_of).reshape([-1 if axis == dim else 1 for axis in range(len(dims))])
    return level


def bell_draw(stream_key, shape, scale, reach, split=(), kind=jnp.bfloat16):
    factor_of = steps_of(stream_key, shape, split, -0.22, 0.18) if split else 1.0
    values = jax.random.normal(stream_key, shape, jnp.float32) * scale * factor_of
    return jnp.minimum(jnp.maximum(values, -reach), reach).astype(kind)


def setup_inputs(seed: int = 0) -> dict:
    arg_keys = jax.random.split(jax.random.key(seed), 8)
    tokens = bell_draw(arg_keys[0], (TOKENS, D), 1.0, 6.0, ((0, 8),))
    qkv_weight = bell_draw(arg_keys[1], (3, D, C), D ** -0.5, 0.09375, ((1, 8), (2, 4)))
    short_filter = bell_draw(arg_keys[2], (3, SHORT, C), 0.4, 2.4, ((2, 4),), jnp.float32)
    long_filter = bell_draw(arg_keys[3], (GROUPS, TAPS), 0.15, 0.9, ((0, 4),), jnp.float32)
    decay_rate = jnp.clip(jnp.exp(math.log(0.2) - 3.912023 * jax.random.uniform(arg_keys[4], (GROUPS,), jnp.float32) ** steps_of(arg_keys[4], (GROUPS,), ((0, 4),), -0.2, 0.2)), 0.004, 0.2)
    skip_gain = bell_draw(arg_keys[5], (C,), 0.5, 3.0, ((0, 4),), jnp.float32)
    out_weight = bell_draw(arg_keys[6], (C, D), C ** -0.5, 0.09375, ((0, 4), (1, 8)))
    return {"tokens": tokens, "qkv_weight": qkv_weight, "short_filter": short_filter, "long_filter": long_filter, "decay_rate": decay_rate, "skip_gain": skip_gain, "out_weight": out_weight}


def reference(tokens, qkv_weight, short_filter, long_filter, decay_rate, skip_gain, out_weight):
    projected = jnp.stack([jnp.dot(tokens, qkv_weight[index], preferred_element_type=jnp.float32) for index in range(3)])
    qkv = projected.astype(jnp.bfloat16)
    padded = jnp.pad(qkv, ((0, 0), (SHORT - 1, 0), (0, 0)))
    features = short_filter[:, 0, None, :] * padded[:, SHORT - 1:, :]
    for offset in range(1, SHORT):
        start = SHORT - 1 - offset
        features = features + short_filter[:, offset, None, :] * padded[:, start:start + TOKENS, :]
    gated = (features[1] * features[2]).astype(jnp.bfloat16)
    tap_index = jnp.arange(TAPS, dtype=jnp.float32)
    filters = (long_filter * jnp.exp(-decay_rate[:, None] * tap_index[None, :])).astype(jnp.bfloat16)
    per_tap = jnp.repeat(filters, G, axis=0).astype(jnp.float32).T
    gated_wide = gated.astype(jnp.float32)
    gated_pad = jnp.pad(gated_wide, ((TAPS - 1, 0), (0, 0)))

    def add_tap(step, total):
        step_int = jnp.asarray(step).astype(jnp.int32)
        weights = lax.dynamic_index_in_dim(per_tap, step_int, 0, keepdims=False)
        window = lax.dynamic_slice_in_dim(gated_pad, (TAPS - 1 - step_int).astype(jnp.int32), TOKENS, 0)
        return total + weights[None, :] * window

    filtered = lax.fori_loop(0, TAPS, add_tap, jnp.zeros((TOKENS, C), jnp.float32))
    mixed = (features[0] * (filtered + skip_gain[None, :] * gated_wide)).astype(jnp.bfloat16)
    return jnp.dot(mixed, out_weight, preferred_element_type=jnp.float32).astype(jnp.bfloat16)
```

```python
import functools

import jax
import jax.numpy as jnp
from jax import lax
from jax.experimental import pallas as pl
from jax.experimental.pallas import tpu as pltpu
from jax.sharding import PartitionSpec as P

AXES = ("ctx", "tp")


class Places:
    def __init__(self, ctx, tp):
        self.ctx, self.tp = ctx, tp
        self.nx = 1 << ((ctx.bit_length() - 1) // 2)

    def device(self, v, w):
        core, zl = (v // self.nx) % 2, w % 2
        return (v + (zl - core) * self.nx) * self.tp + w + core - zl

    def here(self):
        i, j = lax.axis_index("ctx"), lax.axis_index("tp")
        core, zl = j % 2, (i // self.nx) % 2
        return i + (core - zl) * self.nx, j + zl - core

    def swap(self, value):
        pairs = [
            (v * self.tp + w, self.device(v, w)) for v in range(self.ctx) for w in range(self.tp)
        ]
        return lax.ppermute(value, AXES, pairs)

    def send(self, value, target):
        pairs = []
        for v in range(self.ctx):
            for w in range(self.tp):
                to = target(v, w)
                if to is not None:
                    pairs.append((self.device(v, w), self.device(*to)))
        return lax.ppermute(value, AXES, pairs)

    def gather(self, piece):
        have = {0: piece}

        def spread(count, stride):
            for base in list(have):
                for step in range(1, count):
                    mask = step * stride
                    have[base ^ mask] = self.send(have[base], lambda v, w, m=mask: (v ^ m, w))

        spread(self.ctx // (2 * self.nx), 2 * self.nx)
        spread(self.nx, 1)
        spread(2, self.nx)
        return have


def project_kernel(offsets, tokens, *refs):
    pieces, out = refs[:-1], refs[-1]
    depth = pieces[0].shape[1]
    total = None
    for index, piece in enumerate(pieces):
        start = pl.multiple_of(offsets[index], depth)
        term = lax.dot_general(
            piece[...],
            tokens[:, pl.ds(start, depth)],
            (((1,), (1,)), ((), ())),
            preferred_element_type=jnp.float32,
        )
        total = term if total is None else total + term
    out[...] = total.astype(out.dtype)


def project(offsets, tokens, pieces):
    width, depth = pieces[0].shape
    rows = tokens.shape[0]
    tile = min(256, width)
    return pl.pallas_call(
        project_kernel,
        out_shape=jax.ShapeDtypeStruct((width, rows), jnp.bfloat16),
        grid_spec=pltpu.PrefetchScalarGridSpec(
            num_scalar_prefetch=1,
            grid=(width // tile,),
            in_specs=[pl.BlockSpec(tokens.shape, lambda i, o: (0, 0))]
            + [pl.BlockSpec((tile, depth), lambda i, o: (i, 0))] * len(pieces),
            out_specs=pl.BlockSpec((tile, rows), lambda i, o: (i, 0)),
        ),
        compiler_params=pltpu.CompilerParams(vmem_limit_bytes=48 << 20),
        cost_estimate=pl.CostEstimate(
            flops=2 * width * rows * tokens.shape[1],
            bytes_accessed=2 * (width + rows) * tokens.shape[1],
            transcendentals=0,
        ),
    )(offsets, tokens, *pieces)


def output_kernel(offsets, mixed, *refs):
    pieces, out = refs[:-1], refs[-1]
    width = pieces[0].shape[1]
    for index, piece in enumerate(pieces):
        start = pl.multiple_of(offsets[index], width)
        out[:, pl.ds(start, width)] = jnp.dot(
            mixed[...], piece[...], preferred_element_type=jnp.float32
        ).astype(out.dtype)


def output_sums(offsets, mixed, pieces):
    rows, depth = mixed.shape
    width = pieces[0].shape[1]
    features = width * len(pieces)
    tile = min(256, rows)
    return pl.pallas_call(
        output_kernel,
        out_shape=jax.ShapeDtypeStruct((rows, features), jnp.bfloat16),
        grid_spec=pltpu.PrefetchScalarGridSpec(
            num_scalar_prefetch=1,
            grid=(rows // tile,),
            in_specs=[pl.BlockSpec((tile, depth), lambda i, o: (i, 0))]
            + [pl.BlockSpec((depth, width), lambda i, o: (0, 0))] * len(pieces),
            out_specs=pl.BlockSpec((tile, features), lambda i, o: (i, 0)),
        ),
        compiler_params=pltpu.CompilerParams(vmem_limit_bytes=48 << 20),
        cost_estimate=pl.CostEstimate(
            flops=2 * rows * depth * features,
            bytes_accessed=2 * (rows * depth + depth * features + rows * features),
            transcendentals=0,
        ),
    )(offsets, mixed, *pieces)


def short_conv(extended, taps):
    span = taps.shape[0]
    length = extended.shape[1] - (span - 1)
    result = taps[0, :, None] * extended[:, span - 1 :]
    for offset in range(1, span):
        start = span - 1 - offset
        result = result + taps[offset, :, None] * extended[:, start : start + length]
    return result


def banded(filters):
    tap_count = filters.shape[1]
    row_index = jnp.arange(tap_count)[:, None]
    col_index = jnp.arange(tap_count)[None, :]
    distance = (row_index - col_index) % tap_count
    picker = (distance[None, :, :] == jnp.arange(tap_count)[:, None, None]).astype(jnp.bfloat16)
    full_band = jnp.einsum("gk,kij->gij", filters, picker, preferred_element_type=jnp.float32)
    lower_part = row_index >= col_index
    lower_band = jnp.where(lower_part[None], full_band, 0.0).astype(jnp.bfloat16)
    upper_band = jnp.where(lower_part[None], 0.0, full_band).astype(jnp.bfloat16)
    return (lower_band, upper_band)


def long_conv(gated, previous, bands):
    channel_count, length = gated.shape
    lower_band, upper_band = bands
    group_count, tap_count, _ = lower_band.shape
    extended = jnp.concatenate([previous, gated], axis=1)
    blocks = extended.reshape(
        group_count, channel_count // group_count, length // tap_count + 1, tap_count
    )
    current = jnp.einsum(
        "gij,gcbj->gcbi", lower_band, blocks[:, :, 1:], preferred_element_type=jnp.float32
    )
    current = current + jnp.einsum(
        "gij,gcbj->gcbi", upper_band, blocks[:, :, :-1], preferred_element_type=jnp.float32
    )
    return current.reshape(channel_count, length)


def per_device(
    places, tokens, qkv_weight, short_filter, long_filter, decay_rate, skip_gain, out_weight
):
    rows = tokens.shape[0]
    depth, width = qkv_weight.shape[1:]
    features = out_weight.shape[1]
    groups, tap_count = long_filter.shape
    span = short_filter.shape[1]
    bf16, f32 = jnp.bfloat16, jnp.float32
    v, w = places.here()

    tap_index = jnp.arange(tap_count, dtype=f32)
    filters = (long_filter * jnp.exp(-decay_rate[:, None] * tap_index[None, :])).astype(bf16)
    packed = jnp.concatenate(
        [
            short_filter.reshape(3 * span, width),
            skip_gain[None, :],
            filters.astype(f32).reshape(-1, width),
        ]
    )

    tokens = places.swap(tokens)
    packed = places.swap(packed)
    short_filter = packed[: 3 * span].reshape(3, span, width)
    skip_gain = packed[3 * span]
    filters = packed[3 * span + 1 :].reshape(groups, tap_count).astype(bf16)
    bands = banded(filters)

    def forward(a, b):
        return (a + 1, b) if a + 1 < places.ctx else None

    chunks = {}
    for s in (1, 2, 0):
        chunks[s] = places.gather(places.swap(qkv_weight[s].T))
    out_pieces = places.gather(places.swap(out_weight))
    keys = sorted(out_pieces)
    order = jnp.stack([v ^ key for key in keys]).astype(jnp.int32)

    feats = {}
    for s in (1, 2, 0):
        value = project(order * depth, tokens, [chunks[s][key] for key in keys])
        rim = places.send(value[:, rows - (span - 1) :], forward)
        feats[s] = short_conv(jnp.concatenate([rim, value], axis=1), short_filter[s])
    gated = (feats[1] * feats[2]).astype(bf16)
    tail = places.send(gated[:, rows - tap_count :], forward)
    conv = long_conv(gated, tail, bands)
    mixed = (feats[0] * (conv + skip_gain[:, None] * gated.astype(f32))).astype(bf16)
    sums = output_sums(order * features, mixed.T, [out_pieces[key] for key in keys])

    ny = places.tp // 2
    part = rows // ny
    y, zl = w // 2, w % 2
    total = lax.dynamic_slice_in_dim(sums, y * part, part).astype(f32)
    for step in range(1, ny):
        other = lax.dynamic_slice_in_dim(sums, (y ^ step) * part, part)
        total = total + places.send(other, lambda a, b, m=2 * step: (a, b ^ m)).astype(f32)

    core = (v // places.nx) % 2
    half = part // 2
    home = core == zl
    mine = lax.dynamic_slice_in_dim(total, core * half, half)
    yours = lax.dynamic_slice_in_dim(total, (1 - core) * half, half)
    nx = places.nx
    first = jnp.where(home, yours, mine).astype(bf16)

    def at_home(a, b):
        return (a // nx) % 2 == b % 2

    first = places.send(
        first, lambda a, b: (a ^ nx, b) if at_home(a, b) else (a, b ^ 1)
    ).astype(f32)
    second = places.send(
        yours.astype(bf16), lambda a, b: None if at_home(a, b) else (a ^ nx, b ^ 1)
    ).astype(f32)
    return (first + jnp.where(home, mine, second)).astype(bf16)


def solution(mesh):
    in_specs = (
        P("ctx", None),
        P(None, "ctx", "tp"),
        P(None, None, "tp"),
        P("tp", None),
        P("tp"),
        P("tp"),
        P("tp", "ctx"),
    )
    places = Places(mesh.shape["ctx"], mesh.shape["tp"])
    return jax.shard_map(
        functools.partial(per_device, places),
        mesh=mesh,
        in_specs=in_specs,
        out_specs=P(AXES, None),
        check_vma=False,
    )
```

```python
import functools

import jax
import jax.numpy as jnp
from jax import lax
from jax.experimental import pallas as pl
from jax.experimental.pallas import tpu as pltpu
from jax.sharding import PartitionSpec as P

AXES = ("ctx", "tp")
BF16, F32 = jnp.bfloat16, jnp.float32
VMEM_LIMIT = 56 << 20
IN_FLIGHT = 2


class Places:
    def __init__(self, ctx, tp):
        self.ctx, self.tp = ctx, tp
        self.nx = 1 << ((ctx.bit_length() - 1) // 2)
        self.ny = tp // 2

    def device(self, v, w):
        core, zl = (v // self.nx) % 2, w % 2
        return (v + (zl - core) * self.nx) * self.tp + w + core - zl

    def here(self):
        i, j = lax.axis_index("ctx"), lax.axis_index("tp")
        core, zl = j % 2, (i // self.nx) % 2
        return i + (core - zl) * self.nx, j + zl - core

    def at_home(self, v, w):
        return (v // self.nx) % 2 == w % 2

    def deliver(self, value, mask=0):
        pairs = []
        for i in range(self.ctx):
            for j in range(self.tp):
                source, target = i * self.tp + j, self.device(i ^ mask, j)
                if source != target:
                    pairs.append((source, target))
        return lax.ppermute(value, AXES, pairs)

    def send(self, value, target):
        pairs = []
        for v in range(self.ctx):
            for w in range(self.tp):
                to = target(v, w)
                if to is not None:
                    pairs.append((self.device(v, w), self.device(*to)))
        return lax.ppermute(value, AXES, pairs)

    def spread_masks(self):
        far = [step * 2 * self.nx for step in range(self.ctx // (2 * self.nx))]
        groups = [[m ^ step for m in far] for step in range(self.nx)]
        return groups + [[m ^ self.nx for m in group] for group in groups]


def after(value, done):
    return lax.optimization_barrier((value, done))[0] if done is not None else value


def gather(places, home, shard, line):
    far = []
    for step in range(1, places.ctx // (2 * places.nx)):
        far.append(places.deliver(after(shard, line[-IN_FLIGHT]), step * 2 * places.nx))
        line.append(far[-1])
    near = places.deliver(after(shard, line[-IN_FLIGHT]))
    held = jnp.stack([jnp.where(home, shard, near)] + far)
    stacks = [held]
    for step in range(1, places.nx):
        stacks.append(places.send(held, lambda v, w, m=step: (v ^ m, w)))
    return stacks + [places.send(stack, lambda v, w: (v ^ places.nx, w)) for stack in stacks]


def prepare_kernel(per_part, order, flags, own, *refs):
    parts, out = refs[:-1], refs[-1]
    part = order[pl.program_id(0)] // per_part

    @pl.when(flags[0] == 1)
    def _():
        out[...] = own[...].T

    for step, ref in enumerate(parts):

        @pl.when((flags[0] == 0) & (part == flags[1] ^ step))
        def _():
            out[...] = ref[...].T


def prepare(order, flags, own, parts, depth):
    rows, features = own.shape
    count = features // depth
    per_part = count // len(parts)
    return pl.pallas_call(
        functools.partial(prepare_kernel, per_part),
        out_shape=jax.ShapeDtypeStruct((features, rows), BF16),
        grid_spec=pltpu.PrefetchScalarGridSpec(
            num_scalar_prefetch=2,
            grid=(count,),
            in_specs=[pl.BlockSpec((rows, depth), lambda i, o, f: (0, o[i]))]
            + [pl.BlockSpec((rows, depth), lambda i, o, f: (0, o[i] % per_part))] * len(parts),
            out_specs=pl.BlockSpec((depth, rows), lambda i, o, f: (i, 0)),
        ),
        compiler_params=pltpu.CompilerParams(vmem_limit_bytes=VMEM_LIMIT),
        cost_estimate=pl.CostEstimate(
            flops=0, bytes_accessed=6 * rows * features, transcendentals=0
        ),
    )(order, flags, own, *parts)


def project_kernel(tokens, *refs):
    stacks, out = refs[:-1], refs[-1]
    pieces = [stack[index] for stack in stacks for index in range(stack.shape[0])]
    out[...] = jnp.dot(
        jnp.concatenate(pieces, axis=1), tokens[...], preferred_element_type=F32
    ).astype(out.dtype)


def project(tokens, stacks):
    features, rows = tokens.shape
    count, width, depth = stacks[0].shape
    tile = min(256, width)
    return pl.pallas_call(
        project_kernel,
        out_shape=jax.ShapeDtypeStruct((width, rows), BF16),
        grid=(width // tile,),
        in_specs=[pl.BlockSpec((features, rows), lambda i: (0, 0))]
        + [pl.BlockSpec((count, tile, depth), lambda i: (0, i, 0))] * len(stacks),
        out_specs=pl.BlockSpec((tile, rows), lambda i: (i, 0)),
        compiler_params=pltpu.CompilerParams(vmem_limit_bytes=VMEM_LIMIT),
        cost_estimate=pl.CostEstimate(
            flops=2 * width * rows * features,
            bytes_accessed=2 * ((width + rows) * features + width * rows),
            transcendentals=0,
        ),
    )(tokens, *stacks)


def featurize(rim, value, coefficients, first, span):
    wide = jnp.concatenate([rim, value], axis=1).astype(F32)
    total = coefficients[:, first : first + 1] * wide
    for offset in range(1, span):
        total = total + coefficients[:, first + offset : first + offset + 1] * pltpu.roll(
            wide, offset, 1
        )
    return total[:, rim.shape[1] :]


def filter_kernel(span, k, v, k_rim, v_rim, before, coefficients, bands, out):
    coef = coefficients[...]
    first = featurize(k_rim[...], k[...], coef, span, span)
    second = featurize(v_rim[...], v[...], coef, 2 * span, span)
    gated = (first * second).astype(BF16)
    wide = jnp.concatenate([before[...], gated], axis=1)
    groups, reach, taps = bands.shape
    size = wide.shape[0] // groups
    blocks = gated.shape[1] // taps
    for group in range(groups):
        rows = slice(group * size, (group + 1) * size)
        windows = jnp.concatenate(
            [wide[rows, block * taps : block * taps + reach] for block in range(blocks)], axis=0
        )
        sums = jnp.dot(windows, bands[group], preferred_element_type=F32)
        gain = coef[rows, 3 * span : 3 * span + 1]
        for block in range(blocks):
            lanes = slice(block * taps, (block + 1) * taps)
            out[rows, lanes] = sums[block * size : (block + 1) * size] + gain * gated[
                rows, lanes
            ].astype(F32)


def long_filter_part(span, k, v, k_rim, v_rim, before, coefficients, bands):
    width, rows = k.shape
    groups, reach, taps = bands.shape
    tile = min(128, width)
    tall = lambda size: pl.BlockSpec((tile, size), lambda i: (i, 0))
    return pl.pallas_call(
        functools.partial(filter_kernel, span),
        out_shape=jax.ShapeDtypeStruct((width, rows), F32),
        grid=(width // tile,),
        in_specs=[tall(rows), tall(rows), tall(taps), tall(taps), tall(taps)]
        + [
            tall(coefficients.shape[1]),
            pl.BlockSpec((groups * tile // width, reach, taps), lambda i: (i, 0, 0)),
        ],
        out_specs=tall(rows),
        compiler_params=pltpu.CompilerParams(vmem_limit_bytes=VMEM_LIMIT),
        cost_estimate=pl.CostEstimate(
            flops=2 * width * rows * (reach + 4 * span),
            bytes_accessed=8 * width * rows + 2 * groups * reach * taps,
            transcendentals=0,
        ),
    )(k, v, k_rim, v_rim, before, coefficients, bands)


def mix_kernel(span, q, q_rim, filtered, coefficients, out):
    features = featurize(q_rim[...], q[...], coefficients[...], 0, span)
    out[...] = (features * filtered[...]).T.astype(BF16)


def mix(span, q, q_rim, filtered, coefficients):
    width, rows = q.shape
    tile = min(128, width)
    tall = lambda size: pl.BlockSpec((tile, size), lambda i: (i, 0))
    return pl.pallas_call(
        functools.partial(mix_kernel, span),
        out_shape=jax.ShapeDtypeStruct((rows, width), BF16),
        grid=(width // tile,),
        in_specs=[tall(rows), tall(q_rim.shape[1]), tall(rows), tall(coefficients.shape[1])],
        out_specs=pl.BlockSpec((rows, tile), lambda i: (0, i)),
        compiler_params=pltpu.CompilerParams(vmem_limit_bytes=VMEM_LIMIT),
        cost_estimate=pl.CostEstimate(
            flops=2 * width * rows * span, bytes_accessed=8 * width * rows, transcendentals=0
        ),
    )(q, q_rim, filtered, coefficients)


def output_kernel(count, order, *refs):
    mixed, stacks, out = refs[:count], refs[count:-1], refs[-1]
    left = jnp.concatenate([ref[...] for ref in mixed], axis=1)
    width = stacks[0].shape[2]
    place = 0
    for stack in stacks:
        for index in range(stack.shape[0]):
            start = pl.multiple_of(order[place] * width, width)
            out[:, pl.ds(start, width)] = jnp.dot(
                left, stack[index], preferred_element_type=F32
            ).astype(out.dtype)
            place += 1


def output_sums(order, mixed, stacks):
    rows, part = mixed[0].shape
    count, depth, width = stacks[0].shape
    features = width * count * len(stacks)
    tile = min(256, rows)
    return pl.pallas_call(
        functools.partial(output_kernel, len(mixed)),
        out_shape=jax.ShapeDtypeStruct((rows, features), BF16),
        grid_spec=pltpu.PrefetchScalarGridSpec(
            num_scalar_prefetch=1,
            grid=(rows // tile,),
            in_specs=[pl.BlockSpec((tile, part), lambda i, o: (i, 0))] * len(mixed)
            + [pl.BlockSpec((count, depth, width), lambda i, o: (0, 0, 0))] * len(stacks),
            out_specs=pl.BlockSpec((tile, features), lambda i, o: (i, 0)),
        ),
        compiler_params=pltpu.CompilerParams(vmem_limit_bytes=VMEM_LIMIT),
        cost_estimate=pl.CostEstimate(
            flops=2 * rows * depth * features,
            bytes_accessed=2 * (rows * depth + depth * features + rows * features),
            transcendentals=0,
        ),
    )(order, *mixed, *stacks)


def bands_of(filters):
    taps = filters.shape[1]
    source = jnp.arange(taps)[:, None]
    target = jnp.arange(taps)[None, :]
    distance = (target - source) % taps
    picker = (distance[None] == jnp.arange(taps)[:, None, None]).astype(BF16)
    full = jnp.einsum("gk,kji->gji", filters, picker, preferred_element_type=F32)
    same = target >= source
    before, current = jnp.where(same, 0.0, full), jnp.where(same, full, 0.0)
    return jnp.concatenate([before, current], axis=1).astype(BF16)


def tail_gate(k, v, taps_k, taps_v, reach):
    span = taps_k.shape[0]

    def features(value, taps):
        wide = value[:, value.shape[1] - reach - span + 1 :].astype(F32)
        total = taps[0][:, None] * wide[:, span - 1 :]
        for offset in range(1, span):
            start = span - 1 - offset
            total = total + taps[offset][:, None] * wide[:, start : start + reach]
        return total

    return (features(k, taps_k) * features(v, taps_v)).astype(BF16)


def take(value, part, size):
    return lax.dynamic_slice_in_dim(value, part * size, size)


def sum_over_y(places, sums, y):
    part = sums.shape[0] // places.ny
    total = take(sums, y, part).astype(F32)
    for step in range(1, places.ny):
        other = take(sums, y ^ step, part)
        total = total + places.send(other, lambda a, b, m=2 * step: (a, b ^ m)).astype(F32)
    return total


def sum_over_zl(places, mine, yours, home):
    nx = places.nx
    first = places.send(
        jnp.where(home, yours, mine).astype(BF16),
        lambda a, b: (a ^ nx, b) if places.at_home(a, b) else (a, b ^ 1),
    )
    second = places.send(
        yours.astype(BF16), lambda a, b: None if places.at_home(a, b) else (a ^ nx, b ^ 1)
    )
    return first.astype(F32) + jnp.where(home, mine.astype(F32), second.astype(F32))


def per_device(
    places, tokens, qkv_weight, short_filter, long_filter, decay_rate, skip_gain, out_weight
):
    rows, in_features = tokens.shape
    depth, width = qkv_weight.shape[1:]
    groups, taps = long_filter.shape
    span = short_filter.shape[1]
    ny, nx = places.ny, places.nx
    v, w = places.here()
    y, zl = w // 2, w % 2
    core = (v // nx) % 2
    home = core == zl
    half = width // 2
    chunks = max(1, out_weight.shape[1] // 256)
    chunk = out_weight.shape[1] // chunks
    order = jnp.stack([v ^ m for group in places.spread_masks() for m in group]).astype(jnp.int32)
    flags = jnp.stack([home.astype(jnp.int32), y.astype(jnp.int32)])

    line = [None] * IN_FLIGHT
    pieces = {}
    pieces[1, 0] = gather(places, home, qkv_weight[1, :, :half].T, line)

    share = in_features // ny
    mine = places.deliver(lax.dynamic_slice_in_dim(tokens, y * share, share, 1))
    parts = [mine]
    for step in range(1, ny):
        parts.append(
            places.send(
                mine,
                lambda a, b, m=2 * step: None if places.at_home(a, b) else (a, b ^ m),
            )
        )
    tokens = prepare(order, flags, tokens, parts, depth)

    for s, h in ((2, 0), (1, 1), (2, 1), (0, 0), (0, 1)):
        pieces[s, h] = gather(places, home, qkv_weight[s, :, h * half : (h + 1) * half].T, line)
    outs = [
        gather(places, home, out_weight[:, c * chunk : (c + 1) * chunk], line)
        for c in range(chunks)
    ]

    tap_index = jnp.arange(taps, dtype=F32)
    filters = (long_filter * jnp.exp(-decay_rate[:, None] * tap_index[None, :])).astype(BF16)
    packed = jnp.concatenate(
        [
            short_filter.reshape(3 * span, width),
            skip_gain[None, :],
            filters.astype(F32).reshape(-1, width),
        ]
    )
    packed = jnp.where(home, packed, places.deliver(packed))
    short = packed[: 3 * span].reshape(3, span, width)
    coefficients = jnp.pad(packed[: 3 * span + 1].T, ((0, 0), (0, (-3 * span - 1) % 8)))
    bands = bands_of(packed[3 * span + 1 :].reshape(groups, taps).astype(BF16))

    def forward(a, b):
        return (a + 1, b) if a + 1 < places.ctx else None

    def rim_of(value):
        return jnp.pad(value.T, ((0, 0), (taps - value.shape[0], 0)))

    edge = 8 * -(-(span - 1) // 8)
    mixed = []
    filtered = []
    for h in range(2):
        lanes = slice(h * half, (h + 1) * half)
        k = project(tokens, pieces[1, h])
        u = project(tokens, pieces[2, h])
        tail = tail_gate(k, u, short[1, :, lanes], short[2, :, lanes], taps)
        halo = jnp.concatenate([tail.T, k[:, rows - edge :].T, u[:, rows - edge :].T])
        halo = places.send(halo, forward)
        filtered.append(
            long_filter_part(
                span,
                k,
                u,
                rim_of(halo[taps : taps + edge]),
                rim_of(halo[taps + edge :]),
                halo[:taps].T,
                coefficients[lanes],
                bands[h * groups // 2 : (h + 1) * groups // 2],
            )
        )
    for h in range(2):
        lanes = slice(h * half, (h + 1) * half)
        q = project(tokens, pieces[0, h])
        rim = rim_of(places.send(q[:, rows - edge :].T, forward))
        mixed.append(mix(span, q, rim, filtered[h], coefficients[lanes]))

    results = []
    for c in range(chunks):
        sums = output_sums(order, mixed, outs[c])
        if c + 1 < chunks or chunks == 1:
            total = sum_over_y(places, sums, y)
            part = total.shape[0] // 2
            result = sum_over_zl(
                places, take(total, core, part), take(total, 1 - core, part), home
            )
        else:
            quarters = sums.reshape(ny, 2, rows // (2 * ny), -1)
            pick = lambda index: lax.dynamic_index_in_dim(quarters, index, 1, keepdims=False)
            total = sum_over_zl(places, pick(core), pick(1 - core), home)
            total = total.reshape(rows // 2, -1).astype(BF16)
            result = sum_over_y(places, total, y)
        results.append(result.astype(BF16).reshape(result.shape[0], places.ctx, 1, chunk))
    return jnp.concatenate(results, axis=2).reshape(rows // places.tp, -1)


def solution(mesh):
    in_specs = (
        P("ctx", None),
        P(None, "ctx", "tp"),
        P(None, None, "tp"),
        P("tp", None),
        P("tp"),
        P("tp"),
        P("tp", "ctx"),
    )
    places = Places(mesh.shape["ctx"], mesh.shape["tp"])
    return jax.shard_map(
        functools.partial(per_device, places),
        mesh=mesh,
        in_specs=in_specs,
        out_specs=P(AXES, None),
        check_vma=False,
    )
```

```python
import functools

import jax
import jax.numpy as jnp
from jax import lax
from jax.experimental import pallas as pl
from jax.experimental.pallas import tpu as pltpu
from jax.sharding import PartitionSpec as P

AXES = ("ctx", "tp")
BF16, F32 = jnp.bfloat16, jnp.float32
VMEM_LIMIT = 56 << 20


class Places:
    def __init__(self, ctx, tp):
        self.ctx, self.tp = ctx, tp
        self.nx = 1 << ((ctx.bit_length() - 1) // 2)
        self.ny = tp // 2

    def device(self, v, w):
        core, zl = (v // self.nx) % 2, w % 2
        return (v + (zl - core) * self.nx) * self.tp + w + core - zl

    def here(self):
        i, j = lax.axis_index("ctx"), lax.axis_index("tp")
        core, zl = j % 2, (i // self.nx) % 2
        return i + (core - zl) * self.nx, j + zl - core

    def at_home(self, v, w):
        return (v // self.nx) % 2 == w % 2

    def deliver(self, value, mask=0):
        pairs = []
        for i in range(self.ctx):
            for j in range(self.tp):
                source, target = i * self.tp + j, self.device(i ^ mask, j)
                if source != target:
                    pairs.append((source, target))
        return lax.ppermute(value, AXES, pairs)

    def send(self, value, target):
        pairs = []
        for v in range(self.ctx):
            for w in range(self.tp):
                to = target(v, w)
                if to is not None:
                    pairs.append((self.device(v, w), self.device(*to)))
        return lax.ppermute(value, AXES, pairs)

    def spread_masks(self):
        far = [step * 2 * self.nx for step in range(self.ctx // (2 * self.nx))]
        groups = [[m ^ step for m in far] for step in range(self.nx)]
        return groups + [[m ^ self.nx for m in group] for group in groups]


def after(value, *done):
    done = [entry for group in done for entry in group]
    return lax.optimization_barrier((value, *done))[0] if done else value


class Line:
    def __init__(self, places):
        self.places, self.far, self.across, self.sibling = places, [], [], []

    def so_far(self, history, lag):
        return history[-lag] if len(history) >= lag else []

    def gather(self, own, shard):
        places = self.places
        shard = after(
            shard,
            self.so_far(self.far, 2),
            self.so_far(self.across, 2),
            self.so_far(self.sibling, 3),
        )
        far = [
            places.deliver(shard, step * 2 * places.nx)
            for step in range(1, places.ctx // (2 * places.nx))
        ]
        self.far.append(far)
        yield
        held = jnp.stack([own] + far)
        across = [
            places.send(held, lambda v, w, m=step: (v ^ m, w)) for step in range(1, places.nx)
        ]
        self.across.append(across)
        yield
        both = jnp.concatenate([held] + across)
        sibling = places.send(both, lambda v, w: (v ^ places.nx, w))
        self.sibling.append([sibling])
        yield [both, sibling]


def run_line(jobs):
    results = {}
    for turn in range(len(jobs) + 2):
        for lag in (2, 1, 0):
            index = turn - lag
            if 0 <= index < len(jobs):
                results[index] = next(jobs[index])
    return [results[index] for index in range(len(jobs))]


def prepare_kernel(per_part, order, flags, own, *refs):
    parts, out = refs[:-1], refs[-1]
    part = order[pl.program_id(0)] // per_part

    @pl.when(flags[0] == 1)
    def _():
        out[...] = own[...].T

    for step, ref in enumerate(parts):

        @pl.when((flags[0] == 0) & (part == flags[1] ^ step))
        def _():
            out[...] = ref[...].T


def prepare(order, flags, own, parts, depth):
    rows, features = own.shape
    count = features // depth
    per_part = count // len(parts)
    return pl.pallas_call(
        functools.partial(prepare_kernel, per_part),
        out_shape=jax.ShapeDtypeStruct((features, rows), BF16),
        grid_spec=pltpu.PrefetchScalarGridSpec(
            num_scalar_prefetch=2,
            grid=(count,),
            in_specs=[pl.BlockSpec((rows, depth), lambda i, o, f: (0, o[i]))]
            + [pl.BlockSpec((rows, depth), lambda i, o, f: (0, o[i] % per_part))] * len(parts),
            out_specs=pl.BlockSpec((depth, rows), lambda i, o, f: (i, 0)),
        ),
        compiler_params=pltpu.CompilerParams(vmem_limit_bytes=VMEM_LIMIT),
        cost_estimate=pl.CostEstimate(
            flops=0, bytes_accessed=6 * rows * features, transcendentals=0
        ),
    )(order, flags, own, *parts)


def project_kernel(tokens, *refs):
    stacks, out = refs[:-1], refs[-1]
    pieces = [stack[index] for stack in stacks for index in range(stack.shape[0])]
    out[...] = jnp.dot(
        jnp.concatenate(pieces, axis=1), tokens[...], preferred_element_type=F32
    ).astype(out.dtype)


def project(tokens, stacks):
    features, rows = tokens.shape
    count, width, depth = stacks[0].shape
    tile = min(256, width)
    return pl.pallas_call(
        project_kernel,
        out_shape=jax.ShapeDtypeStruct((width, rows), BF16),
        grid=(width // tile,),
        in_specs=[pl.BlockSpec((features, rows), lambda i: (0, 0))]
        + [pl.BlockSpec((count, tile, depth), lambda i: (0, i, 0))] * len(stacks),
        out_specs=pl.BlockSpec((tile, rows), lambda i: (i, 0)),
        compiler_params=pltpu.CompilerParams(vmem_limit_bytes=VMEM_LIMIT),
        cost_estimate=pl.CostEstimate(
            flops=2 * width * rows * features,
            bytes_accessed=2 * ((width + rows) * features + width * rows),
            transcendentals=0,
        ),
    )(tokens, *stacks)


def featurize(rim, value, coefficients, first, span):
    wide = jnp.concatenate([rim, value], axis=1).astype(F32)
    total = coefficients[:, first : first + 1] * wide
    for offset in range(1, span):
        total = total + coefficients[:, first + offset : first + offset + 1] * pltpu.roll(
            wide, offset, 1
        )
    return total[:, rim.shape[1] :]


def filter_kernel(span, k, v, k_rim, v_rim, before, coefficients, bands, out):
    coef = coefficients[...]
    first = featurize(k_rim[...], k[...], coef, span, span)
    second = featurize(v_rim[...], v[...], coef, 2 * span, span)
    gated = (first * second).astype(BF16)
    wide = jnp.concatenate([before[...], gated], axis=1)
    groups, reach, taps = bands.shape
    size = wide.shape[0] // groups
    blocks = gated.shape[1] // taps
    for group in range(groups):
        rows = slice(group * size, (group + 1) * size)
        windows = jnp.concatenate(
            [wide[rows, block * taps : block * taps + reach] for block in range(blocks)], axis=0
        )
        sums = jnp.dot(windows, bands[group], preferred_element_type=F32)
        gain = coef[rows, 3 * span : 3 * span + 1]
        for block in range(blocks):
            lanes = slice(block * taps, (block + 1) * taps)
            out[rows, lanes] = sums[block * size : (block + 1) * size] + gain * gated[
                rows, lanes
            ].astype(F32)


def long_filter_part(span, k, v, k_rim, v_rim, before, coefficients, bands):
    width, rows = k.shape
    groups, reach, taps = bands.shape
    tile = min(128, width)
    tall = lambda size: pl.BlockSpec((tile, size), lambda i: (i, 0))
    return pl.pallas_call(
        functools.partial(filter_kernel, span),
        out_shape=jax.ShapeDtypeStruct((width, rows), F32),
        grid=(width // tile,),
        in_specs=[tall(rows), tall(rows), tall(taps), tall(taps), tall(taps)]
        + [
            tall(coefficients.shape[1]),
            pl.BlockSpec((groups * tile // width, reach, taps), lambda i: (i, 0, 0)),
        ],
        out_specs=tall(rows),
        compiler_params=pltpu.CompilerParams(vmem_limit_bytes=VMEM_LIMIT),
        cost_estimate=pl.CostEstimate(
            flops=2 * width * rows * (reach + 4 * span),
            bytes_accessed=8 * width * rows + 2 * groups * reach * taps,
            transcendentals=0,
        ),
    )(k, v, k_rim, v_rim, before, coefficients, bands)


def mix_kernel(span, q, q_rim, filtered, coefficients, out):
    features = featurize(q_rim[...], q[...], coefficients[...], 0, span)
    out[...] = (features * filtered[...]).T.astype(BF16)


def mix(span, q, q_rim, filtered, coefficients):
    width, rows = q.shape
    tile = min(128, width)
    tall = lambda size: pl.BlockSpec((tile, size), lambda i: (i, 0))
    return pl.pallas_call(
        functools.partial(mix_kernel, span),
        out_shape=jax.ShapeDtypeStruct((rows, width), BF16),
        grid=(width // tile,),
        in_specs=[tall(rows), tall(q_rim.shape[1]), tall(rows), tall(coefficients.shape[1])],
        out_specs=pl.BlockSpec((rows, tile), lambda i: (0, i)),
        compiler_params=pltpu.CompilerParams(vmem_limit_bytes=VMEM_LIMIT),
        cost_estimate=pl.CostEstimate(
            flops=2 * width * rows * span, bytes_accessed=8 * width * rows, transcendentals=0
        ),
    )(q, q_rim, filtered, coefficients)


def output_kernel(count, order, *refs):
    mixed, stacks, out = refs[:count], refs[count:-1], refs[-1]
    left = jnp.concatenate([ref[...] for ref in mixed], axis=1)
    width = stacks[0].shape[2]
    place = 0
    for stack in stacks:
        for index in range(stack.shape[0]):
            start = pl.multiple_of(order[place] * width, width)
            out[:, pl.ds(start, width)] = jnp.dot(
                left, stack[index], preferred_element_type=F32
            ).astype(out.dtype)
            place += 1


def output_sums(order, mixed, stacks):
    rows, part = mixed[0].shape
    count, depth, width = stacks[0].shape
    features = width * count * len(stacks)
    tile = min(256, rows)
    return pl.pallas_call(
        functools.partial(output_kernel, len(mixed)),
        out_shape=jax.ShapeDtypeStruct((rows, features), BF16),
        grid_spec=pltpu.PrefetchScalarGridSpec(
            num_scalar_prefetch=1,
            grid=(rows // tile,),
            in_specs=[pl.BlockSpec((tile, part), lambda i, o: (i, 0))] * len(mixed)
            + [pl.BlockSpec((count, depth, width), lambda i, o: (0, 0, 0))] * len(stacks),
            out_specs=pl.BlockSpec((tile, features), lambda i, o: (i, 0)),
        ),
        compiler_params=pltpu.CompilerParams(vmem_limit_bytes=VMEM_LIMIT),
        cost_estimate=pl.CostEstimate(
            flops=2 * rows * depth * features,
            bytes_accessed=2 * (rows * depth + depth * features + rows * features),
            transcendentals=0,
        ),
    )(order, *mixed, *stacks)


def bands_of(filters):
    taps = filters.shape[1]
    source = jnp.arange(taps)[:, None]
    target = jnp.arange(taps)[None, :]
    distance = (target - source) % taps
    picker = (distance[None] == jnp.arange(taps)[:, None, None]).astype(BF16)
    full = jnp.einsum("gk,kji->gji", filters, picker, preferred_element_type=F32)
    same = target >= source
    before, current = jnp.where(same, 0.0, full), jnp.where(same, full, 0.0)
    return jnp.concatenate([before, current], axis=1).astype(BF16)


def tail_gate(k, v, taps_k, taps_v, reach):
    span = taps_k.shape[0]

    def features(value, taps):
        wide = value[:, value.shape[1] - reach - span + 1 :].astype(F32)
        total = taps[0][:, None] * wide[:, span - 1 :]
        for offset in range(1, span):
            start = span - 1 - offset
            total = total + taps[offset][:, None] * wide[:, start : start + reach]
        return total

    return (features(k, taps_k) * features(v, taps_v)).astype(BF16)


def take(value, part, size):
    return lax.dynamic_slice_in_dim(value, part * size, size)


def sum_over_y(places, sums, y):
    part = sums.shape[0] // places.ny
    total = take(sums, y, part).astype(F32)
    for step in range(1, places.ny):
        other = take(sums, y ^ step, part)
        total = total + places.send(other, lambda a, b, m=2 * step: (a, b ^ m)).astype(F32)
    return total


def sum_over_zl(places, mine, yours, home):
    nx = places.nx
    first = places.send(
        jnp.where(home, yours, mine).astype(BF16),
        lambda a, b: (a ^ nx, b) if places.at_home(a, b) else (a, b ^ 1),
    )
    second = places.send(
        yours.astype(BF16), lambda a, b: None if places.at_home(a, b) else (a ^ nx, b ^ 1)
    )
    return first.astype(F32) + jnp.where(home, mine.astype(F32), second.astype(F32))


def per_device(
    places, tokens, qkv_weight, short_filter, long_filter, decay_rate, skip_gain, out_weight
):
    rows, in_features = tokens.shape
    depth, width = qkv_weight.shape[1:]
    groups, taps = long_filter.shape
    span = short_filter.shape[1]
    ny, nx = places.ny, places.nx
    v, w = places.here()
    y, zl = w // 2, w % 2
    core = (v // nx) % 2
    home = core == zl
    half = width // 2
    chunks = max(1, out_weight.shape[1] // 256)
    chunk = out_weight.shape[1] // chunks
    order = jnp.stack([v ^ m for group in places.spread_masks() for m in group]).astype(jnp.int32)
    flags = jnp.stack([home.astype(jnp.int32), y.astype(jnp.int32)])

    line = Line(places)
    first = qkv_weight[1].T

    share = in_features // ny
    mine = places.deliver(
        lax.dynamic_slice_in_dim(after(tokens, [first]), y * share, share, 1)
    )
    parts = [mine]
    for step in range(1, ny):
        parts.append(
            places.send(
                mine,
                lambda a, b, m=2 * step: None if places.at_home(a, b) else (a, b ^ m),
            )
        )
    tokens = prepare(order, flags, tokens, parts, depth)

    def weights(s, h, state):
        if h == 0:
            weight = qkv_weight[s] if s < 3 else out_weight
            weight = after(weight, line.so_far(line.far, 1))
            state[0] = weight.T if s < 3 else weight
            state[1] = jnp.where(home, state[0], places.deliver(state[0]))
        if s < 3:
            own, shard = (entry[h * half : (h + 1) * half] for entry in (state[1], state[0]))
        else:
            own, shard = (entry[:, h * chunk : (h + 1) * chunk] for entry in (state[1], state[0]))
        yield from line.gather(own, shard)

    jobs, names = [], []
    for s, count in ((1, 2), (2, 2), (0, 2), (3, chunks)):
        state = [None, None]
        for h in range(count):
            jobs.append(weights(s, h, state))
            names.append((s, h))
    pieces = dict(zip(names, run_line(jobs)))
    outs = [pieces[3, c] for c in range(chunks)]

    tap_index = jnp.arange(taps, dtype=F32)
    filters = (long_filter * jnp.exp(-decay_rate[:, None] * tap_index[None, :])).astype(BF16)
    packed = jnp.concatenate(
        [
            short_filter.reshape(3 * span, width),
            skip_gain[None, :],
            filters.astype(F32).reshape(-1, width),
        ]
    )
    packed = jnp.where(
        home,
        packed,
        places.send(packed, lambda a, b: (a ^ nx, b) if places.at_home(a, b) else None),
    )
    short = packed[: 3 * span].reshape(3, span, width)
    coefficients = jnp.pad(packed[: 3 * span + 1].T, ((0, 0), (0, (-3 * span - 1) % 8)))
    bands = bands_of(packed[3 * span + 1 :].reshape(groups, taps).astype(BF16))

    def forward(a, b):
        return (a + 1, b) if a + 1 < places.ctx else None

    def rim_of(value):
        return jnp.pad(value.T, ((0, 0), (taps - value.shape[0], 0)))

    edge = 8 * -(-(span - 1) // 8)
    mixed = []
    filtered = []
    for h in range(2):
        lanes = slice(h * half, (h + 1) * half)
        k = project(tokens, pieces[1, h])
        u = project(tokens, pieces[2, h])
        tail = tail_gate(k, u, short[1, :, lanes], short[2, :, lanes], taps)
        halo = jnp.concatenate([tail.T, k[:, rows - edge :].T, u[:, rows - edge :].T])
        halo = places.send(halo, forward)
        filtered.append(
            long_filter_part(
                span,
                k,
                u,
                rim_of(halo[taps : taps + edge]),
                rim_of(halo[taps + edge :]),
                halo[:taps].T,
                coefficients[lanes],
                bands[h * groups // 2 : (h + 1) * groups // 2],
            )
        )
    for h in range(2):
        lanes = slice(h * half, (h + 1) * half)
        q = project(tokens, pieces[0, h])
        rim = rim_of(places.send(q[:, rows - edge :].T, forward))
        mixed.append(mix(span, q, rim, filtered[h], coefficients[lanes]))

    results = []
    for c in range(chunks):
        sums = output_sums(order, mixed, outs[c])
        if c + 1 < chunks or chunks == 1:
            total = sum_over_y(places, sums, y)
            part = total.shape[0] // 2
            result = sum_over_zl(
                places, take(total, core, part), take(total, 1 - core, part), home
            )
        else:
            quarters = sums.reshape(ny, 2, rows // (2 * ny), -1)
            pick = lambda index: lax.dynamic_index_in_dim(quarters, index, 1, keepdims=False)
            total = sum_over_zl(places, pick(core), pick(1 - core), home)
            total = total.reshape(rows // 2, -1).astype(BF16)
            result = sum_over_y(places, total, y)
        results.append(result.astype(BF16).reshape(result.shape[0], places.ctx, 1, chunk))
    return jnp.concatenate(results, axis=2).reshape(rows // places.tp, -1)


def solution(mesh):
    in_specs = (
        P("ctx", None),
        P(None, "ctx", "tp"),
        P(None, None, "tp"),
        P("tp", None),
        P("tp"),
        P("tp"),
        P("tp", "ctx"),
    )
    places = Places(mesh.shape["ctx"], mesh.shape["tp"])
    return jax.shard_map(
        functools.partial(per_device, places),
        mesh=mesh,
        in_specs=in_specs,
        out_specs=P(AXES, None),
        check_vma=False,
    )
```

```python
import functools

import jax
import jax.numpy as jnp
from jax import lax
from jax.experimental import pallas as pl
from jax.experimental.pallas import tpu as pltpu
from jax.sharding import PartitionSpec as P

AXES = ("ctx", "tp")
BF16, F32 = jnp.bfloat16, jnp.float32
VMEM_LIMIT = 56 << 20


class Places:
    def __init__(self, ctx, tp):
        self.ctx, self.tp = ctx, tp
        self.nx = 1 << ((ctx.bit_length() - 1) // 2)
        self.nz = ctx // self.nx
        self.ny = tp // 2

    def send(self, value, target):
        pairs = []
        for i in range(self.ctx):
            for j in range(self.tp):
                to = target(i, j)
                if to is not None:
                    pairs.append((i * self.tp + j, to[0] * self.tp + to[1]))
        return lax.ppermute(value, AXES, pairs)

    def flip(self, value, ctx=0, tp=0):
        return self.send(value, lambda i, j: (i ^ ctx, j ^ tp))

    def masks(self):
        return [m * self.nx ^ step for step in range(self.nx) for m in range(self.nz)]


def after(value, *done):
    done = [entry for entry in done if entry is not None]
    return lax.optimization_barrier((value, *done))[0] if done else value


class Line:
    def __init__(self, places):
        self.places, self.far, self.across = places, [], []

    def step(self, value, mask):
        result = self.places.flip(
            after(
                value,
                self.far[-3] if len(self.far) >= 3 else None,
                self.across[-2] if len(self.across) >= 2 else None,
            ),
            ctx=mask,
        )
        self.far.append(result)
        return result

    def gather(self, own, other):
        nx, nz = self.places.nx, self.places.nz
        held = {0: own}
        for m in sorted(range(1, nz), key=lambda m: (m < 2, m)):
            held[m] = self.step(other if m % 2 else own, m * nx)
        return held

    def cross(self, held):
        stack = jnp.stack([held[m] for m in range(self.places.nz)])
        others = [self.places.flip(stack, ctx=step) for step in range(1, self.places.nx)]
        self.across.append(others[-1])
        return [stack] + others


def prepare_kernel(per_part, order, flags, own, *refs):
    parts, out = refs[:-1], refs[-1]
    part = order[pl.program_id(0)] // per_part
    rows = own.shape[0]
    out[:, pl.ds(pl.multiple_of(flags[0] * rows, rows), rows)] = own[...].T
    for mask, ref in enumerate(parts):

        @pl.when(part == flags[1] ^ mask)
        def _():
            out[:, pl.ds(pl.multiple_of((1 - flags[0]) * rows, rows), rows)] = ref[...].T


def prepare(order, flags, own, parts, depth):
    rows, features = own.shape
    count = features // depth
    per_part = count // len(parts)
    return pl.pallas_call(
        functools.partial(prepare_kernel, per_part),
        out_shape=jax.ShapeDtypeStruct((features, 2 * rows), BF16),
        grid_spec=pltpu.PrefetchScalarGridSpec(
            num_scalar_prefetch=2,
            grid=(count,),
            in_specs=[pl.BlockSpec((rows, depth), lambda i, o, f: (0, o[i]))]
            + [pl.BlockSpec((rows, depth), lambda i, o, f: (0, o[i] % per_part))] * len(parts),
            out_specs=pl.BlockSpec((depth, 2 * rows), lambda i, o, f: (i, 0)),
        ),
        compiler_params=pltpu.CompilerParams(vmem_limit_bytes=VMEM_LIMIT),
        cost_estimate=pl.CostEstimate(
            flops=0, bytes_accessed=8 * rows * features, transcendentals=0
        ),
    )(order, flags, own, *parts)


def project_kernel(tokens, *refs):
    stacks, out = refs[:-1], refs[-1]
    pieces = [stack[index] for stack in stacks for index in range(stack.shape[0])]
    out[...] = jnp.dot(
        jnp.concatenate(pieces, axis=1), tokens[...], preferred_element_type=F32
    ).astype(out.dtype)


def project(tokens, stacks):
    features, rows = tokens.shape
    count, width, depth = stacks[0].shape
    tile, part = min(256, width), rows // 2
    return pl.pallas_call(
        project_kernel,
        out_shape=jax.ShapeDtypeStruct((width, rows), BF16),
        grid=(2, width // tile),
        in_specs=[pl.BlockSpec((features, part), lambda t, i: (0, t))]
        + [pl.BlockSpec((count, tile, depth), lambda t, i: (0, i, 0))] * len(stacks),
        out_specs=pl.BlockSpec((tile, part), lambda t, i: (i, t)),
        compiler_params=pltpu.CompilerParams(vmem_limit_bytes=VMEM_LIMIT),
        cost_estimate=pl.CostEstimate(
            flops=2 * width * rows * features,
            bytes_accessed=2 * ((2 * width + rows) * features + width * rows),
            transcendentals=0,
        ),
    )(tokens, *stacks)


def featurize(rim, value, coefficients, first, span):
    wide = jnp.concatenate([rim, value], axis=1).astype(F32)
    total = coefficients[:, first : first + 1] * wide
    for offset in range(1, span):
        total = total + coefficients[:, first + offset : first + offset + 1] * pltpu.roll(
            wide, offset, 1
        )
    return total[:, rim.shape[1] :]


def filter_kernel(span, k, v, k_rim, v_rim, before, coefficients, bands, out):
    coef = coefficients[...]
    first = featurize(k_rim[...], k[...], coef, span, span)
    second = featurize(v_rim[...], v[...], coef, 2 * span, span)
    gated = (first * second).astype(BF16)
    wide = jnp.concatenate([before[...], gated], axis=1)
    groups, reach, taps = bands.shape
    size = wide.shape[0] // groups
    blocks = gated.shape[1] // taps
    for group in range(groups):
        rows = slice(group * size, (group + 1) * size)
        windows = jnp.concatenate(
            [wide[rows, block * taps : block * taps + reach] for block in range(blocks)], axis=0
        )
        sums = jnp.dot(windows, bands[group], preferred_element_type=F32)
        gain = coef[rows, 3 * span : 3 * span + 1]
        for block in range(blocks):
            lanes = slice(block * taps, (block + 1) * taps)
            out[rows, lanes] = sums[block * size : (block + 1) * size] + gain * gated[
                rows, lanes
            ].astype(F32)


def long_filter_part(span, k, v, k_rim, v_rim, before, coefficients, bands):
    width, rows = k.shape
    groups, reach, taps = bands.shape
    tile, part = min(128, width), rows // 2
    cell = lambda size: pl.BlockSpec((tile, size), lambda i, t: (i, t))
    return pl.pallas_call(
        functools.partial(filter_kernel, span),
        out_shape=jax.ShapeDtypeStruct((width, rows), F32),
        grid=(width // tile, 2),
        in_specs=[cell(part), cell(part), cell(taps), cell(taps), cell(taps)]
        + [
            pl.BlockSpec((tile, coefficients.shape[1]), lambda i, t: (i, 0)),
            pl.BlockSpec((groups * tile // width, reach, taps), lambda i, t: (i, 0, 0)),
        ],
        out_specs=cell(part),
        compiler_params=pltpu.CompilerParams(vmem_limit_bytes=VMEM_LIMIT),
        cost_estimate=pl.CostEstimate(
            flops=2 * width * rows * (reach + 4 * span),
            bytes_accessed=8 * width * rows + 2 * groups * reach * taps,
            transcendentals=0,
        ),
    )(k, v, k_rim, v_rim, before, coefficients, bands)


def mix_kernel(span, q, q_rim, filtered, coefficients, out):
    features = featurize(q_rim[...], q[...], coefficients[...], 0, span)
    out[...] = (features * filtered[...]).T.astype(BF16)


def mix(span, q, q_rim, filtered, coefficients):
    width, rows = q.shape
    tile, part = min(128, width), rows // 2
    cell = lambda size: pl.BlockSpec((tile, size), lambda i, t: (i, t))
    return pl.pallas_call(
        functools.partial(mix_kernel, span),
        out_shape=jax.ShapeDtypeStruct((rows, width), BF16),
        grid=(width // tile, 2),
        in_specs=[
            cell(part),
            cell(q_rim.shape[1] // 2),
            cell(part),
            pl.BlockSpec((tile, coefficients.shape[1]), lambda i, t: (i, 0)),
        ],
        out_specs=pl.BlockSpec((part, tile), lambda i, t: (t, i)),
        compiler_params=pltpu.CompilerParams(vmem_limit_bytes=VMEM_LIMIT),
        cost_estimate=pl.CostEstimate(
            flops=2 * width * rows * span, bytes_accessed=8 * width * rows, transcendentals=0
        ),
    )(q, q_rim, filtered, coefficients)


def output_kernel(count, order, *refs):
    mixed, stacks, out = refs[:count], refs[count:-1], refs[-1]
    left = jnp.concatenate([ref[...] for ref in mixed], axis=1)
    width = stacks[0].shape[2]
    place = 0
    for stack in stacks:
        pieces = [stack[index] for index in range(stack.shape[0])]
        sums = jnp.dot(left, jnp.concatenate(pieces, axis=1), preferred_element_type=F32)
        for index in range(stack.shape[0]):
            out[order[place]] = sums[:, index * width : (index + 1) * width].astype(out.dtype)
            place += 1


def output_sums(order, mixed, stacks):
    rows, part = mixed[0].shape
    count, depth, width = stacks[0].shape
    blocks = count * len(stacks)
    tile = min(256, rows)
    return pl.pallas_call(
        functools.partial(output_kernel, len(mixed)),
        out_shape=jax.ShapeDtypeStruct((blocks, rows, width), BF16),
        grid_spec=pltpu.PrefetchScalarGridSpec(
            num_scalar_prefetch=1,
            grid=(rows // tile,),
            in_specs=[pl.BlockSpec((tile, part), lambda i, o: (i, 0))] * len(mixed)
            + [pl.BlockSpec((count, depth, width), lambda i, o: (0, 0, 0))] * len(stacks),
            out_specs=pl.BlockSpec((blocks, tile, width), lambda i, o: (0, i, 0)),
        ),
        compiler_params=pltpu.CompilerParams(vmem_limit_bytes=VMEM_LIMIT),
        cost_estimate=pl.CostEstimate(
            flops=2 * rows * depth * blocks * width,
            bytes_accessed=2 * (rows * depth + depth * blocks * width + rows * blocks * width),
            transcendentals=0,
        ),
    )(order, *mixed, *stacks)


def bands_of(filters):
    taps = filters.shape[1]
    source = jnp.arange(taps)[:, None]
    target = jnp.arange(taps)[None, :]
    distance = (target - source) % taps
    picker = (distance[None] == jnp.arange(taps)[:, None, None]).astype(BF16)
    full = jnp.einsum("gk,kji->gji", filters, picker, preferred_element_type=F32)
    same = target >= source
    before, current = jnp.where(same, 0.0, full), jnp.where(same, full, 0.0)
    return jnp.concatenate([before, current], axis=1).astype(BF16)


def tail_gate(k, v, taps_k, taps_v, reach, end):
    span = taps_k.shape[0]

    def features(value, taps):
        wide = value[:, end - reach - span + 1 : end].astype(F32)
        total = taps[0][:, None] * wide[:, span - 1 :]
        for offset in range(1, span):
            start = span - 1 - offset
            total = total + taps[offset][:, None] * wide[:, start : start + reach]
        return total

    return (features(k, taps_k) * features(v, taps_v)).astype(BF16)


def pick(value, index, axis):
    return lax.dynamic_index_in_dim(value, index, axis, keepdims=False)


def per_device(
    places, tokens, qkv_weight, short_filter, long_filter, decay_rate, skip_gain, out_weight
):
    rows, in_features = tokens.shape
    depth, width = qkv_weight.shape[1:]
    features = out_weight.shape[1]
    groups, taps = long_filter.shape
    span = short_filter.shape[1]
    ny, nx, nz = places.ny, places.nx, places.nz
    i, j = lax.axis_index("ctx"), lax.axis_index("tp")
    x, zl = i % nx, (i // nx) % 2
    y, core = j // 2, j % 2
    half = width // 2
    share = features // 2
    chunks = 2 if share >= 256 else 1
    chunk = share // chunks
    order = jnp.stack([i ^ m for m in places.masks()]).astype(jnp.int32)
    flags = jnp.stack([zl, j]).astype(jnp.int32)
    line = Line(places)

    def halves(s, done=None):
        weight = after(qkv_weight, done)[s]
        return [
            lax.dynamic_slice_in_dim(weight, part * half, half, 1).T for part in (zl, 1 - zl)
        ]

    k_parts = halves(1)
    k_held = line.gather(*k_parts)

    size = in_features // places.tp
    parts = {
        0: line.step(
            lax.dynamic_slice_in_dim(after(tokens, k_parts[1]), j * size, size, 1), nx
        )
    }
    for step in range(1, ny):
        parts[2 * step] = places.flip(parts[0], tp=2 * step)
    for mask in list(parts):
        parts[mask ^ 1] = places.flip(parts[mask], tp=1)

    v_held = line.gather(*halves(2, k_parts[1]))
    pieces = {1: line.cross(k_held)}
    q_held = line.gather(*halves(0, k_parts[1]))
    pieces[2] = line.cross(v_held)

    out_halves = out_weight.reshape(width, 2, share)
    rows_of = [pick(out_halves, core, 1), places.flip(pick(out_halves, 1 - core, 1), tp=1)]
    both = jnp.stack(rows_of).reshape(2, 2, half, share)
    out_own, out_other = (pick(both, part, 1).reshape(width, share) for part in (zl, 1 - zl))
    out_held = []
    for c in range(chunks):
        lanes = slice(c * chunk, (c + 1) * chunk)
        out_held.append(line.gather(out_own[:, lanes], out_other[:, lanes]))
        if c == 0:
            pieces[0] = line.cross(q_held)
    outs = [line.cross(held) for held in out_held]

    tokens = prepare(
        order, flags, tokens, [parts[mask] for mask in range(places.tp)], depth
    )

    tap_index = jnp.arange(taps, dtype=F32)
    filters = (long_filter * jnp.exp(-decay_rate[:, None] * tap_index[None, :])).astype(BF16)
    bands = bands_of(lax.dynamic_slice_in_dim(filters, zl * (groups // 2), groups // 2))
    short = lax.dynamic_slice_in_dim(short_filter, zl * half, half, 2)
    gain = lax.dynamic_slice_in_dim(skip_gain, zl * half, half)
    coefficients = jnp.concatenate([short.reshape(3 * span, half), gain[None, :]]).T
    coefficients = jnp.pad(coefficients, ((0, 0), (0, (-3 * span - 1) % 8)))

    def halos(tails):
        beside = places.send(tails, lambda i, j: (i - i % nx + (i + 1) % nx, j))
        below = places.send(
            tails[1],
            lambda i, j: (i + 2 * nx - nx + 1, j)
            if i % nx == nx - 1 and i + 2 * nx < places.ctx
            else None,
        )
        start = x == 0
        return [jnp.where(start, below, beside[0]), jnp.where(start, beside[0], beside[1])]

    def rim_of(value):
        return jnp.pad(value.T, ((0, 0), (taps - value.shape[0], 0)))

    def rims(values):
        return jnp.concatenate([rim_of(value) for value in values], axis=1)

    edge = 8 * -(-(span - 1) // 8)
    ends = (rows, 2 * rows)
    k = project(tokens, pieces[1])
    u = project(tokens, pieces[2])
    tails = [
        jnp.concatenate(
            [
                tail_gate(k, u, short[1], short[2], taps, end).T,
                k[:, end - edge : end].T,
                u[:, end - edge : end].T,
            ]
        )
        for end in ends
    ]
    before = halos(jnp.stack(tails))
    filtered = long_filter_part(
        span,
        k,
        u,
        rims([value[taps : taps + edge] for value in before]),
        rims([value[taps + edge :] for value in before]),
        rims([value[:taps] for value in before]),
        coefficients,
        bands,
    )
    q = project(tokens, pieces[0])
    before = halos(jnp.stack([q[:, end - edge : end].T for end in ends]))
    mixed = mix(span, q, rims(before), filtered, coefficients)
    mixed = [mixed, places.flip(mixed, tp=1)]

    def over_y(value):
        total = pick(value, y, 1).astype(F32)
        for step in range(1, ny):
            total = total + places.flip(pick(value, y ^ step, 1), tp=2 * step).astype(F32)
        return total.astype(BF16)

    def over_z(value):
        other = places.flip(pick(value, 1 - zl, 1), ctx=nx)
        return (pick(value, zl, 1).astype(F32) + other.astype(F32)).astype(BF16)

    results = []
    blocks = places.ctx
    part = rows // ny
    for c in range(chunks):
        sums = output_sums(order, mixed, outs[c])
        if c + 1 < chunks or chunks == 1:
            value = sums.reshape(blocks * 2, ny, part, chunk)
            value = over_z(over_y(value).reshape(blocks, 2, part, chunk))
        else:
            value = over_z(sums.reshape(blocks, 2, rows, chunk))
            value = over_y(value.reshape(blocks, ny, part, chunk))
        value = value.reshape(blocks, 2, part // 2, chunk)
        mine = pick(value, core, 1)
        yours = places.flip(pick(value, 1 - core, 1), tp=1)
        pair = jnp.stack(
            [jnp.where(core == 0, mine, yours), jnp.where(core == 0, yours, mine)], axis=1
        )
        results.append(pair)
    result = jnp.stack(results, axis=2)
    return result.transpose(3, 0, 1, 2, 4).reshape(part // 2, -1)


def solution(mesh):
    in_specs = (
        P("ctx", None),
        P(None, "ctx", "tp"),
        P(None, None, "tp"),
        P("tp", None),
        P("tp"),
        P("tp"),
        P("tp", "ctx"),
    )
    places = Places(mesh.shape["ctx"], mesh.shape["tp"])
    return jax.shard_map(
        functools.partial(per_device, places),
        mesh=mesh,
        in_specs=in_specs,
        out_specs=P(AXES, None),
        check_vma=False,
    )
```

```python
import functools

import jax
import jax.numpy as jnp
from jax import lax
from jax.experimental import pallas as pl
from jax.experimental.pallas import tpu as pltpu
from jax.sharding import PartitionSpec as P

AXES = ("ctx", "tp")
BF16, F32 = jnp.bfloat16, jnp.float32
VMEM_LIMIT = 56 << 20


class Places:
    def __init__(self, ctx, tp):
        self.ctx, self.tp = ctx, tp
        self.nx = 1 << ((ctx.bit_length() - 1) // 2)
        self.nz = ctx // self.nx
        self.ny = tp // 2

    def send(self, value, target):
        pairs = []
        for i in range(self.ctx):
            for j in range(self.tp):
                to = target(i, j)
                if to is not None:
                    pairs.append((i * self.tp + j, to[0] * self.tp + to[1]))
        return lax.ppermute(value, AXES, pairs)

    def flip(self, value, ctx=0, tp=0):
        return self.send(value, lambda i, j: (i ^ ctx, j ^ tp))

    def masks(self):
        return [m * self.nx for m in range(self.nz)]


def after(value, *done):
    done = [entry for entry in done if entry is not None]
    return lax.optimization_barrier((value, *done))[0] if done else value


class Line:
    def __init__(self, places):
        self.places, self.far = places, []

    def step(self, value, mask):
        result = self.places.flip(
            after(value, self.far[-3] if len(self.far) >= 3 else None), ctx=mask
        )
        self.far.append(result)
        return result

    def gather(self, own, other):
        nx, nz = self.places.nx, self.places.nz
        held = {0: own}
        for m in sorted(range(1, nz), key=lambda m: (m < 2, m)):
            held[m] = self.step(other if m % 2 else own, m * nx)
        return held

    def cross(self, held):
        nx, nz = self.places.nx, self.places.nz
        stack = jnp.stack([held[m] for m in range(nz)])
        groups = [[z * nx + x for x in range(nx)] for z in range(nz)]
        return [lax.all_gather(stack, "ctx", axis_index_groups=groups, tiled=True)]


def prepare_kernel(per_part, order, flags, own, *refs):
    parts, out = refs[:-1], refs[-1]
    part = order[pl.program_id(0)] // per_part
    rows = own.shape[0]
    out[:, pl.ds(pl.multiple_of(flags[0] * rows, rows), rows)] = own[...].T
    for mask, ref in enumerate(parts):

        @pl.when(part == flags[1] ^ mask)
        def _():
            out[:, pl.ds(pl.multiple_of((1 - flags[0]) * rows, rows), rows)] = ref[...].T


def prepare(order, flags, own, parts, depth):
    rows, features = own.shape
    count = features // depth
    per_part = count // len(parts)
    return pl.pallas_call(
        functools.partial(prepare_kernel, per_part),
        out_shape=jax.ShapeDtypeStruct((features, 2 * rows), BF16),
        grid_spec=pltpu.PrefetchScalarGridSpec(
            num_scalar_prefetch=2,
            grid=(count,),
            in_specs=[pl.BlockSpec((rows, depth), lambda i, o, f: (0, o[i]))]
            + [pl.BlockSpec((rows, depth), lambda i, o, f: (0, o[i] % per_part))] * len(parts),
            out_specs=pl.BlockSpec((depth, 2 * rows), lambda i, o, f: (i, 0)),
        ),
        compiler_params=pltpu.CompilerParams(vmem_limit_bytes=VMEM_LIMIT),
        cost_estimate=pl.CostEstimate(
            flops=0, bytes_accessed=8 * rows * features, transcendentals=0
        ),
    )(order, flags, own, *parts)


def project_kernel(tokens, *refs):
    stacks, out = refs[:-1], refs[-1]
    pieces = [stack[index] for stack in stacks for index in range(stack.shape[0])]
    out[...] = jnp.dot(
        jnp.concatenate(pieces, axis=1), tokens[...], preferred_element_type=F32
    ).astype(out.dtype)


def project(tokens, stacks):
    features, rows = tokens.shape
    count, width, depth = stacks[0].shape
    tile, part = min(256, width), rows // 2
    return pl.pallas_call(
        project_kernel,
        out_shape=jax.ShapeDtypeStruct((width, rows), BF16),
        grid=(2, width // tile),
        in_specs=[pl.BlockSpec((features, part), lambda t, i: (0, t))]
        + [pl.BlockSpec((count, tile, depth), lambda t, i: (0, i, 0))] * len(stacks),
        out_specs=pl.BlockSpec((tile, part), lambda t, i: (i, t)),
        compiler_params=pltpu.CompilerParams(vmem_limit_bytes=VMEM_LIMIT),
        cost_estimate=pl.CostEstimate(
            flops=2 * width * rows * features,
            bytes_accessed=2 * ((2 * width + rows) * features + width * rows),
            transcendentals=0,
        ),
    )(tokens, *stacks)


def featurize(rim, value, coefficients, first, span):
    wide = jnp.concatenate([rim, value], axis=1).astype(F32)
    total = coefficients[:, first : first + 1] * wide
    for offset in range(1, span):
        total = total + coefficients[:, first + offset : first + offset + 1] * pltpu.roll(
            wide, offset, 1
        )
    return total[:, rim.shape[1] :]


def filter_kernel(span, k, v, k_rim, v_rim, before, coefficients, bands, out):
    coef = coefficients[...]
    first = featurize(k_rim[...], k[...], coef, span, span)
    second = featurize(v_rim[...], v[...], coef, 2 * span, span)
    gated = (first * second).astype(BF16)
    wide = jnp.concatenate([before[...], gated], axis=1)
    groups, reach, taps = bands.shape
    size = wide.shape[0] // groups
    blocks = gated.shape[1] // taps
    for group in range(groups):
        rows = slice(group * size, (group + 1) * size)
        windows = jnp.concatenate(
            [wide[rows, block * taps : block * taps + reach] for block in range(blocks)], axis=0
        )
        sums = jnp.dot(windows, bands[group], preferred_element_type=F32)
        gain = coef[rows, 3 * span : 3 * span + 1]
        for block in range(blocks):
            lanes = slice(block * taps, (block + 1) * taps)
            out[rows, lanes] = sums[block * size : (block + 1) * size] + gain * gated[
                rows, lanes
            ].astype(F32)


def long_filter_part(span, k, v, k_rim, v_rim, before, coefficients, bands):
    width, rows = k.shape
    groups, reach, taps = bands.shape
    tile, part = min(128, width), rows // 2
    cell = lambda size: pl.BlockSpec((tile, size), lambda i, t: (i, t))
    return pl.pallas_call(
        functools.partial(filter_kernel, span),
        out_shape=jax.ShapeDtypeStruct((width, rows), F32),
        grid=(width // tile, 2),
        in_specs=[cell(part), cell(part), cell(taps), cell(taps), cell(taps)]
        + [
            pl.BlockSpec((tile, coefficients.shape[1]), lambda i, t: (i, 0)),
            pl.BlockSpec((groups * tile // width, reach, taps), lambda i, t: (i, 0, 0)),
        ],
        out_specs=cell(part),
        compiler_params=pltpu.CompilerParams(vmem_limit_bytes=VMEM_LIMIT),
        cost_estimate=pl.CostEstimate(
            flops=2 * width * rows * (reach + 4 * span),
            bytes_accessed=8 * width * rows + 2 * groups * reach * taps,
            transcendentals=0,
        ),
    )(k, v, k_rim, v_rim, before, coefficients, bands)


def mix_kernel(span, q, q_rim, filtered, coefficients, out):
    features = featurize(q_rim[...], q[...], coefficients[...], 0, span)
    out[...] = (features * filtered[...]).T.astype(BF16)


def mix(span, q, q_rim, filtered, coefficients):
    width, rows = q.shape
    tile, part = min(128, width), rows // 2
    cell = lambda size: pl.BlockSpec((tile, size), lambda i, t: (i, t))
    return pl.pallas_call(
        functools.partial(mix_kernel, span),
        out_shape=jax.ShapeDtypeStruct((rows, width), BF16),
        grid=(width // tile, 2),
        in_specs=[
            cell(part),
            cell(q_rim.shape[1] // 2),
            cell(part),
            pl.BlockSpec((tile, coefficients.shape[1]), lambda i, t: (i, 0)),
        ],
        out_specs=pl.BlockSpec((part, tile), lambda i, t: (t, i)),
        compiler_params=pltpu.CompilerParams(vmem_limit_bytes=VMEM_LIMIT),
        cost_estimate=pl.CostEstimate(
            flops=2 * width * rows * span, bytes_accessed=8 * width * rows, transcendentals=0
        ),
    )(q, q_rim, filtered, coefficients)


def output_kernel(count, order, *refs):
    mixed, stacks, out = refs[:count], refs[count:-1], refs[-1]
    left = jnp.concatenate([ref[...] for ref in mixed], axis=1)
    width = stacks[0].shape[2]
    place = 0
    for stack in stacks:
        pieces = [stack[index] for index in range(stack.shape[0])]
        sums = jnp.dot(left, jnp.concatenate(pieces, axis=1), preferred_element_type=F32)
        for index in range(stack.shape[0]):
            out[order[place]] = sums[:, index * width : (index + 1) * width].astype(out.dtype)
            place += 1


def output_sums(order, mixed, stacks):
    rows, part = mixed[0].shape
    count, depth, width = stacks[0].shape
    blocks = count * len(stacks)
    tile = min(256, rows)
    return pl.pallas_call(
        functools.partial(output_kernel, len(mixed)),
        out_shape=jax.ShapeDtypeStruct((blocks, rows, width), BF16),
        grid_spec=pltpu.PrefetchScalarGridSpec(
            num_scalar_prefetch=1,
            grid=(rows // tile,),
            in_specs=[pl.BlockSpec((tile, part), lambda i, o: (i, 0))] * len(mixed)
            + [pl.BlockSpec((count, depth, width), lambda i, o: (0, 0, 0))] * len(stacks),
            out_specs=pl.BlockSpec((blocks, tile, width), lambda i, o: (0, i, 0)),
        ),
        compiler_params=pltpu.CompilerParams(vmem_limit_bytes=VMEM_LIMIT),
        cost_estimate=pl.CostEstimate(
            flops=2 * rows * depth * blocks * width,
            bytes_accessed=2 * (rows * depth + depth * blocks * width + rows * blocks * width),
            transcendentals=0,
        ),
    )(order, *mixed, *stacks)


def bands_of(filters):
    taps = filters.shape[1]
    source = jnp.arange(taps)[:, None]
    target = jnp.arange(taps)[None, :]
    distance = (target - source) % taps
    picker = (distance[None] == jnp.arange(taps)[:, None, None]).astype(BF16)
    full = jnp.einsum("gk,kji->gji", filters, picker, preferred_element_type=F32)
    same = target >= source
    before, current = jnp.where(same, 0.0, full), jnp.where(same, full, 0.0)
    return jnp.concatenate([before, current], axis=1).astype(BF16)


def tail_gate(k, v, taps_k, taps_v, reach, end):
    span = taps_k.shape[0]

    def features(value, taps):
        wide = value[:, end - reach - span + 1 : end].astype(F32)
        total = taps[0][:, None] * wide[:, span - 1 :]
        for offset in range(1, span):
            start = span - 1 - offset
            total = total + taps[offset][:, None] * wide[:, start : start + reach]
        return total

    return (features(k, taps_k) * features(v, taps_v)).astype(BF16)


def pick(value, index, axis):
    return lax.dynamic_index_in_dim(value, index, axis, keepdims=False)


def per_device(
    places, tokens, qkv_weight, short_filter, long_filter, decay_rate, skip_gain, out_weight
):
    rows, in_features = tokens.shape
    depth, width = qkv_weight.shape[1:]
    features = out_weight.shape[1]
    groups, taps = long_filter.shape
    span = short_filter.shape[1]
    ny, nx, nz = places.ny, places.nx, places.nz
    i, j = lax.axis_index("ctx"), lax.axis_index("tp")
    x, zl = i % nx, (i // nx) % 2
    y, core = j // 2, j % 2
    half = width // 2
    share = features // 2
    chunks = 2 if share >= 256 else 1
    chunk = share // chunks
    order = jnp.stack([(i - x + step) ^ m for step in range(nx) for m in places.masks()])
    order = order.astype(jnp.int32)
    flags = jnp.stack([zl, j]).astype(jnp.int32)
    line = Line(places)

    def halves(s, done=None):
        weight = after(qkv_weight, done)[s]
        return [
            lax.dynamic_slice_in_dim(weight, part * half, half, 1).T for part in (zl, 1 - zl)
        ]

    k_parts = halves(1)
    k_held = line.gather(*k_parts)

    size = in_features // places.tp
    parts = {
        0: places.flip(lax.dynamic_slice_in_dim(tokens, j * size, size, 1), ctx=nx)
    }
    for step in range(1, ny):
        parts[2 * step] = places.flip(parts[0], tp=2 * step)
    for mask in list(parts):
        parts[mask ^ 1] = places.flip(parts[mask], tp=1)

    v_held = line.gather(*halves(2, k_parts[1]))
    pieces = {1: line.cross(k_held)}
    q_held = line.gather(*halves(0, k_parts[1]))
    pieces[2] = line.cross(v_held)

    out_halves = out_weight.reshape(width, 2, share)
    rows_of = [pick(out_halves, core, 1), places.flip(pick(out_halves, 1 - core, 1), tp=1)]
    both = jnp.stack(rows_of).reshape(2, 2, half, share)
    out_own, out_other = (pick(both, part, 1).reshape(width, share) for part in (zl, 1 - zl))
    out_held = []
    for c in range(chunks):
        lanes = slice(c * chunk, (c + 1) * chunk)
        out_held.append(line.gather(out_own[:, lanes], out_other[:, lanes]))
        if c == 0:
            pieces[0] = line.cross(q_held)
    outs = [line.cross(held) for held in out_held]

    tokens = prepare(
        order, flags, tokens, [parts[mask] for mask in range(places.tp)], depth
    )

    tap_index = jnp.arange(taps, dtype=F32)
    filters = (long_filter * jnp.exp(-decay_rate[:, None] * tap_index[None, :])).astype(BF16)
    bands = bands_of(lax.dynamic_slice_in_dim(filters, zl * (groups // 2), groups // 2))
    short = lax.dynamic_slice_in_dim(short_filter, zl * half, half, 2)
    gain = lax.dynamic_slice_in_dim(skip_gain, zl * half, half)
    coefficients = jnp.concatenate([short.reshape(3 * span, half), gain[None, :]]).T
    coefficients = jnp.pad(coefficients, ((0, 0), (0, (-3 * span - 1) % 8)))

    def halos(tails):
        beside = places.send(tails, lambda i, j: (i - i % nx + (i + 1) % nx, j))
        below = places.send(
            tails[1],
            lambda i, j: (i + 2 * nx - nx + 1, j)
            if i % nx == nx - 1 and i + 2 * nx < places.ctx
            else None,
        )
        start = x == 0
        return [jnp.where(start, below, beside[0]), jnp.where(start, beside[0], beside[1])]

    def rim_of(value):
        return jnp.pad(value.T, ((0, 0), (taps - value.shape[0], 0)))

    def rims(values):
        return jnp.concatenate([rim_of(value) for value in values], axis=1)

    edge = 8 * -(-(span - 1) // 8)
    ends = (rows, 2 * rows)
    k = project(tokens, pieces[1])
    u = project(tokens, pieces[2])
    tails = [
        jnp.concatenate(
            [
                tail_gate(k, u, short[1], short[2], taps, end).T,
                k[:, end - edge : end].T,
                u[:, end - edge : end].T,
            ]
        )
        for end in ends
    ]
    before = halos(jnp.stack(tails))
    filtered = long_filter_part(
        span,
        k,
        u,
        rims([value[taps : taps + edge] for value in before]),
        rims([value[taps + edge :] for value in before]),
        rims([value[:taps] for value in before]),
        coefficients,
        bands,
    )
    q = project(tokens, pieces[0])
    before = halos(jnp.stack([q[:, end - edge : end].T for end in ends]))
    mixed = mix(span, q, rims(before), filtered, coefficients)
    mixed = [mixed, places.flip(mixed, tp=1)]

    def over_y(value):
        total = pick(value, y, 1).astype(F32)
        for step in range(1, ny):
            total = total + places.flip(pick(value, y ^ step, 1), tp=2 * step).astype(F32)
        return total.astype(BF16)

    def over_z(value):
        other = places.flip(pick(value, 1 - zl, 1), ctx=nx)
        return (pick(value, zl, 1).astype(F32) + other.astype(F32)).astype(BF16)

    results = []
    blocks = places.ctx
    part = rows // ny
    for c in range(chunks):
        sums = output_sums(order, mixed, outs[c])
        if c + 1 < chunks or chunks == 1:
            value = sums.reshape(blocks * 2, ny, part, chunk)
            value = over_z(over_y(value).reshape(blocks, 2, part, chunk))
        else:
            value = over_z(sums.reshape(blocks, 2, rows, chunk))
            value = over_y(value.reshape(blocks, ny, part, chunk))
        value = value.reshape(blocks, 2, part // 2, chunk)
        mine = pick(value, core, 1)
        yours = places.flip(pick(value, 1 - core, 1), tp=1)
        pair = jnp.stack(
            [jnp.where(core == 0, mine, yours), jnp.where(core == 0, yours, mine)], axis=1
        )
        results.append(pair)
    result = jnp.stack(results, axis=2)
    return result.transpose(3, 0, 1, 2, 4).reshape(part // 2, -1)


def solution(mesh):
    in_specs = (
        P("ctx", None),
        P(None, "ctx", "tp"),
        P(None, None, "tp"),
        P("tp", None),
        P("tp"),
        P("tp"),
        P("tp", "ctx"),
    )
    places = Places(mesh.shape["ctx"], mesh.shape["tp"])
    return jax.shard_map(
        functools.partial(per_device, places),
        mesh=mesh,
        in_specs=in_specs,
        out_specs=P(AXES, None),
        check_vma=False,
    )
```

```python
import functools

import jax
import jax.numpy as jnp
from jax import lax
from jax.experimental import pallas as pl
from jax.experimental.pallas import tpu as pltpu
from jax.sharding import PartitionSpec as P

AXES = ("ctx", "tp")
BF16, F32 = jnp.bfloat16, jnp.float32
VMEM_LIMIT = 56 << 20


class Places:
    def __init__(self, ctx, tp):
        self.ctx, self.tp = ctx, tp
        self.nx = 1 << ((ctx.bit_length() - 1) // 2)
        self.nz = ctx // self.nx
        self.ny = tp // 2

    def send(self, value, target):
        pairs = []
        for i in range(self.ctx):
            for j in range(self.tp):
                to = target(i, j)
                if to is not None:
                    pairs.append((i * self.tp + j, to[0] * self.tp + to[1]))
        return lax.ppermute(value, AXES, pairs)

    def flip(self, value, ctx=0, tp=0):
        return self.send(value, lambda i, j: (i ^ ctx, j ^ tp))

    def masks(self):
        return [m * self.nx for m in range(1, self.nz)]


def after(value, *done):
    done = [entry for entry in done if entry is not None]
    return lax.optimization_barrier((value, *done))[0] if done else value


class Line:
    def __init__(self, places):
        self.places, self.far = places, []

    def step(self, value, mask, *done):
        result = self.places.flip(
            after(value, self.far[-3] if len(self.far) >= 3 else None, *done), ctx=mask
        )
        self.far.append(result)
        return result

    def gather(self, own, other, *done):
        nx, nz = self.places.nx, self.places.nz
        held = {}
        for m in sorted(range(1, nz), key=lambda m: (m < 2, m)):
            held[m] = self.step(other if m % 2 else own, m * nx, *done)
        return [held[m] for m in range(1, nz)]

    def beside(self, own):
        return [self.places.flip(own, ctx=step) for step in range(1, self.places.nx)]

    def cross(self, held, *done):
        nx, nz = self.places.nx, self.places.nz
        groups = [[z * nx + x for x in range(nx)] for z in range(nz)]
        return lax.all_gather(
            after(jnp.stack(held), *done), "ctx", axis_index_groups=groups, tiled=True
        )


def prepare_kernel(per_part, order, flags, own, *refs):
    parts, out = refs[:-1], refs[-1]
    part = order[pl.program_id(0)] // per_part
    rows = own.shape[0]
    out[:, pl.ds(pl.multiple_of(flags[0] * rows, rows), rows)] = own[...].T
    for mask, ref in enumerate(parts):

        @pl.when(part == flags[1] ^ mask)
        def _():
            out[:, pl.ds(pl.multiple_of((1 - flags[0]) * rows, rows), rows)] = ref[...].T


def prepare(order, flags, own, parts, depth):
    rows, features = own.shape
    count = features // depth
    per_part = count // len(parts)
    return pl.pallas_call(
        functools.partial(prepare_kernel, per_part),
        out_shape=jax.ShapeDtypeStruct((features, 2 * rows), BF16),
        grid_spec=pltpu.PrefetchScalarGridSpec(
            num_scalar_prefetch=2,
            grid=(count,),
            in_specs=[pl.BlockSpec((rows, depth), lambda i, o, f: (0, o[i]))]
            + [pl.BlockSpec((rows, depth), lambda i, o, f: (0, o[i] % per_part))] * len(parts),
            out_specs=pl.BlockSpec((depth, 2 * rows), lambda i, o, f: (i, 0)),
        ),
        compiler_params=pltpu.CompilerParams(vmem_limit_bytes=VMEM_LIMIT),
        cost_estimate=pl.CostEstimate(
            flops=0, bytes_accessed=8 * rows * features, transcendentals=0
        ),
    )(order, flags, own, *parts)


def project_kernel(tokens, *refs):
    stacks, out = refs[:-1], refs[-1]
    pieces = [stack[index] for stack in stacks for index in range(stack.shape[0])]
    out[...] = jnp.dot(
        jnp.concatenate(pieces, axis=1), tokens[...], preferred_element_type=F32
    ).astype(out.dtype)


def project(tokens, entries):
    features, rows = tokens.shape
    width, depth = entries[0][0].shape[1:]
    tile, part = min(256, width), rows // 2
    cell = lambda block, count: pl.BlockSpec((count, tile, depth), lambda t, i: (block, i, 0))
    return pl.pallas_call(
        project_kernel,
        out_shape=jax.ShapeDtypeStruct((width, rows), BF16),
        grid=(2, width // tile),
        in_specs=[pl.BlockSpec((features, part), lambda t, i: (0, t))]
        + [cell(block, count) for _, block, count in entries],
        out_specs=pl.BlockSpec((tile, part), lambda t, i: (i, t)),
        compiler_params=pltpu.CompilerParams(vmem_limit_bytes=VMEM_LIMIT),
        cost_estimate=pl.CostEstimate(
            flops=2 * width * rows * features,
            bytes_accessed=2 * ((2 * width + rows) * features + width * rows),
            transcendentals=0,
        ),
    )(tokens, *[stack for stack, _, _ in entries])


def featurize(rim, value, coefficients, first, span):
    wide = jnp.concatenate([rim, value], axis=1).astype(F32)
    total = coefficients[:, first : first + 1] * wide
    for offset in range(1, span):
        total = total + coefficients[:, first + offset : first + offset + 1] * pltpu.roll(
            wide, offset, 1
        )
    return total[:, rim.shape[1] :]


def filter_kernel(span, k, v, k_rim, v_rim, before, coefficients, bands, out):
    coef = coefficients[...]
    first = featurize(k_rim[...], k[...], coef, span, span)
    second = featurize(v_rim[...], v[...], coef, 2 * span, span)
    gated = (first * second).astype(BF16)
    wide = jnp.concatenate([before[...], gated], axis=1)
    groups, reach, taps = bands.shape
    size = wide.shape[0] // groups
    blocks = gated.shape[1] // taps
    for group in range(groups):
        rows = slice(group * size, (group + 1) * size)
        windows = jnp.concatenate(
            [wide[rows, block * taps : block * taps + reach] for block in range(blocks)], axis=0
        )
        sums = jnp.dot(windows, bands[group], preferred_element_type=F32)
        gain = coef[rows, 3 * span : 3 * span + 1]
        for block in range(blocks):
            lanes = slice(block * taps, (block + 1) * taps)
            out[rows, lanes] = sums[block * size : (block + 1) * size] + gain * gated[
                rows, lanes
            ].astype(F32)


def long_filter_part(span, k, v, k_rim, v_rim, before, coefficients, bands):
    width, rows = k.shape
    groups, reach, taps = bands.shape
    tile, part = min(128, width), rows // 2
    cell = lambda size: pl.BlockSpec((tile, size), lambda i, t: (i, t))
    return pl.pallas_call(
        functools.partial(filter_kernel, span),
        out_shape=jax.ShapeDtypeStruct((width, rows), F32),
        grid=(width // tile, 2),
        in_specs=[cell(part), cell(part), cell(taps), cell(taps), cell(taps)]
        + [
            pl.BlockSpec((tile, coefficients.shape[1]), lambda i, t: (i, 0)),
            pl.BlockSpec((groups * tile // width, reach, taps), lambda i, t: (i, 0, 0)),
        ],
        out_specs=cell(part),
        compiler_params=pltpu.CompilerParams(vmem_limit_bytes=VMEM_LIMIT),
        cost_estimate=pl.CostEstimate(
            flops=2 * width * rows * (reach + 4 * span),
            bytes_accessed=8 * width * rows + 2 * groups * reach * taps,
            transcendentals=0,
        ),
    )(k, v, k_rim, v_rim, before, coefficients, bands)


def mix_kernel(span, q, q_rim, filtered, coefficients, out):
    features = featurize(q_rim[...], q[...], coefficients[...], 0, span)
    out[...] = (features * filtered[...]).T.astype(BF16)


def mix(span, q, q_rim, filtered, coefficients):
    width, rows = q.shape
    tile, part = min(128, width), rows // 2
    cell = lambda size: pl.BlockSpec((tile, size), lambda i, t: (i, t))
    return pl.pallas_call(
        functools.partial(mix_kernel, span),
        out_shape=jax.ShapeDtypeStruct((rows, width), BF16),
        grid=(width // tile, 2),
        in_specs=[
            cell(part),
            cell(q_rim.shape[1] // 2),
            cell(part),
            pl.BlockSpec((tile, coefficients.shape[1]), lambda i, t: (i, 0)),
        ],
        out_specs=pl.BlockSpec((part, tile), lambda i, t: (t, i)),
        compiler_params=pltpu.CompilerParams(vmem_limit_bytes=VMEM_LIMIT),
        cost_estimate=pl.CostEstimate(
            flops=2 * width * rows * span, bytes_accessed=8 * width * rows, transcendentals=0
        ),
    )(q, q_rim, filtered, coefficients)


def output_kernel(count, order, *refs):
    mixed, stacks, out = refs[:count], refs[count:-1], refs[-1]
    left = jnp.concatenate([ref[...] for ref in mixed], axis=1)
    width = stacks[0].shape[2]
    place = 0
    for stack in stacks:
        pieces = [stack[index] for index in range(stack.shape[0])]
        sums = jnp.dot(left, jnp.concatenate(pieces, axis=1), preferred_element_type=F32)
        for index in range(stack.shape[0]):
            out[order[place]] = sums[:, index * width : (index + 1) * width].astype(out.dtype)
            place += 1


def output_sums(order, mixed, stacks):
    rows, part = mixed[0].shape
    depth, width = stacks[0].shape[1:]
    blocks = sum(stack.shape[0] for stack in stacks)
    tile = min(256, rows)
    return pl.pallas_call(
        functools.partial(output_kernel, len(mixed)),
        out_shape=jax.ShapeDtypeStruct((blocks, rows, width), BF16),
        grid_spec=pltpu.PrefetchScalarGridSpec(
            num_scalar_prefetch=1,
            grid=(rows // tile,),
            in_specs=[pl.BlockSpec((tile, part), lambda i, o: (i, 0))] * len(mixed)
            + [pl.BlockSpec(stack.shape, lambda i, o: (0, 0, 0)) for stack in stacks],
            out_specs=pl.BlockSpec((blocks, tile, width), lambda i, o: (0, i, 0)),
        ),
        compiler_params=pltpu.CompilerParams(vmem_limit_bytes=VMEM_LIMIT),
        cost_estimate=pl.CostEstimate(
            flops=2 * rows * depth * blocks * width,
            bytes_accessed=2 * (rows * depth + depth * blocks * width + rows * blocks * width),
            transcendentals=0,
        ),
    )(order, *mixed, *stacks)


def bands_of(filters):
    taps = filters.shape[1]
    source = jnp.arange(taps)[:, None]
    target = jnp.arange(taps)[None, :]
    distance = (target - source) % taps
    picker = (distance[None] == jnp.arange(taps)[:, None, None]).astype(BF16)
    full = jnp.einsum("gk,kji->gji", filters, picker, preferred_element_type=F32)
    same = target >= source
    before, current = jnp.where(same, 0.0, full), jnp.where(same, full, 0.0)
    return jnp.concatenate([before, current], axis=1).astype(BF16)


def tail_gate(k, v, taps_k, taps_v, reach, end):
    span = taps_k.shape[0]

    def features(value, taps):
        wide = value[:, end - reach - span + 1 : end].astype(F32)
        total = taps[0][:, None] * wide[:, span - 1 :]
        for offset in range(1, span):
            start = span - 1 - offset
            total = total + taps[offset][:, None] * wide[:, start : start + reach]
        return total

    return (features(k, taps_k) * features(v, taps_v)).astype(BF16)


def pick(value, index, axis):
    return lax.dynamic_index_in_dim(value, index, axis, keepdims=False)


def per_device(
    places, tokens, qkv_weight, short_filter, long_filter, decay_rate, skip_gain, out_weight
):
    rows, in_features = tokens.shape
    depth, width = qkv_weight.shape[1:]
    features = out_weight.shape[1]
    groups, taps = long_filter.shape
    span = short_filter.shape[1]
    ny, nx, nz = places.ny, places.nx, places.nz
    i, j = lax.axis_index("ctx"), lax.axis_index("tp")
    x, zl = i % nx, (i // nx) % 2
    y, core = j // 2, j % 2
    half = width // 2
    share = features // 2
    chunks = 2 if share >= 256 else 1
    chunk = share // chunks
    order = [i ^ step for step in range(nx)]
    order += [(i - x + step) ^ m for step in range(nx) for m in places.masks()]
    order = jnp.stack(order).astype(jnp.int32)
    flags = jnp.stack([zl, j]).astype(jnp.int32)
    line = Line(places)

    def halves(s):
        return [
            lax.dynamic_slice_in_dim(qkv_weight[s], part * half, half, 1).T
            for part in (zl, 1 - zl)
        ]

    q_parts, k_parts, v_parts = (halves(s) for s in range(3))
    own = jnp.stack([q_parts[0], k_parts[0], v_parts[0]])
    k_held = line.gather(*k_parts)
    beside = line.beside(own)

    size = in_features // places.tp
    parts = {
        0: places.flip(
            after(lax.dynamic_slice_in_dim(tokens, j * size, size, 1), line.far[0]), ctx=nx
        )
    }
    v_held = line.gather(*v_parts, *beside)
    k_cross = line.cross(k_held)
    for step in range(1, ny):
        parts[2 * step] = places.flip(parts[0], tp=2 * step)

    out_halves = out_weight.reshape(width, 2, share)
    rows_of = [pick(out_halves, core, 1), places.flip(pick(out_halves, 1 - core, 1), tp=1)]
    both = jnp.stack(rows_of).reshape(2, 2, half, share)
    out_own, out_other = (pick(both, part, 1).reshape(width, share) for part in (zl, 1 - zl))
    out_beside = line.beside(out_own)

    q_held = line.gather(*q_parts, parts[0], k_cross)
    v_cross = line.cross(v_held)
    for mask in list(parts):
        parts[mask ^ 1] = places.flip(parts[mask], tp=1)
    out_held = []
    for c in range(chunks):
        lanes = slice(c * chunk, (c + 1) * chunk)
        done = parts.values() if c else [parts[mask] for mask in parts if mask % 2 == 0]
        out_held.append(
            line.gather(out_own[:, lanes], out_other[:, lanes], *done, *out_beside, v_cross)
        )
        if c == 0:
            q_cross = line.cross(q_held)

    def entries(s, crossed):
        return [(stack, s, 1) for stack in [own] + beside] + [(crossed, 0, crossed.shape[0])]

    tokens = prepare(
        order, flags, tokens, [parts[mask] for mask in range(places.tp)], depth
    )

    tap_index = jnp.arange(taps, dtype=F32)
    filters = (long_filter * jnp.exp(-decay_rate[:, None] * tap_index[None, :])).astype(BF16)
    bands = bands_of(lax.dynamic_slice_in_dim(filters, zl * (groups // 2), groups // 2))
    short = lax.dynamic_slice_in_dim(short_filter, zl * half, half, 2)
    gain = lax.dynamic_slice_in_dim(skip_gain, zl * half, half)
    coefficients = jnp.concatenate([short.reshape(3 * span, half), gain[None, :]]).T
    coefficients = jnp.pad(coefficients, ((0, 0), (0, (-3 * span - 1) % 8)))

    def halos(tails):
        beside = places.send(tails, lambda i, j: (i - i % nx + (i + 1) % nx, j))
        below = places.send(
            tails[1],
            lambda i, j: (i + 2 * nx - nx + 1, j)
            if i % nx == nx - 1 and i + 2 * nx < places.ctx
            else None,
        )
        start = x == 0
        return [jnp.where(start, below, beside[0]), jnp.where(start, beside[0], beside[1])]

    def rim_of(value):
        return jnp.pad(value.T, ((0, 0), (taps - value.shape[0], 0)))

    def rims(values):
        return jnp.concatenate([rim_of(value) for value in values], axis=1)

    edge = 8 * -(-(span - 1) // 8)
    ends = (rows, 2 * rows)
    k = project(tokens, entries(1, k_cross))
    u = project(tokens, entries(2, v_cross))
    outs, out_cross = [], []
    for held in out_held:
        out_cross.append(line.cross(held, q_cross, k, u, *out_held[-1], *out_cross))
    for c in range(chunks):
        near = [stack[None, :, c * chunk : (c + 1) * chunk] for stack in [out_own] + out_beside]
        outs.append(near + [out_cross[c]])
    tails = [
        jnp.concatenate(
            [
                tail_gate(k, u, short[1], short[2], taps, end).T,
                k[:, end - edge : end].T,
                u[:, end - edge : end].T,
            ]
        )
        for end in ends
    ]
    before = halos(jnp.stack(tails))
    filtered = long_filter_part(
        span,
        k,
        u,
        rims([value[taps : taps + edge] for value in before]),
        rims([value[taps + edge :] for value in before]),
        rims([value[:taps] for value in before]),
        after(coefficients, out_cross[0]),
        bands,
    )
    q = project(tokens, entries(0, q_cross))
    before = halos(jnp.stack([q[:, end - edge : end].T for end in ends]))
    mixed = mix(span, q, rims(before), filtered, after(coefficients, out_cross[-1]))
    mixed = [mixed, places.flip(mixed, tp=1)]

    def over_y(value):
        total = pick(value, y, 1).astype(F32)
        for step in range(1, ny):
            total = total + places.flip(pick(value, y ^ step, 1), tp=2 * step).astype(F32)
        return total.astype(BF16)

    def over_z(value):
        other = places.flip(pick(value, 1 - zl, 1), ctx=nx)
        return (pick(value, zl, 1).astype(F32) + other.astype(F32)).astype(BF16)

    results = []
    blocks = places.ctx
    part = rows // ny
    sums = None
    for c in range(chunks):
        sums = output_sums(after(order, sums), mixed, outs[c])
        if c + 1 < chunks or chunks == 1:
            value = sums.reshape(blocks * 2, ny, part, chunk)
            value = over_z(over_y(value).reshape(blocks, 2, part, chunk))
        else:
            value = over_z(sums.reshape(blocks, 2, rows, chunk))
            value = over_y(value.reshape(blocks, ny, part, chunk))
        value = value.reshape(blocks, 2, part // 2, chunk)
        mine = pick(value, core, 1)
        yours = places.flip(pick(value, 1 - core, 1), tp=1)
        pair = jnp.stack(
            [jnp.where(core == 0, mine, yours), jnp.where(core == 0, yours, mine)], axis=1
        )
        results.append(pair)
    result = jnp.stack(results, axis=2)
    return result.transpose(3, 0, 1, 2, 4).reshape(part // 2, -1)


def solution(mesh):
    in_specs = (
        P("ctx", None),
        P(None, "ctx", "tp"),
        P(None, None, "tp"),
        P("tp", None),
        P("tp"),
        P("tp"),
        P("tp", "ctx"),
    )
    places = Places(mesh.shape["ctx"], mesh.shape["tp"])
    return jax.shard_map(
        functools.partial(per_device, places),
        mesh=mesh,
        in_specs=in_specs,
        out_specs=P(AXES, None),
        check_vma=False,
    )
```

```python
import functools

import jax
import jax.numpy as jnp
from jax import lax
from jax.experimental import pallas as pl
from jax.experimental.pallas import tpu as pltpu
from jax.sharding import PartitionSpec as P

AXES = ("ctx", "tp")
BF16, F32 = jnp.bfloat16, jnp.float32
VMEM_LIMIT = 56 << 20


class Places:
    def __init__(self, ctx, tp):
        self.ctx, self.tp = ctx, tp
        self.nx = 1 << ((ctx.bit_length() - 1) // 2)
        self.nz = ctx // self.nx
        self.ny = tp // 2

    def send(self, value, target):
        pairs = []
        for i in range(self.ctx):
            for j in range(self.tp):
                to = target(i, j)
                if to is not None:
                    pairs.append((i * self.tp + j, to[0] * self.tp + to[1]))
        return lax.ppermute(value, AXES, pairs)

    def flip(self, value, ctx=0, tp=0):
        return self.send(value, lambda i, j: (i ^ ctx, j ^ tp))

    def masks(self):
        return [m * self.nx for m in range(self.nz)]


def after(value, *done):
    done = [entry for entry in done if entry is not None]
    return lax.optimization_barrier((value, *done))[0] if done else value


class Line:
    def __init__(self, places):
        self.places, self.far = places, []

    def step(self, value, mask, *done):
        result = self.places.flip(
            after(value, self.far[-3] if len(self.far) >= 3 else None, *done), ctx=mask
        )
        self.far.append(result)
        return result

    def gather(self, own, other, *last):
        nx, nz = self.places.nx, self.places.nz
        held = {0: own}
        masks = sorted(range(1, nz), key=lambda m: (m < 2, m))
        for m in masks:
            held[m] = self.step(
                other if m % 2 else own, m * nx, *(last if m == masks[-1] else ())
            )
        return held

    def cross(self, held, *done):
        nx, nz = self.places.nx, self.places.nz
        stack = after(jnp.stack([held[m] for m in range(nz)]), *done)
        groups = [[z * nx + x for x in range(nx)] for z in range(nz)]
        return [lax.all_gather(stack, "ctx", axis_index_groups=groups, tiled=True)]


def prepare_kernel(per_part, order, flags, own, *refs):
    parts, out = refs[:-1], refs[-1]
    part = order[pl.program_id(0)] // per_part
    rows = own.shape[0]
    out[:, pl.ds(pl.multiple_of(flags[0] * rows, rows), rows)] = own[...].T
    for mask, ref in enumerate(parts):

        @pl.when(part == flags[1] ^ mask)
        def _():
            out[:, pl.ds(pl.multiple_of((1 - flags[0]) * rows, rows), rows)] = ref[...].T


def prepare(order, flags, own, parts, depth):
    rows, features = own.shape
    count = features // depth
    per_part = count // len(parts)
    return pl.pallas_call(
        functools.partial(prepare_kernel, per_part),
        out_shape=jax.ShapeDtypeStruct((features, 2 * rows), BF16),
        grid_spec=pltpu.PrefetchScalarGridSpec(
            num_scalar_prefetch=2,
            grid=(count,),
            in_specs=[pl.BlockSpec((rows, depth), lambda i, o, f: (0, o[i]))]
            + [pl.BlockSpec((rows, depth), lambda i, o, f: (0, o[i] % per_part))] * len(parts),
            out_specs=pl.BlockSpec((depth, 2 * rows), lambda i, o, f: (i, 0)),
        ),
        compiler_params=pltpu.CompilerParams(vmem_limit_bytes=VMEM_LIMIT),
        cost_estimate=pl.CostEstimate(
            flops=0, bytes_accessed=8 * rows * features, transcendentals=0
        ),
    )(order, flags, own, *parts)


def project_kernel(tokens, *refs):
    stacks, out = refs[:-1], refs[-1]
    pieces = [stack[index] for stack in stacks for index in range(stack.shape[0])]
    out[...] = jnp.dot(
        jnp.concatenate(pieces, axis=1), tokens[...], preferred_element_type=F32
    ).astype(out.dtype)


def project(tokens, stacks):
    features, rows = tokens.shape
    count, width, depth = stacks[0].shape
    tile, part = min(256, width), rows // 2
    return pl.pallas_call(
        project_kernel,
        out_shape=jax.ShapeDtypeStruct((width, rows), BF16),
        grid=(2, width // tile),
        in_specs=[pl.BlockSpec((features, part), lambda t, i: (0, t))]
        + [pl.BlockSpec((count, tile, depth), lambda t, i: (0, i, 0))] * len(stacks),
        out_specs=pl.BlockSpec((tile, part), lambda t, i: (i, t)),
        compiler_params=pltpu.CompilerParams(vmem_limit_bytes=VMEM_LIMIT),
        cost_estimate=pl.CostEstimate(
            flops=2 * width * rows * features,
            bytes_accessed=2 * ((2 * width + rows) * features + width * rows),
            transcendentals=0,
        ),
    )(tokens, *stacks)


def featurize(rim, value, coefficients, first, span):
    wide = jnp.concatenate([rim, value], axis=1).astype(F32)
    total = coefficients[:, first : first + 1] * wide
    for offset in range(1, span):
        total = total + coefficients[:, first + offset : first + offset + 1] * pltpu.roll(
            wide, offset, 1
        )
    return total[:, rim.shape[1] :]


def filter_kernel(span, k, v, k_rim, v_rim, before, coefficients, bands, out):
    coef = coefficients[...]
    first = featurize(k_rim[...], k[...], coef, span, span)
    second = featurize(v_rim[...], v[...], coef, 2 * span, span)
    gated = (first * second).astype(BF16)
    wide = jnp.concatenate([before[...], gated], axis=1)
    groups, reach, taps = bands.shape
    size = wide.shape[0] // groups
    blocks = gated.shape[1] // taps
    for group in range(groups):
        rows = slice(group * size, (group + 1) * size)
        windows = jnp.concatenate(
            [wide[rows, block * taps : block * taps + reach] for block in range(blocks)], axis=0
        )
        sums = jnp.dot(windows, bands[group], preferred_element_type=F32)
        gain = coef[rows, 3 * span : 3 * span + 1]
        for block in range(blocks):
            lanes = slice(block * taps, (block + 1) * taps)
            out[rows, lanes] = sums[block * size : (block + 1) * size] + gain * gated[
                rows, lanes
            ].astype(F32)


def long_filter_part(span, k, v, k_rim, v_rim, before, coefficients, bands):
    width, rows = k.shape
    groups, reach, taps = bands.shape
    tile, part = min(128, width), rows // 2
    cell = lambda size: pl.BlockSpec((tile, size), lambda i, t: (i, t))
    return pl.pallas_call(
        functools.partial(filter_kernel, span),
        out_shape=jax.ShapeDtypeStruct((width, rows), F32),
        grid=(width // tile, 2),
        in_specs=[cell(part), cell(part), cell(taps), cell(taps), cell(taps)]
        + [
            pl.BlockSpec((tile, coefficients.shape[1]), lambda i, t: (i, 0)),
            pl.BlockSpec((groups * tile // width, reach, taps), lambda i, t: (i, 0, 0)),
        ],
        out_specs=cell(part),
        compiler_params=pltpu.CompilerParams(vmem_limit_bytes=VMEM_LIMIT),
        cost_estimate=pl.CostEstimate(
            flops=2 * width * rows * (reach + 4 * span),
            bytes_accessed=8 * width * rows + 2 * groups * reach * taps,
            transcendentals=0,
        ),
    )(k, v, k_rim, v_rim, before, coefficients, bands)


def mix_kernel(span, q, q_rim, filtered, coefficients, out):
    features = featurize(q_rim[...], q[...], coefficients[...], 0, span)
    out[...] = (features * filtered[...]).T.astype(BF16)


def mix(span, q, q_rim, filtered, coefficients):
    width, rows = q.shape
    tile, part = min(128, width), rows // 2
    cell = lambda size: pl.BlockSpec((tile, size), lambda i, t: (i, t))
    return pl.pallas_call(
        functools.partial(mix_kernel, span),
        out_shape=jax.ShapeDtypeStruct((rows, width), BF16),
        grid=(width // tile, 2),
        in_specs=[
            cell(part),
            cell(q_rim.shape[1] // 2),
            cell(part),
            pl.BlockSpec((tile, coefficients.shape[1]), lambda i, t: (i, 0)),
        ],
        out_specs=pl.BlockSpec((part, tile), lambda i, t: (t, i)),
        compiler_params=pltpu.CompilerParams(vmem_limit_bytes=VMEM_LIMIT),
        cost_estimate=pl.CostEstimate(
            flops=2 * width * rows * span, bytes_accessed=8 * width * rows, transcendentals=0
        ),
    )(q, q_rim, filtered, coefficients)


def output_kernel(count, order, *refs):
    mixed, stacks, out = refs[:count], refs[count:-1], refs[-1]
    left = jnp.concatenate([ref[...] for ref in mixed], axis=1)
    width = stacks[0].shape[2]
    place = 0
    for stack in stacks:
        pieces = [stack[index] for index in range(stack.shape[0])]
        sums = jnp.dot(left, jnp.concatenate(pieces, axis=1), preferred_element_type=F32)
        for index in range(stack.shape[0]):
            out[order[place]] = sums[:, index * width : (index + 1) * width].astype(out.dtype)
            place += 1


def output_sums(order, mixed, stacks, c, width):
    rows, part = mixed[0].shape
    count, depth, _ = stacks[0].shape
    blocks = count * len(stacks)
    tile = min(256, rows)
    return pl.pallas_call(
        functools.partial(output_kernel, len(mixed)),
        out_shape=jax.ShapeDtypeStruct((blocks, rows, width), BF16),
        grid_spec=pltpu.PrefetchScalarGridSpec(
            num_scalar_prefetch=1,
            grid=(rows // tile,),
            in_specs=[pl.BlockSpec((tile, part), lambda i, o: (i, 0))] * len(mixed)
            + [pl.BlockSpec((count, depth, width), lambda i, o: (0, 0, c))] * len(stacks),
            out_specs=pl.BlockSpec((blocks, tile, width), lambda i, o: (0, i, 0)),
        ),
        compiler_params=pltpu.CompilerParams(vmem_limit_bytes=VMEM_LIMIT),
        cost_estimate=pl.CostEstimate(
            flops=2 * rows * depth * blocks * width,
            bytes_accessed=2 * (rows * depth + depth * blocks * width + rows * blocks * width),
            transcendentals=0,
        ),
    )(order, *mixed, *stacks)


def bands_of(filters):
    taps = filters.shape[1]
    source = jnp.arange(taps)[:, None]
    target = jnp.arange(taps)[None, :]
    distance = (target - source) % taps
    picker = (distance[None] == jnp.arange(taps)[:, None, None]).astype(BF16)
    full = jnp.einsum("gk,kji->gji", filters, picker, preferred_element_type=F32)
    same = target >= source
    before, current = jnp.where(same, 0.0, full), jnp.where(same, full, 0.0)
    return jnp.concatenate([before, current], axis=1).astype(BF16)


def tail_gate(k, v, taps_k, taps_v, reach, end):
    span = taps_k.shape[0]

    def features(value, taps):
        wide = value[:, end - reach - span + 1 : end].astype(F32)
        total = taps[0][:, None] * wide[:, span - 1 :]
        for offset in range(1, span):
            start = span - 1 - offset
            total = total + taps[offset][:, None] * wide[:, start : start + reach]
        return total

    return (features(k, taps_k) * features(v, taps_v)).astype(BF16)


def pick(value, index, axis):
    return lax.dynamic_index_in_dim(value, index, axis, keepdims=False)


def per_device(
    places, tokens, qkv_weight, short_filter, long_filter, decay_rate, skip_gain, out_weight
):
    rows, in_features = tokens.shape
    depth, width = qkv_weight.shape[1:]
    features = out_weight.shape[1]
    groups, taps = long_filter.shape
    span = short_filter.shape[1]
    ny, nx, nz = places.ny, places.nx, places.nz
    i, j = lax.axis_index("ctx"), lax.axis_index("tp")
    x, zl = i % nx, (i // nx) % 2
    y, core = j // 2, j % 2
    half = width // 2
    share = features // 2
    chunks = 2 if share >= 256 else 1
    chunk = share // chunks
    order = jnp.stack([(i - x + step) ^ m for step in range(nx) for m in places.masks()])
    order = order.astype(jnp.int32)
    flags = jnp.stack([zl, j]).astype(jnp.int32)
    line = Line(places)

    def halves(s):
        return [
            lax.dynamic_slice_in_dim(qkv_weight[s], part * half, half, 1).T
            for part in (zl, 1 - zl)
        ]

    size = in_features // places.tp
    parts = {0: places.flip(lax.dynamic_slice_in_dim(tokens, j * size, size, 1), ctx=nx)}
    k_held = line.gather(*halves(1), parts[0])
    for step in range(1, ny):
        parts[2 * step] = places.flip(parts[0], tp=2 * step)
    pieces = {1: line.cross(k_held)}
    v_held = line.gather(*halves(2), *parts.values())
    for mask in list(parts):
        parts[mask ^ 1] = places.flip(parts[mask], tp=1)
    pieces[2] = line.cross(v_held)
    q_held = line.gather(*halves(0), *parts.values())
    pieces[0] = line.cross(q_held)
    tokens = prepare(
        order, flags, tokens, [parts[mask] for mask in range(places.tp)], depth
    )

    out_halves = out_weight.reshape(width, 2, share)
    rows_of = [pick(out_halves, core, 1), places.flip(pick(out_halves, 1 - core, 1), tp=1)]
    both = jnp.stack(rows_of).reshape(2, 2, half, share)
    out_own, out_other = (pick(both, part, 1).reshape(width, share) for part in (zl, 1 - zl))
    out_held = line.gather(out_own, out_other)

    tap_index = jnp.arange(taps, dtype=F32)
    filters = (long_filter * jnp.exp(-decay_rate[:, None] * tap_index[None, :])).astype(BF16)
    bands = bands_of(lax.dynamic_slice_in_dim(filters, zl * (groups // 2), groups // 2))
    short = lax.dynamic_slice_in_dim(short_filter, zl * half, half, 2)
    gain = lax.dynamic_slice_in_dim(skip_gain, zl * half, half)
    coefficients = jnp.concatenate([short.reshape(3 * span, half), gain[None, :]]).T
    coefficients = jnp.pad(coefficients, ((0, 0), (0, (-3 * span - 1) % 8)))

    def halos(tails):
        beside = places.send(tails, lambda i, j: (i - i % nx + (i + 1) % nx, j))
        below = places.send(
            tails[1],
            lambda i, j: (i + 2 * nx - nx + 1, j)
            if i % nx == nx - 1 and i + 2 * nx < places.ctx
            else None,
        )
        start = x == 0
        return [jnp.where(start, below, beside[0]), jnp.where(start, beside[0], beside[1])]

    def rim_of(value):
        return jnp.pad(value.T, ((0, 0), (taps - value.shape[0], 0)))

    def rims(values):
        return jnp.concatenate([rim_of(value) for value in values], axis=1)

    edge = 8 * -(-(span - 1) // 8)
    ends = (rows, 2 * rows)
    k = project(tokens, pieces[1])
    u = project(tokens, pieces[2])
    outs = line.cross(out_held, k, u)
    tails = [
        jnp.concatenate(
            [
                tail_gate(k, u, short[1], short[2], taps, end).T,
                k[:, end - edge : end].T,
                u[:, end - edge : end].T,
            ]
        )
        for end in ends
    ]
    before = halos(jnp.stack(tails))
    filtered = long_filter_part(
        span,
        k,
        u,
        rims([value[taps : taps + edge] for value in before]),
        rims([value[taps + edge :] for value in before]),
        rims([value[:taps] for value in before]),
        coefficients,
        bands,
    )
    q = project(tokens, [after(stack, filtered) for stack in pieces[0]])
    before = halos(jnp.stack([q[:, end - edge : end].T for end in ends]))
    mixed = mix(span, q, rims(before), filtered, coefficients)
    mixed = [mixed, places.flip(mixed, tp=1)]

    def over_y(value):
        total = pick(value, y, 1).astype(F32)
        for step in range(1, ny):
            total = total + places.flip(pick(value, y ^ step, 1), tp=2 * step).astype(F32)
        return total.astype(BF16)

    def over_z(value):
        other = places.flip(pick(value, 1 - zl, 1), ctx=nx)
        return (pick(value, zl, 1).astype(F32) + other.astype(F32)).astype(BF16)

    results = []
    blocks = places.ctx
    part = rows // ny
    sums = None
    for c in range(chunks):
        sums = output_sums(after(order, sums), mixed, outs, c, chunk)
        if c + 1 < chunks or chunks == 1:
            value = sums.reshape(blocks * 2, ny, part, chunk)
            value = over_z(over_y(value).reshape(blocks, 2, part, chunk))
        else:
            value = over_z(sums.reshape(blocks, 2, rows, chunk))
            value = over_y(value.reshape(blocks, ny, part, chunk))
        value = value.reshape(blocks, 2, part // 2, chunk)
        mine = pick(value, core, 1)
        yours = places.flip(pick(value, 1 - core, 1), tp=1)
        pair = jnp.stack(
            [jnp.where(core == 0, mine, yours), jnp.where(core == 0, yours, mine)], axis=1
        )
        results.append(pair)
    result = jnp.stack(results, axis=2)
    return result.transpose(3, 0, 1, 2, 4).reshape(part // 2, -1)


def solution(mesh):
    in_specs = (
        P("ctx", None),
        P(None, "ctx", "tp"),
        P(None, None, "tp"),
        P("tp", None),
        P("tp"),
        P("tp"),
        P("tp", "ctx"),
    )
    places = Places(mesh.shape["ctx"], mesh.shape["tp"])
    return jax.shard_map(
        functools.partial(per_device, places),
        mesh=mesh,
        in_specs=in_specs,
        out_specs=P(AXES, None),
        check_vma=False,
    )
```

```python
import functools

import jax
import jax.numpy as jnp
from jax import lax
from jax.experimental import pallas as pl
from jax.experimental.pallas import tpu as pltpu
from jax.sharding import PartitionSpec as P

AXES = ("ctx", "tp")
BF16, F32 = jnp.bfloat16, jnp.float32
VMEM_LIMIT = 56 << 20


class Places:
    def __init__(self, ctx, tp):
        self.ctx, self.tp = ctx, tp
        self.nx = 1 << ((ctx.bit_length() - 1) // 2)
        self.nz = ctx // self.nx
        self.ny = tp // 2

    def send(self, value, target):
        pairs = []
        for i in range(self.ctx):
            for j in range(self.tp):
                to = target(i, j)
                if to is not None:
                    pairs.append((i * self.tp + j, to[0] * self.tp + to[1]))
        return lax.ppermute(value, AXES, pairs)

    def flip(self, value, ctx=0, tp=0):
        return self.send(value, lambda i, j: (i ^ ctx, j ^ tp))

    def masks(self):
        return [m * self.nx for m in range(1, self.nz)]


def after(value, *done):
    done = [entry for entry in done if entry is not None]
    return lax.optimization_barrier((value, *done))[0] if done else value


class Line:
    def __init__(self, places):
        self.places, self.far = places, []

    def step(self, value, mask, *done):
        result = self.places.flip(
            after(value, self.far[-3] if len(self.far) >= 3 else None, *done), ctx=mask
        )
        self.far.append(result)
        return result

    def gather(self, own, other, *last):
        nx, nz = self.places.nx, self.places.nz
        held = {}
        masks = sorted(range(1, nz), key=lambda m: (m < 2, m))
        for m in masks:
            held[m] = self.step(
                other if m % 2 else own, m * nx, *(last if m == masks[-1] else ())
            )
        return held

    def beside(self, own):
        return [self.places.flip(own, ctx=step) for step in range(1, self.places.nx)]

    def cross(self, held, *done):
        nx, nz = self.places.nx, self.places.nz
        stack = after(jnp.stack([held[m] for m in range(1, nz)]), *done)
        groups = [[z * nx + x for x in range(nx)] for z in range(nz)]
        return lax.all_gather(stack, "ctx", axis_index_groups=groups, tiled=True)


def prepare_kernel(per_part, order, flags, own, *refs):
    parts, out = refs[:-1], refs[-1]
    part = order[pl.program_id(0)] // per_part
    rows = own.shape[0]
    out[:, pl.ds(pl.multiple_of(flags[0] * rows, rows), rows)] = own[...].T
    for mask, ref in enumerate(parts):

        @pl.when(part == flags[1] ^ mask)
        def _():
            out[:, pl.ds(pl.multiple_of((1 - flags[0]) * rows, rows), rows)] = ref[...].T


def prepare(order, flags, own, parts, depth):
    rows, features = own.shape
    count = features // depth
    per_part = count // len(parts)
    return pl.pallas_call(
        functools.partial(prepare_kernel, per_part),
        out_shape=jax.ShapeDtypeStruct((features, 2 * rows), BF16),
        grid_spec=pltpu.PrefetchScalarGridSpec(
            num_scalar_prefetch=2,
            grid=(count,),
            in_specs=[pl.BlockSpec((rows, depth), lambda i, o, f: (0, o[i]))]
            + [pl.BlockSpec((rows, depth), lambda i, o, f: (0, o[i] % per_part))] * len(parts),
            out_specs=pl.BlockSpec((depth, 2 * rows), lambda i, o, f: (i, 0)),
        ),
        compiler_params=pltpu.CompilerParams(vmem_limit_bytes=VMEM_LIMIT),
        cost_estimate=pl.CostEstimate(
            flops=0, bytes_accessed=8 * rows * features, transcendentals=0
        ),
    )(order, flags, own, *parts)


def project_kernel(tokens, *refs):
    stacks, out = refs[:-1], refs[-1]
    pieces = [stack[index] for stack in stacks for index in range(stack.shape[0])]
    out[...] = jnp.dot(
        jnp.concatenate(pieces, axis=1), tokens[...], preferred_element_type=F32
    ).astype(out.dtype)


def project(tokens, entries):
    features, rows = tokens.shape
    width, depth = entries[0][0].shape[1:]
    tile, part = min(256, width), rows // 2
    cell = lambda block, count: pl.BlockSpec((count, tile, depth), lambda t, i: (block, i, 0))
    return pl.pallas_call(
        project_kernel,
        out_shape=jax.ShapeDtypeStruct((width, rows), BF16),
        grid=(2, width // tile),
        in_specs=[pl.BlockSpec((features, part), lambda t, i: (0, t))]
        + [cell(block, count) for _, block, count in entries],
        out_specs=pl.BlockSpec((tile, part), lambda t, i: (i, t)),
        compiler_params=pltpu.CompilerParams(vmem_limit_bytes=VMEM_LIMIT),
        cost_estimate=pl.CostEstimate(
            flops=2 * width * rows * features,
            bytes_accessed=2 * ((2 * width + rows) * features + width * rows),
            transcendentals=0,
        ),
    )(tokens, *[stack for stack, _, _ in entries])


def featurize(rim, value, coefficients, first, span):
    wide = jnp.concatenate([rim, value], axis=1).astype(F32)
    total = coefficients[:, first : first + 1] * wide
    for offset in range(1, span):
        total = total + coefficients[:, first + offset : first + offset + 1] * pltpu.roll(
            wide, offset, 1
        )
    return total[:, rim.shape[1] :]


def filter_kernel(span, k, v, k_rim, v_rim, before, coefficients, bands, out):
    coef = coefficients[...]
    first = featurize(k_rim[...], k[...], coef, span, span)
    second = featurize(v_rim[...], v[...], coef, 2 * span, span)
    gated = (first * second).astype(BF16)
    wide = jnp.concatenate([before[...], gated], axis=1)
    groups, reach, taps = bands.shape
    size = wide.shape[0] // groups
    blocks = gated.shape[1] // taps
    for group in range(groups):
        rows = slice(group * size, (group + 1) * size)
        windows = jnp.concatenate(
            [wide[rows, block * taps : block * taps + reach] for block in range(blocks)], axis=0
        )
        sums = jnp.dot(windows, bands[group], preferred_element_type=F32)
        gain = coef[rows, 3 * span : 3 * span + 1]
        for block in range(blocks):
            lanes = slice(block * taps, (block + 1) * taps)
            out[rows, lanes] = sums[block * size : (block + 1) * size] + gain * gated[
                rows, lanes
            ].astype(F32)


def long_filter_part(span, k, v, k_rim, v_rim, before, coefficients, bands):
    width, rows = k.shape
    groups, reach, taps = bands.shape
    tile, part = min(128, width), rows // 2
    cell = lambda size: pl.BlockSpec((tile, size), lambda i, t: (i, t))
    return pl.pallas_call(
        functools.partial(filter_kernel, span),
        out_shape=jax.ShapeDtypeStruct((width, rows), F32),
        grid=(width // tile, 2),
        in_specs=[cell(part), cell(part), cell(taps), cell(taps), cell(taps)]
        + [
            pl.BlockSpec((tile, coefficients.shape[1]), lambda i, t: (i, 0)),
            pl.BlockSpec((groups * tile // width, reach, taps), lambda i, t: (i, 0, 0)),
        ],
        out_specs=cell(part),
        compiler_params=pltpu.CompilerParams(vmem_limit_bytes=VMEM_LIMIT),
        cost_estimate=pl.CostEstimate(
            flops=2 * width * rows * (reach + 4 * span),
            bytes_accessed=8 * width * rows + 2 * groups * reach * taps,
            transcendentals=0,
        ),
    )(k, v, k_rim, v_rim, before, coefficients, bands)


def mix_kernel(span, q, q_rim, filtered, coefficients, out):
    features = featurize(q_rim[...], q[...], coefficients[...], 0, span)
    out[...] = (features * filtered[...]).T.astype(BF16)


def mix(span, q, q_rim, filtered, coefficients):
    width, rows = q.shape
    tile, part = min(128, width), rows // 2
    cell = lambda size: pl.BlockSpec((tile, size), lambda i, t: (i, t))
    return pl.pallas_call(
        functools.partial(mix_kernel, span),
        out_shape=jax.ShapeDtypeStruct((rows, width), BF16),
        grid=(width // tile, 2),
        in_specs=[
            cell(part),
            cell(q_rim.shape[1] // 2),
            cell(part),
            pl.BlockSpec((tile, coefficients.shape[1]), lambda i, t: (i, 0)),
        ],
        out_specs=pl.BlockSpec((part, tile), lambda i, t: (t, i)),
        compiler_params=pltpu.CompilerParams(vmem_limit_bytes=VMEM_LIMIT),
        cost_estimate=pl.CostEstimate(
            flops=2 * width * rows * span, bytes_accessed=8 * width * rows, transcendentals=0
        ),
    )(q, q_rim, filtered, coefficients)


def output_kernel(count, chunks, order, *refs):
    mixed, stacks, outs = refs[:count], refs[count:-chunks], refs[-chunks:]
    left = jnp.concatenate([ref[...] for ref in mixed], axis=1)
    pieces = [stack[index] for stack in stacks for index in range(stack.shape[0])]
    width = outs[0].shape[2]
    for place, piece in enumerate(pieces):
        sums = jnp.dot(left, piece, preferred_element_type=F32)
        for c, out in enumerate(outs):
            out[order[place]] = sums[:, c * width : (c + 1) * width].astype(out.dtype)


def output_sums(order, mixed, stacks, chunks):
    rows, part = mixed[0].shape
    depth, share = stacks[0].shape[1:]
    width = share // chunks
    blocks = sum(stack.shape[0] for stack in stacks)
    tile = min(256, rows)
    return pl.pallas_call(
        functools.partial(output_kernel, len(mixed), chunks),
        out_shape=[jax.ShapeDtypeStruct((blocks, rows, width), BF16)] * chunks,
        grid_spec=pltpu.PrefetchScalarGridSpec(
            num_scalar_prefetch=1,
            grid=(rows // tile,),
            in_specs=[pl.BlockSpec((tile, part), lambda i, o: (i, 0))] * len(mixed)
            + [pl.BlockSpec(stack.shape, lambda i, o: (0, 0, 0)) for stack in stacks],
            out_specs=[pl.BlockSpec((blocks, tile, width), lambda i, o: (0, i, 0))] * chunks,
        ),
        compiler_params=pltpu.CompilerParams(vmem_limit_bytes=VMEM_LIMIT),
        cost_estimate=pl.CostEstimate(
            flops=2 * rows * depth * blocks * share,
            bytes_accessed=2 * (rows * depth + depth * blocks * share + rows * blocks * share),
            transcendentals=0,
        ),
    )(order, *mixed, *stacks)


def bands_of(filters):
    taps = filters.shape[1]
    source = jnp.arange(taps)[:, None]
    target = jnp.arange(taps)[None, :]
    distance = (target - source) % taps
    picker = (distance[None] == jnp.arange(taps)[:, None, None]).astype(BF16)
    full = jnp.einsum("gk,kji->gji", filters, picker, preferred_element_type=F32)
    same = target >= source
    before, current = jnp.where(same, 0.0, full), jnp.where(same, full, 0.0)
    return jnp.concatenate([before, current], axis=1).astype(BF16)


def tail_gate(k, v, taps_k, taps_v, reach, end):
    span = taps_k.shape[0]

    def features(value, taps):
        wide = value[:, end - reach - span + 1 : end].astype(F32)
        total = taps[0][:, None] * wide[:, span - 1 :]
        for offset in range(1, span):
            start = span - 1 - offset
            total = total + taps[offset][:, None] * wide[:, start : start + reach]
        return total

    return (features(k, taps_k) * features(v, taps_v)).astype(BF16)


def pick(value, index, axis):
    return lax.dynamic_index_in_dim(value, index, axis, keepdims=False)


def per_device(
    places, tokens, qkv_weight, short_filter, long_filter, decay_rate, skip_gain, out_weight
):
    rows, in_features = tokens.shape
    depth, width = qkv_weight.shape[1:]
    features = out_weight.shape[1]
    groups, taps = long_filter.shape
    span = short_filter.shape[1]
    ny, nx, nz = places.ny, places.nx, places.nz
    i, j = lax.axis_index("ctx"), lax.axis_index("tp")
    x, zl = i % nx, (i // nx) % 2
    y, core = j // 2, j % 2
    half = width // 2
    share = features // 2
    chunks = 2 if share >= 256 else 1
    chunk = share // chunks
    order = [i ^ step for step in range(nx)]
    order += [(i - x + step) ^ m for step in range(nx) for m in places.masks()]
    order = jnp.stack(order).astype(jnp.int32)
    flags = jnp.stack([zl, j]).astype(jnp.int32)
    line = Line(places)

    def halves(s):
        return [
            lax.dynamic_slice_in_dim(qkv_weight[s], part * half, half, 1).T
            for part in (zl, 1 - zl)
        ]

    q_parts, k_parts, v_parts = (halves(s) for s in range(3))
    own = jnp.stack([q_parts[0], k_parts[0], v_parts[0]])
    beside = line.beside(own)

    size = in_features // places.tp
    parts = {0: places.flip(lax.dynamic_slice_in_dim(tokens, j * size, size, 1), ctx=nx)}
    k_held = line.gather(*k_parts, parts[0], *beside)
    for step in range(1, ny):
        parts[2 * step] = places.flip(parts[0], tp=2 * step)
    k_cross = line.cross(k_held)

    out_halves = out_weight.reshape(width, 2, share)
    rows_of = [pick(out_halves, core, 1), places.flip(pick(out_halves, 1 - core, 1), tp=1)]
    both = jnp.stack(rows_of).reshape(2, 2, half, share)
    out_own, out_other = (pick(both, part, 1).reshape(width, share) for part in (zl, 1 - zl))

    v_held = line.gather(*v_parts, *parts.values())
    for mask in list(parts):
        parts[mask ^ 1] = places.flip(parts[mask], tp=1)
    v_cross = line.cross(v_held)
    tokens = prepare(
        order, flags, tokens, [parts[mask] for mask in range(places.tp)], depth
    )
    q_held = line.gather(*q_parts, tokens)
    q_cross = line.cross(q_held)
    out_beside = line.beside(out_own)

    def entries(s, crossed):
        return [(stack, s, 1) for stack in [own] + beside] + [(crossed, 0, crossed.shape[0])]

    k = project(tokens, entries(1, k_cross))
    out_held = line.gather(out_own, out_other, k, *out_beside)
    u = project(tokens, entries(2, v_cross))
    outs = [stack[None] for stack in [out_own] + out_beside]
    outs.append(line.cross(out_held, u))

    tap_index = jnp.arange(taps, dtype=F32)
    filters = (long_filter * jnp.exp(-decay_rate[:, None] * tap_index[None, :])).astype(BF16)
    bands = bands_of(lax.dynamic_slice_in_dim(filters, zl * (groups // 2), groups // 2))
    short = lax.dynamic_slice_in_dim(short_filter, zl * half, half, 2)
    gain = lax.dynamic_slice_in_dim(skip_gain, zl * half, half)
    coefficients = jnp.concatenate([short.reshape(3 * span, half), gain[None, :]]).T
    coefficients = jnp.pad(coefficients, ((0, 0), (0, (-3 * span - 1) % 8)))

    def halos(tails):
        beside = places.send(tails, lambda i, j: (i - i % nx + (i + 1) % nx, j))
        below = places.send(
            tails[1],
            lambda i, j: (i + 2 * nx - nx + 1, j)
            if i % nx == nx - 1 and i + 2 * nx < places.ctx
            else None,
        )
        start = x == 0
        return [jnp.where(start, below, beside[0]), jnp.where(start, beside[0], beside[1])]

    def rim_of(value):
        return jnp.pad(value.T, ((0, 0), (taps - value.shape[0], 0)))

    def rims(values):
        return jnp.concatenate([rim_of(value) for value in values], axis=1)

    edge = 8 * -(-(span - 1) // 8)
    ends = (rows, 2 * rows)
    tails = [
        jnp.concatenate(
            [
                tail_gate(k, u, short[1], short[2], taps, end).T,
                k[:, end - edge : end].T,
                u[:, end - edge : end].T,
            ]
        )
        for end in ends
    ]
    before = halos(jnp.stack(tails))
    filtered = long_filter_part(
        span,
        k,
        u,
        rims([value[taps : taps + edge] for value in before]),
        rims([value[taps + edge :] for value in before]),
        rims([value[:taps] for value in before]),
        coefficients,
        bands,
    )
    q = project(tokens, entries(0, after(q_cross, filtered, *out_held.values())))
    before = halos(jnp.stack([q[:, end - edge : end].T for end in ends]))
    mixed = mix(span, q, rims(before), filtered, coefficients)
    mixed = [mixed, places.flip(mixed, tp=1)]

    def over_y(value):
        total = pick(value, y, 1).astype(F32)
        for step in range(1, ny):
            total = total + places.flip(pick(value, y ^ step, 1), tp=2 * step).astype(F32)
        return total.astype(BF16)

    def over_z(value):
        other = places.flip(pick(value, 1 - zl, 1), ctx=nx)
        return (pick(value, zl, 1).astype(F32) + other.astype(F32)).astype(BF16)

    results = []
    blocks = places.ctx
    part = rows // ny
    for c, sums in enumerate(output_sums(order, mixed, outs, chunks)):
        if c + 1 < chunks or chunks == 1:
            value = sums.reshape(blocks * 2, ny, part, chunk)
            value = over_z(over_y(value).reshape(blocks, 2, part, chunk))
        else:
            value = over_z(sums.reshape(blocks, 2, rows, chunk))
            value = over_y(value.reshape(blocks, ny, part, chunk))
        value = value.reshape(blocks, 2, part // 2, chunk)
        mine = pick(value, core, 1)
        yours = places.flip(pick(value, 1 - core, 1), tp=1)
        pair = jnp.stack(
            [jnp.where(core == 0, mine, yours), jnp.where(core == 0, yours, mine)], axis=1
        )
        results.append(pair)
    result = jnp.stack(results, axis=2)
    return result.transpose(3, 0, 1, 2, 4).reshape(part // 2, -1)


def solution(mesh):
    in_specs = (
        P("ctx", None),
        P(None, "ctx", "tp"),
        P(None, None, "tp"),
        P("tp", None),
        P("tp"),
        P("tp"),
        P("tp", "ctx"),
    )
    places = Places(mesh.shape["ctx"], mesh.shape["tp"])
    return jax.shard_map(
        functools.partial(per_device, places),
        mesh=mesh,
        in_specs=in_specs,
        out_specs=P(AXES, None),
        check_vma=False,
    )
```

```python
import functools

import jax
import jax.numpy as jnp
from jax import lax
from jax.experimental import pallas as pl
from jax.experimental.pallas import tpu as pltpu
from jax.sharding import PartitionSpec as P

AXES = ("ctx", "tp")
BF16, F32 = jnp.bfloat16, jnp.float32
VMEM_LIMIT = 56 << 20


class Places:
    def __init__(self, ctx, tp):
        self.ctx, self.tp = ctx, tp
        self.nx = 1 << ((ctx.bit_length() - 1) // 2)
        self.nz = ctx // self.nx
        self.ny = tp // 2

    def send(self, value, target):
        pairs = []
        for i in range(self.ctx):
            for j in range(self.tp):
                to = target(i, j)
                if to is not None:
                    pairs.append((i * self.tp + j, to[0] * self.tp + to[1]))
        return lax.ppermute(value, AXES, pairs)

    def flip(self, value, ctx=0, tp=0):
        return self.send(value, lambda i, j: (i ^ ctx, j ^ tp))

    def masks(self):
        return [m * self.nx for m in range(1, self.nz)]


def after(value, *done):
    done = [entry for entry in done if entry is not None]
    return lax.optimization_barrier((value, *done))[0] if done else value


class Line:
    def __init__(self, places):
        self.places, self.far = places, []

    def step(self, value, mask, *done):
        result = self.places.flip(
            after(value, self.far[-3] if len(self.far) >= 3 else None, *done), ctx=mask
        )
        self.far.append(result)
        return result

    def gather(self, own, other, *last):
        nx, nz = self.places.nx, self.places.nz
        held = {}
        masks = sorted(range(1, nz), key=lambda m: (m < 2, m))
        for m in masks:
            held[m] = self.step(
                other if m % 2 else own, m * nx, *(last if m == masks[-1] else ())
            )
        return held

    def beside(self, own):
        return [self.places.flip(own, ctx=step) for step in range(1, self.places.nx)]

    def cross(self, held, *done):
        nx, nz = self.places.nx, self.places.nz
        stack = after(jnp.stack([held[m] for m in range(1, nz)]), *done)
        groups = [[z * nx + x for x in range(nx)] for z in range(nz)]
        return lax.all_gather(stack, "ctx", axis_index_groups=groups, tiled=True)


def prepare_kernel(per_part, order, flags, own, *refs):
    parts, out = refs[:-1], refs[-1]
    part = order[pl.program_id(0)] // per_part
    quarter, which = part // 2, part % 2
    rows = own.shape[0]
    out[:, pl.ds(pl.multiple_of(flags[0] * rows, rows), rows)] = own[...].T
    for index, ref in enumerate(parts):

        @pl.when((quarter == flags[1] ^ (index // 2)) & (which == index % 2))
        def _():
            out[:, pl.ds(pl.multiple_of((1 - flags[0]) * rows, rows), rows)] = ref[...].T


def prepare(order, flags, own, parts, depth):
    rows, features = own.shape
    count = features // depth
    per_part = count // len(parts)
    return pl.pallas_call(
        functools.partial(prepare_kernel, per_part),
        out_shape=jax.ShapeDtypeStruct((features, 2 * rows), BF16),
        grid_spec=pltpu.PrefetchScalarGridSpec(
            num_scalar_prefetch=2,
            grid=(count,),
            in_specs=[pl.BlockSpec((rows, depth), lambda i, o, f: (0, o[i]))]
            + [pl.BlockSpec((rows, depth), lambda i, o, f: (0, o[i] % per_part))] * len(parts),
            out_specs=pl.BlockSpec((depth, 2 * rows), lambda i, o, f: (i, 0)),
        ),
        compiler_params=pltpu.CompilerParams(vmem_limit_bytes=VMEM_LIMIT),
        cost_estimate=pl.CostEstimate(
            flops=0, bytes_accessed=8 * rows * features, transcendentals=0
        ),
    )(order, flags, own, *parts)


def project_kernel(tokens, *refs):
    stacks, out = refs[:-1], refs[-1]
    pieces = [stack[index] for stack in stacks for index in range(stack.shape[0])]
    out[...] = jnp.dot(
        jnp.concatenate(pieces, axis=1), tokens[...], preferred_element_type=F32
    ).astype(out.dtype)


def project(tokens, entries):
    features, rows = tokens.shape
    width, depth = entries[0][0].shape[1:]
    tile, part = min(256, width), rows // 2
    cell = lambda block, count: pl.BlockSpec((count, tile, depth), lambda t, i: (block, i, 0))
    return pl.pallas_call(
        project_kernel,
        out_shape=jax.ShapeDtypeStruct((width, rows), BF16),
        grid=(2, width // tile),
        in_specs=[pl.BlockSpec((features, part), lambda t, i: (0, t))]
        + [cell(block, count) for _, block, count in entries],
        out_specs=pl.BlockSpec((tile, part), lambda t, i: (i, t)),
        compiler_params=pltpu.CompilerParams(vmem_limit_bytes=VMEM_LIMIT),
        cost_estimate=pl.CostEstimate(
            flops=2 * width * rows * features,
            bytes_accessed=2 * ((2 * width + rows) * features + width * rows),
            transcendentals=0,
        ),
    )(tokens, *[stack for stack, _, _ in entries])


def featurize(rim, value, coefficients, first, span):
    wide = jnp.concatenate([rim, value], axis=1).astype(F32)
    total = coefficients[:, first : first + 1] * wide
    for offset in range(1, span):
        total = total + coefficients[:, first + offset : first + offset + 1] * pltpu.roll(
            wide, offset, 1
        )
    return total[:, rim.shape[1] :]


def filter_kernel(span, k, v, k_rim, v_rim, before, coefficients, bands, out):
    coef = coefficients[...]
    first = featurize(k_rim[...], k[...], coef, span, span)
    second = featurize(v_rim[...], v[...], coef, 2 * span, span)
    gated = (first * second).astype(BF16)
    wide = jnp.concatenate([before[...], gated], axis=1)
    groups, reach, taps = bands.shape
    size = wide.shape[0] // groups
    blocks = gated.shape[1] // taps
    for group in range(groups):
        rows = slice(group * size, (group + 1) * size)
        windows = jnp.concatenate(
            [wide[rows, block * taps : block * taps + reach] for block in range(blocks)], axis=0
        )
        sums = jnp.dot(windows, bands[group], preferred_element_type=F32)
        gain = coef[rows, 3 * span : 3 * span + 1]
        for block in range(blocks):
            lanes = slice(block * taps, (block + 1) * taps)
            out[rows, lanes] = sums[block * size : (block + 1) * size] + gain * gated[
                rows, lanes
            ].astype(F32)


def long_filter_part(span, k, v, k_rim, v_rim, before, coefficients, bands):
    width, rows = k.shape
    groups, reach, taps = bands.shape
    tile, part = min(128, width), rows // 2
    cell = lambda size: pl.BlockSpec((tile, size), lambda i, t: (i, t))
    return pl.pallas_call(
        functools.partial(filter_kernel, span),
        out_shape=jax.ShapeDtypeStruct((width, rows), F32),
        grid=(width // tile, 2),
        in_specs=[cell(part), cell(part), cell(taps), cell(taps), cell(taps)]
        + [
            pl.BlockSpec((tile, coefficients.shape[1]), lambda i, t: (i, 0)),
            pl.BlockSpec((groups * tile // width, reach, taps), lambda i, t: (i, 0, 0)),
        ],
        out_specs=cell(part),
        compiler_params=pltpu.CompilerParams(vmem_limit_bytes=VMEM_LIMIT),
        cost_estimate=pl.CostEstimate(
            flops=2 * width * rows * (reach + 4 * span),
            bytes_accessed=8 * width * rows + 2 * groups * reach * taps,
            transcendentals=0,
        ),
    )(k, v, k_rim, v_rim, before, coefficients, bands)


def mix_kernel(span, q, q_rim, filtered, coefficients, out):
    features = featurize(q_rim[...], q[...], coefficients[...], 0, span)
    out[...] = (features * filtered[...]).T.astype(BF16)


def mix(span, q, q_rim, filtered, coefficients):
    width, rows = q.shape
    tile, part = min(128, width), rows // 2
    cell = lambda size: pl.BlockSpec((tile, size), lambda i, t: (i, t))
    return pl.pallas_call(
        functools.partial(mix_kernel, span),
        out_shape=jax.ShapeDtypeStruct((rows, width), BF16),
        grid=(width // tile, 2),
        in_specs=[
            cell(part),
            cell(q_rim.shape[1] // 2),
            cell(part),
            pl.BlockSpec((tile, coefficients.shape[1]), lambda i, t: (i, 0)),
        ],
        out_specs=pl.BlockSpec((part, tile), lambda i, t: (t, i)),
        compiler_params=pltpu.CompilerParams(vmem_limit_bytes=VMEM_LIMIT),
        cost_estimate=pl.CostEstimate(
            flops=2 * width * rows * span, bytes_accessed=8 * width * rows, transcendentals=0
        ),
    )(q, q_rim, filtered, coefficients)


def output_kernel(count, chunks, order, *refs):
    mixed, stacks, outs = refs[:count], refs[count:-chunks], refs[-chunks:]
    left = jnp.concatenate([ref[...] for ref in mixed], axis=1)
    pieces = [stack[index] for stack in stacks for index in range(stack.shape[0])]
    width = outs[0].shape[2]
    for place, piece in enumerate(pieces):
        sums = jnp.dot(left, piece, preferred_element_type=F32)
        for c, out in enumerate(outs):
            out[order[place]] = sums[:, c * width : (c + 1) * width].astype(out.dtype)


def output_sums(order, mixed, stacks, chunks):
    rows, part = mixed[0].shape
    depth, share = stacks[0].shape[1:]
    width = share // chunks
    blocks = sum(stack.shape[0] for stack in stacks)
    tile = min(256, rows)
    return pl.pallas_call(
        functools.partial(output_kernel, len(mixed), chunks),
        out_shape=[jax.ShapeDtypeStruct((blocks, rows, width), BF16)] * chunks,
        grid_spec=pltpu.PrefetchScalarGridSpec(
            num_scalar_prefetch=1,
            grid=(rows // tile,),
            in_specs=[pl.BlockSpec((tile, part), lambda i, o: (i, 0))] * len(mixed)
            + [pl.BlockSpec(stack.shape, lambda i, o: (0, 0, 0)) for stack in stacks],
            out_specs=[pl.BlockSpec((blocks, tile, width), lambda i, o: (0, i, 0))] * chunks,
        ),
        compiler_params=pltpu.CompilerParams(vmem_limit_bytes=VMEM_LIMIT),
        cost_estimate=pl.CostEstimate(
            flops=2 * rows * depth * blocks * share,
            bytes_accessed=2 * (rows * depth + depth * blocks * share + rows * blocks * share),
            transcendentals=0,
        ),
    )(order, *mixed, *stacks)


def bands_of(filters):
    taps = filters.shape[1]
    source = jnp.arange(taps)[:, None]
    target = jnp.arange(taps)[None, :]
    distance = (target - source) % taps
    picker = (distance[None] == jnp.arange(taps)[:, None, None]).astype(BF16)
    full = jnp.einsum("gk,kji->gji", filters, picker, preferred_element_type=F32)
    same = target >= source
    before, current = jnp.where(same, 0.0, full), jnp.where(same, full, 0.0)
    return jnp.concatenate([before, current], axis=1).astype(BF16)


def tail_gate(k, v, taps_k, taps_v, reach, end):
    span = taps_k.shape[0]

    def features(value, taps):
        wide = value[:, end - reach - span + 1 : end].astype(F32)
        total = taps[0][:, None] * wide[:, span - 1 :]
        for offset in range(1, span):
            start = span - 1 - offset
            total = total + taps[offset][:, None] * wide[:, start : start + reach]
        return total

    return (features(k, taps_k) * features(v, taps_v)).astype(BF16)


def pick(value, index, axis):
    return lax.dynamic_index_in_dim(value, index, axis, keepdims=False)


def per_device(
    places, tokens, qkv_weight, short_filter, long_filter, decay_rate, skip_gain, out_weight
):
    rows, in_features = tokens.shape
    depth, width = qkv_weight.shape[1:]
    features = out_weight.shape[1]
    groups, taps = long_filter.shape
    span = short_filter.shape[1]
    ny, nx, nz = places.ny, places.nx, places.nz
    i, j = lax.axis_index("ctx"), lax.axis_index("tp")
    x, zl = i % nx, (i // nx) % 2
    y, core = j // 2, j % 2
    half = width // 2
    share = features // 2
    chunks = 2 if share >= 256 else 1
    chunk = share // chunks
    order = [i ^ step for step in range(nx)]
    order += [(i - x + step) ^ m for step in range(nx) for m in places.masks()]
    order = jnp.stack(order).astype(jnp.int32)
    flags = jnp.stack([zl, j]).astype(jnp.int32)
    line = Line(places)

    def halves(s):
        return [
            lax.dynamic_slice_in_dim(qkv_weight[s], part * half, half, 1).T
            for part in (zl, 1 - zl)
        ]

    q_parts, k_parts, v_parts = (halves(s) for s in range(3))
    own = jnp.stack([q_parts[0], k_parts[0], v_parts[0]])
    beside = line.beside(own)

    size = in_features // places.tp
    parts = [
        {
            0: places.flip(
                lax.dynamic_slice_in_dim(tokens, j * size + h * (size // 2), size // 2, 1), ctx=nx
            )
        }
        for h in range(2)
    ]
    k_held = line.gather(*k_parts, parts[0][0], *beside)
    for part in parts:
        for step in range(1, ny):
            part[2 * step] = places.flip(part[0], tp=2 * step)
    k_cross = line.cross(k_held)

    out_halves = out_weight.reshape(width, 2, share)
    rows_of = [pick(out_halves, core, 1), places.flip(pick(out_halves, 1 - core, 1), tp=1)]
    both = jnp.stack(rows_of).reshape(2, 2, half, share)
    out_own, out_other = (pick(both, part, 1).reshape(width, share) for part in (zl, 1 - zl))

    v_held = line.gather(*v_parts, parts[1][0], *parts[0].values())
    for part in parts:
        for mask in list(part):
            part[mask ^ 1] = places.flip(part[mask], tp=1)
    v_cross = line.cross(v_held)
    tokens = prepare(
        order,
        flags,
        tokens,
        [part[mask] for mask in range(places.tp) for part in parts],
        depth,
    )
    q_held = line.gather(*q_parts, tokens)
    q_cross = line.cross(q_held)
    out_beside = line.beside(out_own)

    def entries(s, crossed):
        return [(stack, s, 1) for stack in [own] + beside] + [(crossed, 0, crossed.shape[0])]

    k = project(tokens, entries(1, k_cross))
    out_held = line.gather(out_own, out_other, k, *out_beside)
    u = project(tokens, entries(2, v_cross))
    outs = [stack[None] for stack in [out_own] + out_beside]
    outs.append(line.cross(out_held, u))

    tap_index = jnp.arange(taps, dtype=F32)
    filters = (long_filter * jnp.exp(-decay_rate[:, None] * tap_index[None, :])).astype(BF16)
    bands = bands_of(lax.dynamic_slice_in_dim(filters, zl * (groups // 2), groups // 2))
    short = lax.dynamic_slice_in_dim(short_filter, zl * half, half, 2)
    gain = lax.dynamic_slice_in_dim(skip_gain, zl * half, half)
    coefficients = jnp.concatenate([short.reshape(3 * span, half), gain[None, :]]).T
    coefficients = jnp.pad(coefficients, ((0, 0), (0, (-3 * span - 1) % 8)))

    def halos(tails):
        beside = places.send(tails, lambda i, j: (i - i % nx + (i + 1) % nx, j))
        below = places.send(
            tails[1],
            lambda i, j: (i + 2 * nx - nx + 1, j)
            if i % nx == nx - 1 and i + 2 * nx < places.ctx
            else None,
        )
        start = x == 0
        return [jnp.where(start, below, beside[0]), jnp.where(start, beside[0], beside[1])]

    def rim_of(value):
        return jnp.pad(value.T, ((0, 0), (taps - value.shape[0], 0)))

    def rims(values):
        return jnp.concatenate([rim_of(value) for value in values], axis=1)

    edge = 8 * -(-(span - 1) // 8)
    ends = (rows, 2 * rows)
    tails = [
        jnp.concatenate(
            [
                tail_gate(k, u, short[1], short[2], taps, end).T,
                k[:, end - edge : end].T,
                u[:, end - edge : end].T,
            ]
        )
        for end in ends
    ]
    before = halos(jnp.stack(tails))
    q = project(tokens, entries(0, after(q_cross, *out_held.values())))
    edges = halos(jnp.stack([q[:, end - edge : end].T for end in ends]))
    filtered = long_filter_part(
        span,
        k,
        u,
        rims([value[taps : taps + edge] for value in before]),
        rims([value[taps + edge :] for value in before]),
        rims([value[:taps] for value in before]),
        after(coefficients, q),
        bands,
    )
    mixed = mix(span, q, rims(edges), filtered, coefficients)
    mixed = [mixed, places.flip(mixed, tp=1)]

    def over_y(value):
        total = pick(value, y, 1).astype(F32)
        for step in range(1, ny):
            total = total + places.flip(pick(value, y ^ step, 1), tp=2 * step).astype(F32)
        return total.astype(BF16)

    def over_z(value):
        other = places.flip(pick(value, 1 - zl, 1), ctx=nx)
        return (pick(value, zl, 1).astype(F32) + other.astype(F32)).astype(BF16)

    results = []
    blocks = places.ctx
    part = rows // ny
    for c, sums in enumerate(output_sums(order, mixed, outs, chunks)):
        if c + 1 < chunks or chunks == 1:
            value = sums.reshape(blocks * 2, ny, part, chunk)
            value = over_z(over_y(value).reshape(blocks, 2, part, chunk))
        else:
            value = over_z(sums.reshape(blocks, 2, rows, chunk))
            value = over_y(value.reshape(blocks, ny, part, chunk))
        value = value.reshape(blocks, 2, part // 2, chunk)
        mine = pick(value, core, 1)
        yours = places.flip(pick(value, 1 - core, 1), tp=1)
        pair = jnp.stack(
            [jnp.where(core == 0, mine, yours), jnp.where(core == 0, yours, mine)], axis=1
        )
        results.append(pair)
    result = jnp.stack(results, axis=2)
    return result.transpose(3, 0, 1, 2, 4).reshape(part // 2, -1)


def solution(mesh):
    in_specs = (
        P("ctx", None),
        P(None, "ctx", "tp"),
        P(None, None, "tp"),
        P("tp", None),
        P("tp"),
        P("tp"),
        P("tp", "ctx"),
    )
    places = Places(mesh.shape["ctx"], mesh.shape["tp"])
    return jax.shard_map(
        functools.partial(per_device, places),
        mesh=mesh,
        in_specs=in_specs,
        out_specs=P(AXES, None),
        check_vma=False,
    )
```

```python
import functools

import jax
import jax.numpy as jnp
from jax import lax
from jax.experimental import pallas as pl
from jax.experimental.pallas import tpu as pltpu
from jax.sharding import PartitionSpec as P

AXES = ("ctx", "tp")
BF16, F32 = jnp.bfloat16, jnp.float32
VMEM_LIMIT = 56 << 20


class Places:
    def __init__(self, ctx, tp):
        self.ctx, self.tp = ctx, tp
        self.nx = 1 << ((ctx.bit_length() - 1) // 2)
        self.nz = ctx // self.nx
        self.ny = tp // 2

    def send(self, value, target):
        pairs = []
        for i in range(self.ctx):
            for j in range(self.tp):
                to = target(i, j)
                if to is not None:
                    pairs.append((i * self.tp + j, to[0] * self.tp + to[1]))
        return lax.ppermute(value, AXES, pairs)

    def flip(self, value, ctx=0, tp=0):
        return self.send(value, lambda i, j: (i ^ ctx, j ^ tp))

    def masks(self):
        return [m * self.nx for m in range(1, self.nz)]


def after(value, *done):
    done = [entry for entry in done if entry is not None]
    return lax.optimization_barrier((value, *done))[0] if done else value


class Line:
    def __init__(self, places):
        self.places, self.far = places, []

    def step(self, value, mask, *done):
        result = self.places.flip(
            after(value, self.far[-3] if len(self.far) >= 3 else None, *done), ctx=mask
        )
        self.far.append(result)
        return result

    def gather(self, own, other, *last, first=()):
        nx, nz = self.places.nx, self.places.nz
        held = {}
        masks = sorted(range(1, nz), key=lambda m: (m < 2, m))
        for m in masks:
            held[m] = self.step(
                other if m % 2 else own, m * nx, *(last if m == masks[-1] else first)
            )
        return held

    def beside(self, own):
        return [self.places.flip(own, ctx=step) for step in range(1, self.places.nx)]

    def cross(self, held, *done):
        nx, nz = self.places.nx, self.places.nz
        stack = after(jnp.stack([held[m] for m in range(1, nz)]), *done)
        groups = [[z * nx + x for x in range(nx)] for z in range(nz)]
        return lax.all_gather(stack, "ctx", axis_index_groups=groups, tiled=True)


def prepare_kernel(per_part, order, flags, own, *refs):
    parts, out = refs[:-1], refs[-1]
    part = order[pl.program_id(0)] // per_part
    quarter, which = part // 2, part % 2
    rows = own.shape[0]
    out[:, pl.ds(pl.multiple_of(flags[0] * rows, rows), rows)] = own[...].T
    for index, ref in enumerate(parts):

        @pl.when((quarter == flags[1] ^ (index // 2)) & (which == index % 2))
        def _():
            out[:, pl.ds(pl.multiple_of((1 - flags[0]) * rows, rows), rows)] = ref[...].T


def prepare(order, flags, own, parts, depth):
    rows, features = own.shape
    count = features // depth
    per_part = count // len(parts)
    return pl.pallas_call(
        functools.partial(prepare_kernel, per_part),
        out_shape=jax.ShapeDtypeStruct((features, 2 * rows), BF16),
        grid_spec=pltpu.PrefetchScalarGridSpec(
            num_scalar_prefetch=2,
            grid=(count,),
            in_specs=[pl.BlockSpec((rows, depth), lambda i, o, f: (0, o[i]))]
            + [pl.BlockSpec((rows, depth), lambda i, o, f: (0, o[i] % per_part))] * len(parts),
            out_specs=pl.BlockSpec((depth, 2 * rows), lambda i, o, f: (i, 0)),
        ),
        compiler_params=pltpu.CompilerParams(vmem_limit_bytes=VMEM_LIMIT),
        cost_estimate=pl.CostEstimate(
            flops=0, bytes_accessed=8 * rows * features, transcendentals=0
        ),
    )(order, flags, own, *parts)


def project_kernel(tokens, *refs):
    stacks, out = refs[:-1], refs[-1]
    pieces = [stack[index] for stack in stacks for index in range(stack.shape[0])]
    out[...] = jnp.dot(
        jnp.concatenate(pieces, axis=1), tokens[...], preferred_element_type=F32
    ).astype(out.dtype)


def project(tokens, entries):
    features, rows = tokens.shape
    width, depth = entries[0][0].shape[1:]
    tile, part = min(256, width), rows // 2
    cell = lambda block, count: pl.BlockSpec((count, tile, depth), lambda t, i: (block, i, 0))
    return pl.pallas_call(
        project_kernel,
        out_shape=jax.ShapeDtypeStruct((width, rows), BF16),
        grid=(2, width // tile),
        in_specs=[pl.BlockSpec((features, part), lambda t, i: (0, t))]
        + [cell(block, count) for _, block, count in entries],
        out_specs=pl.BlockSpec((tile, part), lambda t, i: (i, t)),
        compiler_params=pltpu.CompilerParams(vmem_limit_bytes=VMEM_LIMIT),
        cost_estimate=pl.CostEstimate(
            flops=2 * width * rows * features,
            bytes_accessed=2 * ((2 * width + rows) * features + width * rows),
            transcendentals=0,
        ),
    )(tokens, *[stack for stack, _, _ in entries])


def featurize(rim, value, coefficients, first, span):
    wide = jnp.concatenate([rim, value], axis=1).astype(F32)
    total = coefficients[:, first : first + 1] * wide
    for offset in range(1, span):
        total = total + coefficients[:, first + offset : first + offset + 1] * pltpu.roll(
            wide, offset, 1
        )
    return total[:, rim.shape[1] :]


def filter_kernel(span, k, v, k_rim, v_rim, before, coefficients, bands, out):
    coef = coefficients[...]
    first = featurize(k_rim[...], k[...], coef, span, span)
    second = featurize(v_rim[...], v[...], coef, 2 * span, span)
    gated = (first * second).astype(BF16)
    wide = jnp.concatenate([before[...], gated], axis=1)
    groups, reach, taps = bands.shape
    size = wide.shape[0] // groups
    blocks = gated.shape[1] // taps
    for group in range(groups):
        rows = slice(group * size, (group + 1) * size)
        windows = jnp.concatenate(
            [wide[rows, block * taps : block * taps + reach] for block in range(blocks)], axis=0
        )
        sums = jnp.dot(windows, bands[group], preferred_element_type=F32)
        gain = coef[rows, 3 * span : 3 * span + 1]
        for block in range(blocks):
            lanes = slice(block * taps, (block + 1) * taps)
            out[rows, lanes] = sums[block * size : (block + 1) * size] + gain * gated[
                rows, lanes
            ].astype(F32)


def long_filter_part(span, k, v, k_rim, v_rim, before, coefficients, bands):
    width, rows = k.shape
    groups, reach, taps = bands.shape
    tile, part = min(128, width), rows // 2
    cell = lambda size: pl.BlockSpec((tile, size), lambda i, t: (i, t))
    return pl.pallas_call(
        functools.partial(filter_kernel, span),
        out_shape=jax.ShapeDtypeStruct((width, rows), F32),
        grid=(width // tile, 2),
        in_specs=[cell(part), cell(part), cell(taps), cell(taps), cell(taps)]
        + [
            pl.BlockSpec((tile, coefficients.shape[1]), lambda i, t: (i, 0)),
            pl.BlockSpec((groups * tile // width, reach, taps), lambda i, t: (i, 0, 0)),
        ],
        out_specs=cell(part),
        compiler_params=pltpu.CompilerParams(vmem_limit_bytes=VMEM_LIMIT),
        cost_estimate=pl.CostEstimate(
            flops=2 * width * rows * (reach + 4 * span),
            bytes_accessed=8 * width * rows + 2 * groups * reach * taps,
            transcendentals=0,
        ),
    )(k, v, k_rim, v_rim, before, coefficients, bands)


def mix_kernel(span, q, q_rim, filtered, coefficients, out):
    features = featurize(q_rim[...], q[...], coefficients[...], 0, span)
    out[...] = (features * filtered[...]).T.astype(BF16)


def mix(span, q, q_rim, filtered, coefficients):
    width, rows = q.shape
    tile, part = min(128, width), rows // 2
    cell = lambda size: pl.BlockSpec((tile, size), lambda i, t: (i, t))
    return pl.pallas_call(
        functools.partial(mix_kernel, span),
        out_shape=jax.ShapeDtypeStruct((rows, width), BF16),
        grid=(width // tile, 2),
        in_specs=[
            cell(part),
            cell(q_rim.shape[1] // 2),
            cell(part),
            pl.BlockSpec((tile, coefficients.shape[1]), lambda i, t: (i, 0)),
        ],
        out_specs=pl.BlockSpec((part, tile), lambda i, t: (t, i)),
        compiler_params=pltpu.CompilerParams(vmem_limit_bytes=VMEM_LIMIT),
        cost_estimate=pl.CostEstimate(
            flops=2 * width * rows * span, bytes_accessed=8 * width * rows, transcendentals=0
        ),
    )(q, q_rim, filtered, coefficients)


def output_kernel(count, chunks, order, *refs):
    mixed, stacks, outs = refs[:count], refs[count:-chunks], refs[-chunks:]
    left = jnp.concatenate([ref[...] for ref in mixed], axis=1)
    pieces = [stack[index] for stack in stacks for index in range(stack.shape[0])]
    width = outs[0].shape[2]
    for place, piece in enumerate(pieces):
        sums = jnp.dot(left, piece, preferred_element_type=F32)
        for c, out in enumerate(outs):
            out[order[place]] = sums[:, c * width : (c + 1) * width].astype(out.dtype)


def output_sums(order, mixed, stacks, chunks):
    rows, part = mixed[0].shape
    depth, share = stacks[0].shape[1:]
    width = share // chunks
    blocks = sum(stack.shape[0] for stack in stacks)
    tile = min(256, rows)
    return pl.pallas_call(
        functools.partial(output_kernel, len(mixed), chunks),
        out_shape=[jax.ShapeDtypeStruct((blocks, rows, width), BF16)] * chunks,
        grid_spec=pltpu.PrefetchScalarGridSpec(
            num_scalar_prefetch=1,
            grid=(rows // tile,),
            in_specs=[pl.BlockSpec((tile, part), lambda i, o: (i, 0))] * len(mixed)
            + [pl.BlockSpec(stack.shape, lambda i, o: (0, 0, 0)) for stack in stacks],
            out_specs=[pl.BlockSpec((blocks, tile, width), lambda i, o: (0, i, 0))] * chunks,
        ),
        compiler_params=pltpu.CompilerParams(vmem_limit_bytes=VMEM_LIMIT),
        cost_estimate=pl.CostEstimate(
            flops=2 * rows * depth * blocks * share,
            bytes_accessed=2 * (rows * depth + depth * blocks * share + rows * blocks * share),
            transcendentals=0,
        ),
    )(order, *mixed, *stacks)


def bands_of(filters):
    taps = filters.shape[1]
    source = jnp.arange(taps)[:, None]
    target = jnp.arange(taps)[None, :]
    distance = (target - source) % taps
    picker = (distance[None] == jnp.arange(taps)[:, None, None]).astype(BF16)
    full = jnp.einsum("gk,kji->gji", filters, picker, preferred_element_type=F32)
    same = target >= source
    before, current = jnp.where(same, 0.0, full), jnp.where(same, full, 0.0)
    return jnp.concatenate([before, current], axis=1).astype(BF16)


def tail_gate(k, v, taps_k, taps_v, reach, end):
    span = taps_k.shape[0]

    def features(value, taps):
        wide = value[:, end - reach - span + 1 : end].astype(F32)
        total = taps[0][:, None] * wide[:, span - 1 :]
        for offset in range(1, span):
            start = span - 1 - offset
            total = total + taps[offset][:, None] * wide[:, start : start + reach]
        return total

    return (features(k, taps_k) * features(v, taps_v)).astype(BF16)


def pick(value, index, axis):
    return lax.dynamic_index_in_dim(value, index, axis, keepdims=False)


def per_device(
    places, tokens, qkv_weight, short_filter, long_filter, decay_rate, skip_gain, out_weight
):
    rows, in_features = tokens.shape
    depth, width = qkv_weight.shape[1:]
    features = out_weight.shape[1]
    groups, taps = long_filter.shape
    span = short_filter.shape[1]
    ny, nx, nz = places.ny, places.nx, places.nz
    i, j = lax.axis_index("ctx"), lax.axis_index("tp")
    x, zl = i % nx, (i // nx) % 2
    y, core = j // 2, j % 2
    half = width // 2
    share = features // 2
    chunks = 2 if share >= 256 else 1
    chunk = share // chunks
    order = [i ^ step for step in range(nx)]
    order += [(i - x + step) ^ m for step in range(nx) for m in places.masks()]
    order = jnp.stack(order).astype(jnp.int32)
    flags = jnp.stack([zl, j]).astype(jnp.int32)
    line = Line(places)

    def halves(s):
        return [
            lax.dynamic_slice_in_dim(qkv_weight[s], part * half, half, 1).T
            for part in (zl, 1 - zl)
        ]

    q_parts, k_parts, v_parts = (halves(s) for s in range(3))
    own = jnp.stack([q_parts[0], k_parts[0], v_parts[0]])
    beside = line.beside(own)

    size = in_features // places.tp
    parts = [
        {
            0: places.flip(
                lax.dynamic_slice_in_dim(tokens, j * size + h * (size // 2), size // 2, 1), ctx=nx
            )
        }
        for h in range(2)
    ]
    out_halves = out_weight.reshape(width, 2, share)
    rows_of = [pick(out_halves, core, 1), places.flip(pick(out_halves, 1 - core, 1), tp=1)]
    both = jnp.stack(rows_of).reshape(2, 2, half, share)
    out_own, out_other = (pick(both, part, 1).reshape(width, share) for part in (zl, 1 - zl))
    k_held = line.gather(*k_parts, parts[0][0], *beside, rows_of[1])
    for part in parts:
        for step in range(1, ny):
            part[2 * step] = places.flip(part[0], tp=2 * step)
    k_cross = line.cross(k_held)

    v_held = line.gather(*v_parts, parts[1][0], *parts[0].values())
    for part in parts:
        for mask in list(part):
            part[mask ^ 1] = places.flip(part[mask], tp=1)
    v_cross = line.cross(v_held)
    tokens = prepare(
        order,
        flags,
        tokens,
        [part[mask] for mask in range(places.tp) for part in parts],
        depth,
    )
    near, far = ([part[mask] for mask in part if mask % 2] for part in parts)
    q_held = line.gather(*q_parts, *far, first=near)
    q_cross = line.cross(q_held, tokens)
    out_beside = line.beside(out_own)

    def entries(s, crossed):
        return [(stack, s, 1) for stack in [own] + beside] + [(crossed, 0, crossed.shape[0])]

    k = project(tokens, entries(1, k_cross))
    out_held = line.gather(out_own, out_other, k, *out_beside)
    u = project(tokens, entries(2, v_cross))
    outs = [stack[None] for stack in [out_own] + out_beside]
    outs.append(line.cross(out_held, u))

    tap_index = jnp.arange(taps, dtype=F32)
    filters = (long_filter * jnp.exp(-decay_rate[:, None] * tap_index[None, :])).astype(BF16)
    bands = bands_of(lax.dynamic_slice_in_dim(filters, zl * (groups // 2), groups // 2))
    short = lax.dynamic_slice_in_dim(short_filter, zl * half, half, 2)
    gain = lax.dynamic_slice_in_dim(skip_gain, zl * half, half)
    coefficients = jnp.concatenate([short.reshape(3 * span, half), gain[None, :]]).T
    coefficients = jnp.pad(coefficients, ((0, 0), (0, (-3 * span - 1) % 8)))

    def halos(tails, *done):
        beside = places.send(tails, lambda i, j: (i - i % nx + (i + 1) % nx, j))
        below = places.send(
            tails[1],
            lambda i, j: (i + 2 * nx - nx + 1, j)
            if i % nx == nx - 1 and i + 2 * nx < places.ctx
            else None,
        )
        beside, below = after(beside, *done), after(below, *done)
        start = x == 0
        return [jnp.where(start, below, beside[0]), jnp.where(start, beside[0], beside[1])]

    def rim_of(value):
        return jnp.pad(value.T, ((0, 0), (taps - value.shape[0], 0)))

    def rims(values):
        return jnp.concatenate([rim_of(value) for value in values], axis=1)

    edge = 8 * -(-(span - 1) // 8)
    ends = (rows, 2 * rows)
    tails = [
        jnp.concatenate(
            [
                tail_gate(k, u, short[1], short[2], taps, end).T,
                k[:, end - edge : end].T,
                u[:, end - edge : end].T,
            ]
        )
        for end in ends
    ]
    q = project(tokens, entries(0, after(q_cross, *out_held.values())))
    before = halos(jnp.stack(tails), q)
    edges = halos(jnp.stack([q[:, end - edge : end].T for end in ends]))
    filtered = long_filter_part(
        span,
        k,
        u,
        rims([value[taps : taps + edge] for value in before]),
        rims([value[taps + edge :] for value in before]),
        rims([value[:taps] for value in before]),
        after(coefficients, q),
        bands,
    )
    mixed = mix(span, q, rims(edges), filtered, coefficients)
    mixed = [mixed, places.flip(mixed, tp=1)]

    def over_y(value):
        total = pick(value, y, 1).astype(F32)
        for step in range(1, ny):
            total = total + places.flip(pick(value, y ^ step, 1), tp=2 * step).astype(F32)
        return total.astype(BF16)

    def over_z(value):
        other = places.flip(pick(value, 1 - zl, 1), ctx=nx)
        return (pick(value, zl, 1).astype(F32) + other.astype(F32)).astype(BF16)

    results = []
    blocks = places.ctx
    part = rows // ny
    for c, sums in enumerate(output_sums(order, mixed, outs, chunks)):
        if c + 1 < chunks or chunks == 1:
            value = sums.reshape(blocks * 2, ny, part, chunk)
            value = over_z(over_y(value).reshape(blocks, 2, part, chunk))
        else:
            value = over_z(sums.reshape(blocks, 2, rows, chunk))
            value = over_y(value.reshape(blocks, ny, part, chunk))
        value = value.reshape(blocks, 2, part // 2, chunk)
        mine = pick(value, core, 1)
        yours = places.flip(pick(value, 1 - core, 1), tp=1)
        pair = jnp.stack(
            [jnp.where(core == 0, mine, yours), jnp.where(core == 0, yours, mine)], axis=1
        )
        results.append(pair)
    result = jnp.stack(results, axis=2)
    return result.transpose(3, 0, 1, 2, 4).reshape(part // 2, -1)


def solution(mesh):
    in_specs = (
        P("ctx", None),
        P(None, "ctx", "tp"),
        P(None, None, "tp"),
        P("tp", None),
        P("tp"),
        P("tp"),
        P("tp", "ctx"),
    )
    places = Places(mesh.shape["ctx"], mesh.shape["tp"])
    return jax.shard_map(
        functools.partial(per_device, places),
        mesh=mesh,
        in_specs=in_specs,
        out_specs=P(AXES, None),
        check_vma=False,
    )
```

```python
import functools

import jax
import jax.numpy as jnp
from jax import lax
from jax.experimental import pallas as pl
from jax.experimental.pallas import tpu as pltpu
from jax.sharding import PartitionSpec as P

AXES = ("ctx", "tp")
BF16, F32 = jnp.bfloat16, jnp.float32
VMEM_LIMIT = 56 << 20


class Places:
    def __init__(self, ctx, tp):
        self.ctx, self.tp = ctx, tp
        self.nx = 1 << ((ctx.bit_length() - 1) // 2)
        self.nz = ctx // self.nx
        self.ny = tp // 2

    def send(self, value, target):
        pairs = []
        for i in range(self.ctx):
            for j in range(self.tp):
                to = target(i, j)
                if to is not None:
                    pairs.append((i * self.tp + j, to[0] * self.tp + to[1]))
        return lax.ppermute(value, AXES, pairs)

    def flip(self, value, ctx=0, tp=0):
        return self.send(value, lambda i, j: (i ^ ctx, j ^ tp))

    def masks(self):
        return [m * self.nx for m in range(1, self.nz)]


def after(value, *done):
    done = [entry for entry in done if entry is not None]
    return lax.optimization_barrier((value, *done))[0] if done else value


class Line:
    def __init__(self, places):
        self.places, self.far = places, []

    def step(self, value, mask, *done):
        result = self.places.flip(
            after(value, self.far[-3] if len(self.far) >= 3 else None, *done), ctx=mask
        )
        self.far.append(result)
        return result

    def gather(self, own, other, *last, first=()):
        nx, nz = self.places.nx, self.places.nz
        held = {}
        masks = sorted(range(1, nz), key=lambda m: (m < 2, m))
        for m in masks:
            held[m] = self.step(
                other if m % 2 else own, m * nx, *(last if m == masks[-1] else first)
            )
        return held

    def beside(self, own):
        return [self.places.flip(own, ctx=step) for step in range(1, self.places.nx)]

    def stack(self, held):
        return jnp.stack([held[m] for m in range(1, self.places.nz)])

    def cross(self, stack):
        nx, nz = self.places.nx, self.places.nz
        groups = [[z * nx + x for x in range(nx)] for z in range(nz)]
        return lax.all_gather(stack, "ctx", axis_index_groups=groups, tiled=True)


def prepare_kernel(per_part, order, flags, own, *refs):
    parts, out = refs[:-1], refs[-1]
    part = order[pl.program_id(0)] // per_part
    rows = own.shape[0]
    out[:, pl.ds(pl.multiple_of(flags[0] * rows, rows), rows)] = own[...].T
    for mask, ref in enumerate(parts):

        @pl.when(part == flags[1] ^ mask)
        def _():
            out[:, pl.ds(pl.multiple_of((1 - flags[0]) * rows, rows), rows)] = ref[...].T


def prepare(order, flags, own, parts, depth):
    rows, features = own.shape
    count = features // depth
    per_part = count // len(parts)
    return pl.pallas_call(
        functools.partial(prepare_kernel, per_part),
        out_shape=jax.ShapeDtypeStruct((features, 2 * rows), BF16),
        grid_spec=pltpu.PrefetchScalarGridSpec(
            num_scalar_prefetch=2,
            grid=(count,),
            in_specs=[pl.BlockSpec((rows, depth), lambda i, o, f: (0, o[i]))]
            + [pl.BlockSpec((rows, depth), lambda i, o, f: (0, o[i] % per_part))] * len(parts),
            out_specs=pl.BlockSpec((depth, 2 * rows), lambda i, o, f: (i, 0)),
        ),
        compiler_params=pltpu.CompilerParams(vmem_limit_bytes=VMEM_LIMIT),
        cost_estimate=pl.CostEstimate(
            flops=0, bytes_accessed=8 * rows * features, transcendentals=0
        ),
    )(order, flags, own, *parts)


def project_kernel(tokens, *refs):
    stacks, out = refs[:-1], refs[-1]
    pieces = [stack[index] for stack in stacks for index in range(stack.shape[0])]
    out[...] = jnp.dot(
        jnp.concatenate(pieces, axis=1), tokens[...], preferred_element_type=F32
    ).astype(out.dtype)


def project(tokens, entries):
    features, rows = tokens.shape
    width, depth = entries[0][0].shape[1:]
    tile, part = min(256, width), rows // 2
    cell = lambda block, count: pl.BlockSpec((count, tile, depth), lambda t, i: (block, i, 0))
    return pl.pallas_call(
        project_kernel,
        out_shape=jax.ShapeDtypeStruct((width, rows), BF16),
        grid=(2, width // tile),
        in_specs=[pl.BlockSpec((features, part), lambda t, i: (0, t))]
        + [cell(block, count) for _, block, count in entries],
        out_specs=pl.BlockSpec((tile, part), lambda t, i: (i, t)),
        compiler_params=pltpu.CompilerParams(vmem_limit_bytes=VMEM_LIMIT),
        cost_estimate=pl.CostEstimate(
            flops=2 * width * rows * features,
            bytes_accessed=2 * ((2 * width + rows) * features + width * rows),
            transcendentals=0,
        ),
    )(tokens, *[stack for stack, _, _ in entries])


def featurize(rim, value, coefficients, first, span):
    wide = jnp.concatenate([rim, value], axis=1).astype(F32)
    total = coefficients[:, first : first + 1] * wide
    for offset in range(1, span):
        total = total + coefficients[:, first + offset : first + offset + 1] * pltpu.roll(
            wide, offset, 1
        )
    return total[:, rim.shape[1] :]


def filter_kernel(span, k, v, k_rim, v_rim, before, coefficients, bands, out):
    coef = coefficients[...]
    first = featurize(k_rim[...], k[...], coef, span, span)
    second = featurize(v_rim[...], v[...], coef, 2 * span, span)
    gated = (first * second).astype(BF16)
    wide = jnp.concatenate([before[...], gated], axis=1)
    groups, reach, taps = bands.shape
    size = wide.shape[0] // groups
    blocks = gated.shape[1] // taps
    for group in range(groups):
        rows = slice(group * size, (group + 1) * size)
        windows = jnp.concatenate(
            [wide[rows, block * taps : block * taps + reach] for block in range(blocks)], axis=0
        )
        sums = jnp.dot(windows, bands[group], preferred_element_type=F32)
        gain = coef[rows, 3 * span : 3 * span + 1]
        for block in range(blocks):
            lanes = slice(block * taps, (block + 1) * taps)
            out[rows, lanes] = sums[block * size : (block + 1) * size] + gain * gated[
                rows, lanes
            ].astype(F32)


def long_filter_part(span, k, v, k_rim, v_rim, before, coefficients, bands):
    width, rows = k.shape
    groups, reach, taps = bands.shape
    tile, part = min(128, width), rows // 2
    cell = lambda size: pl.BlockSpec((tile, size), lambda i, t: (i, t))
    return pl.pallas_call(
        functools.partial(filter_kernel, span),
        out_shape=jax.ShapeDtypeStruct((width, rows), F32),
        grid=(width // tile, 2),
        in_specs=[cell(part), cell(part), cell(taps), cell(taps), cell(taps)]
        + [
            pl.BlockSpec((tile, coefficients.shape[1]), lambda i, t: (i, 0)),
            pl.BlockSpec((groups * tile // width, reach, taps), lambda i, t: (i, 0, 0)),
        ],
        out_specs=cell(part),
        compiler_params=pltpu.CompilerParams(vmem_limit_bytes=VMEM_LIMIT),
        cost_estimate=pl.CostEstimate(
            flops=2 * width * rows * (reach + 4 * span),
            bytes_accessed=8 * width * rows + 2 * groups * reach * taps,
            transcendentals=0,
        ),
    )(k, v, k_rim, v_rim, before, coefficients, bands)


def mix_kernel(span, q, q_rim, filtered, coefficients, out):
    features = featurize(q_rim[...], q[...], coefficients[...], 0, span)
    out[...] = (features * filtered[...]).T.astype(BF16)


def mix(span, q, q_rim, filtered, coefficients):
    width, rows = q.shape
    tile, part = min(128, width), rows // 2
    cell = lambda size: pl.BlockSpec((tile, size), lambda i, t: (i, t))
    return pl.pallas_call(
        functools.partial(mix_kernel, span),
        out_shape=jax.ShapeDtypeStruct((rows, width), BF16),
        grid=(width // tile, 2),
        in_specs=[
            cell(part),
            cell(q_rim.shape[1] // 2),
            cell(part),
            pl.BlockSpec((tile, coefficients.shape[1]), lambda i, t: (i, 0)),
        ],
        out_specs=pl.BlockSpec((part, tile), lambda i, t: (t, i)),
        compiler_params=pltpu.CompilerParams(vmem_limit_bytes=VMEM_LIMIT),
        cost_estimate=pl.CostEstimate(
            flops=2 * width * rows * span, bytes_accessed=8 * width * rows, transcendentals=0
        ),
    )(q, q_rim, filtered, coefficients)


def output_kernel(count, chunks, order, *refs):
    mixed, stacks, outs = refs[:count], refs[count:-chunks], refs[-chunks:]
    left = jnp.concatenate([ref[...] for ref in mixed], axis=1)
    pieces = [stack[index] for stack in stacks for index in range(stack.shape[0])]
    width = outs[0].shape[2]
    for place, piece in enumerate(pieces):
        sums = jnp.dot(left, piece, preferred_element_type=F32)
        for c, out in enumerate(outs):
            out[order[place]] = sums[:, c * width : (c + 1) * width].astype(out.dtype)


def output_sums(order, mixed, stacks, chunks):
    rows, part = mixed[0].shape
    depth, share = stacks[0].shape[1:]
    width = share // chunks
    blocks = sum(stack.shape[0] for stack in stacks)
    tile = min(256, rows)
    return pl.pallas_call(
        functools.partial(output_kernel, len(mixed), chunks),
        out_shape=[jax.ShapeDtypeStruct((blocks, rows, width), BF16)] * chunks,
        grid_spec=pltpu.PrefetchScalarGridSpec(
            num_scalar_prefetch=1,
            grid=(rows // tile,),
            in_specs=[pl.BlockSpec((tile, part), lambda i, o: (i, 0))] * len(mixed)
            + [pl.BlockSpec(stack.shape, lambda i, o: (0, 0, 0)) for stack in stacks],
            out_specs=[pl.BlockSpec((blocks, tile, width), lambda i, o: (0, i, 0))] * chunks,
        ),
        compiler_params=pltpu.CompilerParams(vmem_limit_bytes=VMEM_LIMIT),
        cost_estimate=pl.CostEstimate(
            flops=2 * rows * depth * blocks * share,
            bytes_accessed=2 * (rows * depth + depth * blocks * share + rows * blocks * share),
            transcendentals=0,
        ),
    )(order, *mixed, *stacks)


def bands_of(filters):
    taps = filters.shape[1]
    source = jnp.arange(taps)[:, None]
    target = jnp.arange(taps)[None, :]
    distance = (target - source) % taps
    picker = (distance[None] == jnp.arange(taps)[:, None, None]).astype(BF16)
    full = jnp.einsum("gk,kji->gji", filters, picker, preferred_element_type=F32)
    same = target >= source
    before, current = jnp.where(same, 0.0, full), jnp.where(same, full, 0.0)
    return jnp.concatenate([before, current], axis=1).astype(BF16)


def tail_gate(k, v, taps_k, taps_v, reach, end):
    span = taps_k.shape[0]

    def features(value, taps):
        wide = value[:, end - reach - span + 1 : end].astype(F32)
        total = taps[0][:, None] * wide[:, span - 1 :]
        for offset in range(1, span):
            start = span - 1 - offset
            total = total + taps[offset][:, None] * wide[:, start : start + reach]
        return total

    return (features(k, taps_k) * features(v, taps_v)).astype(BF16)


def pick(value, index, axis):
    return lax.dynamic_index_in_dim(value, index, axis, keepdims=False)


def per_device(
    places, tokens, qkv_weight, short_filter, long_filter, decay_rate, skip_gain, out_weight
):
    rows, in_features = tokens.shape
    depth, width = qkv_weight.shape[1:]
    features = out_weight.shape[1]
    groups, taps = long_filter.shape
    span = short_filter.shape[1]
    ny, nx, nz = places.ny, places.nx, places.nz
    i, j = lax.axis_index("ctx"), lax.axis_index("tp")
    x, zl = i % nx, (i // nx) % 2
    y, core = j // 2, j % 2
    half = width // 2
    share = features // 2
    chunks = 2 if share >= 256 else 1
    chunk = share // chunks
    order = [i ^ step for step in range(nx)]
    order += [(i - x + step) ^ m for step in range(nx) for m in places.masks()]
    order = jnp.stack(order).astype(jnp.int32)
    flags = jnp.stack([zl, j]).astype(jnp.int32)
    line = Line(places)

    def halves(s):
        return [
            lax.dynamic_slice_in_dim(qkv_weight[s], part * half, half, 1).T
            for part in (zl, 1 - zl)
        ]

    q_parts, k_parts, v_parts = (halves(s) for s in range(3))
    own = jnp.stack([q_parts[0], k_parts[0], v_parts[0]])
    beside = line.beside(own)

    size = in_features // places.tp
    parts = {0: places.flip(lax.dynamic_slice_in_dim(tokens, j * size, size, 1), ctx=nx)}

    out_halves = out_weight.reshape(width, 2, share)
    rows_of = [pick(out_halves, core, 1), places.flip(pick(out_halves, 1 - core, 1), tp=1)]
    both = jnp.stack(rows_of).reshape(2, 2, half, share)
    out_own, out_other = (pick(both, part, 1).reshape(width, share) for part in (zl, 1 - zl))
    k_held = line.gather(*k_parts, parts[0], rows_of[1])
    k_cross = line.cross(line.stack(k_held))
    mine = after(parts[0], *k_held.values(), *beside)
    for step in range(1, ny):
        parts[2 * step] = places.flip(mine, tp=2 * step)
    for mask in list(parts):
        parts[mask ^ 1] = places.flip(parts[mask] if mask else mine, tp=1)
    v_held = line.gather(*v_parts, *parts.values())
    v_cross = line.cross(line.stack(v_held))
    tokens = prepare(
        order, flags, tokens, [parts[mask] for mask in range(places.tp)], depth
    )
    q_held = line.gather(*q_parts, tokens)
    q_cross = line.cross(line.stack(q_held))
    out_beside = line.beside(out_own)

    def entries(s, crossed):
        return [(stack, s, 1) for stack in [own] + beside] + [(crossed, 0, crossed.shape[0])]

    k = project(tokens, entries(1, k_cross))
    u = project(tokens, entries(2, v_cross))
    out_held = line.gather(out_own, out_other, k, u, *out_beside)
    outs = [stack[None] for stack in [out_own] + out_beside]
    out_stack = line.stack(out_held)
    outs.append(line.cross(out_stack))

    tap_index = jnp.arange(taps, dtype=F32)
    filters = (long_filter * jnp.exp(-decay_rate[:, None] * tap_index[None, :])).astype(BF16)
    bands = bands_of(lax.dynamic_slice_in_dim(filters, zl * (groups // 2), groups // 2))
    short = lax.dynamic_slice_in_dim(short_filter, zl * half, half, 2)
    gain = lax.dynamic_slice_in_dim(skip_gain, zl * half, half)
    coefficients = jnp.concatenate([short.reshape(3 * span, half), gain[None, :]]).T
    coefficients = jnp.pad(coefficients, ((0, 0), (0, (-3 * span - 1) % 8)))

    def halos(tails, *done):
        beside = places.send(tails, lambda i, j: (i - i % nx + (i + 1) % nx, j))
        below = places.send(
            tails[1],
            lambda i, j: (i + 2 * nx - nx + 1, j)
            if i % nx == nx - 1 and i + 2 * nx < places.ctx
            else None,
        )
        beside, below = after(beside, *done), after(below, *done)
        start = x == 0
        return [jnp.where(start, below, beside[0]), jnp.where(start, beside[0], beside[1])]

    def rim_of(value):
        return jnp.pad(value.T, ((0, 0), (taps - value.shape[0], 0)))

    def rims(values):
        return jnp.concatenate([rim_of(value) for value in values], axis=1)

    edge = 8 * -(-(span - 1) // 8)
    ends = (rows, 2 * rows)
    tails = [
        jnp.concatenate(
            [
                tail_gate(k, u, short[1], short[2], taps, end).T,
                k[:, end - edge : end].T,
                u[:, end - edge : end].T,
            ]
        )
        for end in ends
    ]
    q = project(tokens, entries(0, after(q_cross, out_stack)))
    before = halos(jnp.stack(tails), q)
    edges = halos(jnp.stack([q[:, end - edge : end].T for end in ends]))
    filtered = long_filter_part(
        span,
        k,
        u,
        rims([value[taps : taps + edge] for value in before]),
        rims([value[taps + edge :] for value in before]),
        rims([value[:taps] for value in before]),
        after(coefficients, q),
        bands,
    )
    mixed = mix(span, q, rims(edges), filtered, coefficients)
    mixed = [mixed, places.flip(mixed, tp=1)]

    def over_y(value):
        total = pick(value, y, 1).astype(F32)
        for step in range(1, ny):
            total = total + places.flip(pick(value, y ^ step, 1), tp=2 * step).astype(F32)
        return total.astype(BF16)

    def over_z(value):
        other = places.flip(pick(value, 1 - zl, 1), ctx=nx)
        return (pick(value, zl, 1).astype(F32) + other.astype(F32)).astype(BF16)

    results = []
    blocks = places.ctx
    part = rows // ny
    for c, sums in enumerate(output_sums(order, mixed, outs, chunks)):
        if c + 1 < chunks or chunks == 1:
            value = sums.reshape(blocks * 2, ny, part, chunk)
            value = over_z(over_y(value).reshape(blocks, 2, part, chunk))
        else:
            value = over_z(sums.reshape(blocks, 2, rows, chunk))
            value = over_y(value.reshape(blocks, ny, part, chunk))
        value = value.reshape(blocks, 2, part // 2, chunk)
        mine = pick(value, core, 1)
        yours = places.flip(pick(value, 1 - core, 1), tp=1)
        pair = jnp.stack(
            [jnp.where(core == 0, mine, yours), jnp.where(core == 0, yours, mine)], axis=1
        )
        results.append(pair)
    result = jnp.stack(results, axis=2)
    return result.transpose(3, 0, 1, 2, 4).reshape(part // 2, -1)


def solution(mesh):
    in_specs = (
        P("ctx", None),
        P(None, "ctx", "tp"),
        P(None, None, "tp"),
        P("tp", None),
        P("tp"),
        P("tp"),
        P("tp", "ctx"),
    )
    places = Places(mesh.shape["ctx"], mesh.shape["tp"])
    return jax.shard_map(
        functools.partial(per_device, places),
        mesh=mesh,
        in_specs=in_specs,
        out_specs=P(AXES, None),
        check_vma=False,
    )
```

```python
import functools

import jax
import jax.numpy as jnp
from jax import lax
from jax.experimental import pallas as pl
from jax.experimental.pallas import tpu as pltpu
from jax.sharding import PartitionSpec as P

AXES = ("ctx", "tp")
BF16, F32 = jnp.bfloat16, jnp.float32
VMEM_LIMIT = 56 << 20


class Places:
    def __init__(self, ctx, tp):
        self.ctx, self.tp = ctx, tp
        self.nx = 1 << ((ctx.bit_length() - 1) // 2)
        self.nz = ctx // self.nx
        self.ny = tp // 2

    def send(self, value, target):
        pairs = []
        for i in range(self.ctx):
            for j in range(self.tp):
                to = target(i, j)
                if to is not None:
                    pairs.append((i * self.tp + j, to[0] * self.tp + to[1]))
        return lax.ppermute(value, AXES, pairs)

    def flip(self, value, ctx=0, tp=0):
        return self.send(value, lambda i, j: (i ^ ctx, j ^ tp))

    def masks(self):
        return [m * self.nx for m in range(1, self.nz)]


def after(value, *done):
    done = [entry for entry in done if entry is not None]
    return lax.optimization_barrier((value, *done))[0] if done else value


class Line:
    def __init__(self, places):
        self.places, self.far = places, []

    def step(self, value, mask, *done):
        result = self.places.flip(
            after(value, self.far[-3] if len(self.far) >= 3 else None, *done), ctx=mask
        )
        self.far.append(result)
        return result

    def gather(self, own, other, *last):
        return self.finish(self.begin(own, other), own, other, *last)

    def begin(self, own, other):
        masks = sorted(range(2, self.places.nz))
        return {m: self.step(other if m % 2 else own, m * self.places.nx) for m in masks}

    def finish(self, held, own, other, *last):
        return {**held, 1: self.step(other, self.places.nx, *last)}

    def beside(self, own):
        return [self.places.flip(own, ctx=step) for step in range(1, self.places.nx)]

    def cross(self, held, *done):
        nx, nz = self.places.nx, self.places.nz
        stack = after(jnp.stack([held[m] for m in range(1, nz)]), *done)
        groups = [[z * nx + x for x in range(nx)] for z in range(nz)]
        return lax.all_gather(stack, "ctx", axis_index_groups=groups, tiled=True)


def prepare_kernel(per_part, order, flags, own, *refs):
    parts, out = refs[:-1], refs[-1]
    part = order[pl.program_id(0)] // per_part
    quarter, which = part // 2, part % 2
    rows = own.shape[0]
    out[:, pl.ds(pl.multiple_of(flags[0] * rows, rows), rows)] = own[...].T
    for index, ref in enumerate(parts):

        @pl.when((quarter == flags[1] ^ (index // 2)) & (which == index % 2))
        def _():
            out[:, pl.ds(pl.multiple_of((1 - flags[0]) * rows, rows), rows)] = ref[...].T


def prepare(order, flags, own, parts, depth):
    rows, features = own.shape
    count = features // depth
    per_part = count // len(parts)
    return pl.pallas_call(
        functools.partial(prepare_kernel, per_part),
        out_shape=jax.ShapeDtypeStruct((features, 2 * rows), BF16),
        grid_spec=pltpu.PrefetchScalarGridSpec(
            num_scalar_prefetch=2,
            grid=(count,),
            in_specs=[pl.BlockSpec((rows, depth), lambda i, o, f: (0, o[i]))]
            + [pl.BlockSpec((rows, depth), lambda i, o, f: (0, o[i] % per_part))] * len(parts),
            out_specs=pl.BlockSpec((depth, 2 * rows), lambda i, o, f: (i, 0)),
        ),
        compiler_params=pltpu.CompilerParams(vmem_limit_bytes=VMEM_LIMIT),
        cost_estimate=pl.CostEstimate(
            flops=0, bytes_accessed=8 * rows * features, transcendentals=0
        ),
    )(order, flags, own, *parts)


def project_kernel(tokens, *refs):
    stacks, out = refs[:-1], refs[-1]
    pieces = [stack[index] for stack in stacks for index in range(stack.shape[0])]
    out[...] = jnp.dot(
        jnp.concatenate(pieces, axis=1), tokens[...], preferred_element_type=F32
    ).astype(out.dtype)


def project(tokens, entries):
    features, rows = tokens.shape
    width, depth = entries[0][0].shape[1:]
    tile, part = min(256, width), rows // 2
    cell = lambda block, count: pl.BlockSpec((count, tile, depth), lambda t, i: (block, i, 0))
    return pl.pallas_call(
        project_kernel,
        out_shape=jax.ShapeDtypeStruct((width, rows), BF16),
        grid=(2, width // tile),
        in_specs=[pl.BlockSpec((features, part), lambda t, i: (0, t))]
        + [cell(block, count) for _, block, count in entries],
        out_specs=pl.BlockSpec((tile, part), lambda t, i: (i, t)),
        compiler_params=pltpu.CompilerParams(vmem_limit_bytes=VMEM_LIMIT),
        cost_estimate=pl.CostEstimate(
            flops=2 * width * rows * features,
            bytes_accessed=2 * ((2 * width + rows) * features + width * rows),
            transcendentals=0,
        ),
    )(tokens, *[stack for stack, _, _ in entries])


def featurize(rim, value, coefficients, first, span):
    wide = jnp.concatenate([rim, value], axis=1).astype(F32)
    total = coefficients[:, first : first + 1] * wide
    for offset in range(1, span):
        total = total + coefficients[:, first + offset : first + offset + 1] * pltpu.roll(
            wide, offset, 1
        )
    return total[:, rim.shape[1] :]


def filter_kernel(span, k, v, k_rim, v_rim, before, coefficients, bands, out):
    coef = coefficients[...]
    first = featurize(k_rim[...], k[...], coef, span, span)
    second = featurize(v_rim[...], v[...], coef, 2 * span, span)
    gated = (first * second).astype(BF16)
    wide = jnp.concatenate([before[...], gated], axis=1)
    groups, reach, taps = bands.shape
    size = wide.shape[0] // groups
    blocks = gated.shape[1] // taps
    for group in range(groups):
        rows = slice(group * size, (group + 1) * size)
        windows = jnp.concatenate(
            [wide[rows, block * taps : block * taps + reach] for block in range(blocks)], axis=0
        )
        sums = jnp.dot(windows, bands[group], preferred_element_type=F32)
        gain = coef[rows, 3 * span : 3 * span + 1]
        for block in range(blocks):
            lanes = slice(block * taps, (block + 1) * taps)
            out[rows, lanes] = sums[block * size : (block + 1) * size] + gain * gated[
                rows, lanes
            ].astype(F32)


def long_filter_part(span, k, v, k_rim, v_rim, before, coefficients, bands):
    width, rows = k.shape
    groups, reach, taps = bands.shape
    tile, part = min(128, width), rows // 2
    cell = lambda size: pl.BlockSpec((tile, size), lambda i, t: (i, t))
    return pl.pallas_call(
        functools.partial(filter_kernel, span),
        out_shape=jax.ShapeDtypeStruct((width, rows), F32),
        grid=(width // tile, 2),
        in_specs=[cell(part), cell(part), cell(taps), cell(taps), cell(taps)]
        + [
            pl.BlockSpec((tile, coefficients.shape[1]), lambda i, t: (i, 0)),
            pl.BlockSpec((groups * tile // width, reach, taps), lambda i, t: (i, 0, 0)),
        ],
        out_specs=cell(part),
        compiler_params=pltpu.CompilerParams(vmem_limit_bytes=VMEM_LIMIT),
        cost_estimate=pl.CostEstimate(
            flops=2 * width * rows * (reach + 4 * span),
            bytes_accessed=8 * width * rows + 2 * groups * reach * taps,
            transcendentals=0,
        ),
    )(k, v, k_rim, v_rim, before, coefficients, bands)


def mix_kernel(span, q, q_rim, filtered, coefficients, out):
    features = featurize(q_rim[...], q[...], coefficients[...], 0, span)
    out[...] = (features * filtered[...]).T.astype(BF16)


def mix(span, q, q_rim, filtered, coefficients):
    width, rows = q.shape
    tile, part = min(128, width), rows // 2
    cell = lambda size: pl.BlockSpec((tile, size), lambda i, t: (i, t))
    return pl.pallas_call(
        functools.partial(mix_kernel, span),
        out_shape=jax.ShapeDtypeStruct((rows, width), BF16),
        grid=(width // tile, 2),
        in_specs=[
            cell(part),
            cell(q_rim.shape[1] // 2),
            cell(part),
            pl.BlockSpec((tile, coefficients.shape[1]), lambda i, t: (i, 0)),
        ],
        out_specs=pl.BlockSpec((part, tile), lambda i, t: (t, i)),
        compiler_params=pltpu.CompilerParams(vmem_limit_bytes=VMEM_LIMIT),
        cost_estimate=pl.CostEstimate(
            flops=2 * width * rows * span, bytes_accessed=8 * width * rows, transcendentals=0
        ),
    )(q, q_rim, filtered, coefficients)


def output_kernel(count, chunks, order, *refs):
    mixed, stacks, outs = refs[:count], refs[count:-chunks], refs[-chunks:]
    left = jnp.concatenate([ref[...] for ref in mixed], axis=1)
    pieces = [stack[index] for stack in stacks for index in range(stack.shape[0])]
    width = outs[0].shape[2]
    for place, piece in enumerate(pieces):
        sums = jnp.dot(left, piece, preferred_element_type=F32)
        for c, out in enumerate(outs):
            out[order[place]] = sums[:, c * width : (c + 1) * width].astype(out.dtype)


def output_sums(order, mixed, stacks, chunks):
    rows, part = mixed[0].shape
    depth, share = stacks[0].shape[1:]
    width = share // chunks
    blocks = sum(stack.shape[0] for stack in stacks)
    tile = min(256, rows)
    return pl.pallas_call(
        functools.partial(output_kernel, len(mixed), chunks),
        out_shape=[jax.ShapeDtypeStruct((blocks, rows, width), BF16)] * chunks,
        grid_spec=pltpu.PrefetchScalarGridSpec(
            num_scalar_prefetch=1,
            grid=(rows // tile,),
            in_specs=[pl.BlockSpec((tile, part), lambda i, o: (i, 0))] * len(mixed)
            + [pl.BlockSpec(stack.shape, lambda i, o: (0, 0, 0)) for stack in stacks],
            out_specs=[pl.BlockSpec((blocks, tile, width), lambda i, o: (0, i, 0))] * chunks,
        ),
        compiler_params=pltpu.CompilerParams(vmem_limit_bytes=VMEM_LIMIT),
        cost_estimate=pl.CostEstimate(
            flops=2 * rows * depth * blocks * share,
            bytes_accessed=2 * (rows * depth + depth * blocks * share + rows * blocks * share),
            transcendentals=0,
        ),
    )(order, *mixed, *stacks)


def bands_of(filters):
    taps = filters.shape[1]
    source = jnp.arange(taps)[:, None]
    target = jnp.arange(taps)[None, :]
    distance = (target - source) % taps
    picker = (distance[None] == jnp.arange(taps)[:, None, None]).astype(BF16)
    full = jnp.einsum("gk,kji->gji", filters, picker, preferred_element_type=F32)
    same = target >= source
    before, current = jnp.where(same, 0.0, full), jnp.where(same, full, 0.0)
    return jnp.concatenate([before, current], axis=1).astype(BF16)


def tail_gate(k, v, taps_k, taps_v, reach, end):
    span = taps_k.shape[0]

    def features(value, taps):
        wide = value[:, end - reach - span + 1 : end].astype(F32)
        total = taps[0][:, None] * wide[:, span - 1 :]
        for offset in range(1, span):
            start = span - 1 - offset
            total = total + taps[offset][:, None] * wide[:, start : start + reach]
        return total

    return (features(k, taps_k) * features(v, taps_v)).astype(BF16)


def pick(value, index, axis):
    return lax.dynamic_index_in_dim(value, index, axis, keepdims=False)


def per_device(
    places, tokens, qkv_weight, short_filter, long_filter, decay_rate, skip_gain, out_weight
):
    rows, in_features = tokens.shape
    depth, width = qkv_weight.shape[1:]
    features = out_weight.shape[1]
    groups, taps = long_filter.shape
    span = short_filter.shape[1]
    ny, nx, nz = places.ny, places.nx, places.nz
    i, j = lax.axis_index("ctx"), lax.axis_index("tp")
    x, zl = i % nx, (i // nx) % 2
    y, core = j // 2, j % 2
    half = width // 2
    share = features // 2
    chunks = 2 if share >= 256 else 1
    chunk = share // chunks
    order = [i ^ step for step in range(nx)]
    order += [(i - x + step) ^ m for step in range(nx) for m in places.masks()]
    order = jnp.stack(order).astype(jnp.int32)
    flags = jnp.stack([zl, j]).astype(jnp.int32)
    line = Line(places)

    def halves(s):
        return [
            lax.dynamic_slice_in_dim(qkv_weight[s], part * half, half, 1).T
            for part in (zl, 1 - zl)
        ]

    q_parts, k_parts, v_parts = (halves(s) for s in range(3))
    own = jnp.stack([q_parts[0], k_parts[0], v_parts[0]])
    beside = line.beside(own)

    size = in_features // places.tp
    parts = [
        {
            0: places.flip(
                lax.dynamic_slice_in_dim(tokens, j * size + h * (size // 2), size // 2, 1), ctx=nx
            )
        }
        for h in range(2)
    ]
    out_halves = out_weight.reshape(width, 2, share)
    rows_of = [pick(out_halves, core, 1), places.flip(pick(out_halves, 1 - core, 1), tp=1)]
    both = jnp.stack(rows_of).reshape(2, 2, half, share)
    out_own, out_other = (pick(both, part, 1).reshape(width, share) for part in (zl, 1 - zl))
    k_held = line.gather(*k_parts, parts[0][0], *beside, rows_of[1])
    for part in parts:
        for step in range(1, ny):
            part[2 * step] = places.flip(part[0], tp=2 * step)
    k_cross = line.cross(k_held)

    v_held = line.gather(*v_parts, parts[1][0], *parts[0].values())
    v_cross = line.cross(v_held)
    q_held = line.begin(*q_parts)
    for part, done in zip(parts, ((), (q_held[nz - 1],))):
        for mask in list(part):
            part[mask ^ 1] = places.flip(after(part[mask], *done), tp=1)
    tokens = prepare(
        order,
        flags,
        tokens,
        [part[mask] for mask in range(places.tp) for part in parts],
        depth,
    )
    q_held = line.finish(q_held, *q_parts, tokens)
    q_cross = line.cross(q_held)
    out_beside = line.beside(out_own)

    def entries(s, crossed):
        return [(stack, s, 1) for stack in [own] + beside] + [(crossed, 0, crossed.shape[0])]

    k = project(tokens, entries(1, k_cross))
    u = project(tokens, entries(2, v_cross))
    out_held = line.gather(out_own, out_other, k, u, *out_beside)
    outs = [stack[None] for stack in [out_own] + out_beside]
    outs.append(line.cross(out_held, u))

    tap_index = jnp.arange(taps, dtype=F32)
    filters = (long_filter * jnp.exp(-decay_rate[:, None] * tap_index[None, :])).astype(BF16)
    bands = bands_of(lax.dynamic_slice_in_dim(filters, zl * (groups // 2), groups // 2))
    short = lax.dynamic_slice_in_dim(short_filter, zl * half, half, 2)
    gain = lax.dynamic_slice_in_dim(skip_gain, zl * half, half)
    coefficients = jnp.concatenate([short.reshape(3 * span, half), gain[None, :]]).T
    coefficients = jnp.pad(coefficients, ((0, 0), (0, (-3 * span - 1) % 8)))

    def halos(tails, *done):
        beside = places.send(tails, lambda i, j: (i - i % nx + (i + 1) % nx, j))
        below = places.send(
            tails[1],
            lambda i, j: (i + 2 * nx - nx + 1, j)
            if i % nx == nx - 1 and i + 2 * nx < places.ctx
            else None,
        )
        beside, below = after(beside, *done), after(below, *done)
        start = x == 0
        return [jnp.where(start, below, beside[0]), jnp.where(start, beside[0], beside[1])]

    def rim_of(value):
        return jnp.pad(value.T, ((0, 0), (taps - value.shape[0], 0)))

    def rims(values):
        return jnp.concatenate([rim_of(value) for value in values], axis=1)

    edge = 8 * -(-(span - 1) // 8)
    ends = (rows, 2 * rows)
    tails = [
        jnp.concatenate(
            [
                tail_gate(k, u, short[1], short[2], taps, end).T,
                k[:, end - edge : end].T,
                u[:, end - edge : end].T,
            ]
        )
        for end in ends
    ]
    q = project(tokens, entries(0, after(q_cross, *out_held.values())))
    before = halos(jnp.stack(tails), q)
    edges = halos(jnp.stack([q[:, end - edge : end].T for end in ends]))
    filtered = long_filter_part(
        span,
        k,
        u,
        rims([value[taps : taps + edge] for value in before]),
        rims([value[taps + edge :] for value in before]),
        rims([value[:taps] for value in before]),
        after(coefficients, q),
        bands,
    )
    mixed = mix(span, q, rims(edges), filtered, coefficients)
    mixed = [mixed, places.flip(mixed, tp=1)]

    def over_y(value):
        total = pick(value, y, 1).astype(F32)
        for step in range(1, ny):
            total = total + places.flip(pick(value, y ^ step, 1), tp=2 * step).astype(F32)
        return total.astype(BF16)

    def over_z(value):
        other = places.flip(pick(value, 1 - zl, 1), ctx=nx)
        return (pick(value, zl, 1).astype(F32) + other.astype(F32)).astype(BF16)

    results = []
    blocks = places.ctx
    part = rows // ny
    for c, sums in enumerate(output_sums(order, mixed, outs, chunks)):
        if c + 1 < chunks or chunks == 1:
            value = sums.reshape(blocks * 2, ny, part, chunk)
            value = over_z(over_y(value).reshape(blocks, 2, part, chunk))
        else:
            value = over_z(sums.reshape(blocks, 2, rows, chunk))
            value = over_y(value.reshape(blocks, ny, part, chunk))
        value = value.reshape(blocks, 2, part // 2, chunk)
        mine = pick(value, core, 1)
        yours = places.flip(pick(value, 1 - core, 1), tp=1)
        pair = jnp.stack(
            [jnp.where(core == 0, mine, yours), jnp.where(core == 0, yours, mine)], axis=1
        )
        results.append(pair)
    result = jnp.stack(results, axis=2)
    return result.transpose(3, 0, 1, 2, 4).reshape(part // 2, -1)


def solution(mesh):
    in_specs = (
        P("ctx", None),
        P(None, "ctx", "tp"),
        P(None, None, "tp"),
        P("tp", None),
        P("tp"),
        P("tp"),
        P("tp", "ctx"),
    )
    places = Places(mesh.shape["ctx"], mesh.shape["tp"])
    return jax.shard_map(
        functools.partial(per_device, places),
        mesh=mesh,
        in_specs=in_specs,
        out_specs=P(AXES, None),
        check_vma=False,
    )
```

```python
import functools

import jax
import jax.numpy as jnp
from jax import lax
from jax.experimental import pallas as pl
from jax.experimental.pallas import tpu as pltpu
from jax.sharding import PartitionSpec as P

AXES = ("ctx", "tp")
BF16, F32 = jnp.bfloat16, jnp.float32
VMEM_LIMIT = 56 << 20


class Places:
    def __init__(self, ctx, tp):
        self.ctx, self.tp = ctx, tp
        self.nx = 1 << ((ctx.bit_length() - 1) // 2)
        self.nz = ctx // self.nx
        self.ny = tp // 2

    def send(self, value, target):
        pairs = []
        for i in range(self.ctx):
            for j in range(self.tp):
                to = target(i, j)
                if to is not None:
                    pairs.append((i * self.tp + j, to[0] * self.tp + to[1]))
        return lax.ppermute(value, AXES, pairs)

    def flip(self, value, ctx=0, tp=0):
        return self.send(value, lambda i, j: (i ^ ctx, j ^ tp))

    def masks(self):
        return [m * self.nx for m in range(1, self.nz)]


def after(value, *done):
    done = [entry for entry in done if entry is not None]
    return lax.optimization_barrier((value, *done))[0] if done else value


class Line:
    def __init__(self, places):
        self.places, self.far = places, []

    def step(self, value, mask, *done):
        result = self.places.flip(
            after(value, self.far[-3] if len(self.far) >= 3 else None, *done), ctx=mask
        )
        self.far.append(result)
        return result

    def gather(self, own, other, *last):
        return self.finish(self.begin(own, other), own, other, *last)

    def begin(self, own, other):
        masks = sorted(range(2, self.places.nz))
        return {m: self.step(other if m % 2 else own, m * self.places.nx) for m in masks}

    def finish(self, held, own, other, *last):
        return {**held, 1: self.step(other, self.places.nx, *last)}

    def beside(self, own):
        return [self.places.flip(own, ctx=step) for step in range(1, self.places.nx)]

    def cross(self, held, *done):
        nx, nz = self.places.nx, self.places.nz
        stack = after(jnp.stack([held[m] for m in range(1, nz)]), *done)
        groups = [[z * nx + x for x in range(nx)] for z in range(nz)]
        return lax.all_gather(stack, "ctx", axis_index_groups=groups, tiled=True)


def prepare_kernel(per_part, order, flags, own, *refs):
    parts, out = refs[:-1], refs[-1]
    part = order[pl.program_id(0)] // per_part
    quarter, which = part // 2, part % 2
    rows = own.shape[0]
    out[:, pl.ds(pl.multiple_of(flags[0] * rows, rows), rows)] = own[...].T
    for index, ref in enumerate(parts):

        @pl.when((quarter == flags[1] ^ (index // 2)) & (which == index % 2))
        def _():
            out[:, pl.ds(pl.multiple_of((1 - flags[0]) * rows, rows), rows)] = ref[...].T


def prepare(order, flags, own, parts, depth):
    rows, features = own.shape
    count = features // depth
    per_part = count // len(parts)
    return pl.pallas_call(
        functools.partial(prepare_kernel, per_part),
        out_shape=jax.ShapeDtypeStruct((features, 2 * rows), BF16),
        grid_spec=pltpu.PrefetchScalarGridSpec(
            num_scalar_prefetch=2,
            grid=(count,),
            in_specs=[pl.BlockSpec((rows, depth), lambda i, o, f: (0, o[i]))]
            + [pl.BlockSpec((rows, depth), lambda i, o, f: (0, o[i] % per_part))] * len(parts),
            out_specs=pl.BlockSpec((depth, 2 * rows), lambda i, o, f: (i, 0)),
        ),
        compiler_params=pltpu.CompilerParams(vmem_limit_bytes=VMEM_LIMIT),
        cost_estimate=pl.CostEstimate(
            flops=0, bytes_accessed=8 * rows * features, transcendentals=0
        ),
    )(order, flags, own, *parts)


def project_kernel(tokens, *refs):
    stacks, out = refs[:-1], refs[-1]
    pieces = [stack[index] for stack in stacks for index in range(stack.shape[0])]
    out[...] = jnp.dot(
        jnp.concatenate(pieces, axis=1), tokens[...], preferred_element_type=F32
    ).astype(out.dtype)


def project(tokens, entries):
    features, rows = tokens.shape
    width, depth = entries[0][0].shape[1:]
    tile, part = min(256, width), rows // 2
    cell = lambda block, count: pl.BlockSpec((count, tile, depth), lambda t, i: (block, i, 0))
    return pl.pallas_call(
        project_kernel,
        out_shape=jax.ShapeDtypeStruct((width, rows), BF16),
        grid=(2, width // tile),
        in_specs=[pl.BlockSpec((features, part), lambda t, i: (0, t))]
        + [cell(block, count) for _, block, count in entries],
        out_specs=pl.BlockSpec((tile, part), lambda t, i: (i, t)),
        compiler_params=pltpu.CompilerParams(vmem_limit_bytes=VMEM_LIMIT),
        cost_estimate=pl.CostEstimate(
            flops=2 * width * rows * features,
            bytes_accessed=2 * ((2 * width + rows) * features + width * rows),
            transcendentals=0,
        ),
    )(tokens, *[stack for stack, _, _ in entries])


def featurize(rim, value, coefficients, first, span):
    wide = jnp.concatenate([rim, value], axis=1).astype(F32)
    total = coefficients[:, first : first + 1] * wide
    for offset in range(1, span):
        total = total + coefficients[:, first + offset : first + offset + 1] * pltpu.roll(
            wide, offset, 1
        )
    return total[:, rim.shape[1] :]


def filter_kernel(span, k, v, k_rim, v_rim, before, coefficients, bands, out):
    coef = coefficients[...]
    first = featurize(k_rim[...], k[...], coef, span, span)
    second = featurize(v_rim[...], v[...], coef, 2 * span, span)
    gated = (first * second).astype(BF16)
    wide = jnp.concatenate([before[...], gated], axis=1)
    groups, reach, taps = bands.shape
    size = wide.shape[0] // groups
    blocks = gated.shape[1] // taps
    for group in range(groups):
        rows = slice(group * size, (group + 1) * size)
        windows = jnp.concatenate(
            [wide[rows, block * taps : block * taps + reach] for block in range(blocks)], axis=0
        )
        sums = jnp.dot(windows, bands[group], preferred_element_type=F32)
        gain = coef[rows, 3 * span : 3 * span + 1]
        for block in range(blocks):
            lanes = slice(block * taps, (block + 1) * taps)
            out[rows, lanes] = sums[block * size : (block + 1) * size] + gain * gated[
                rows, lanes
            ].astype(F32)


def long_filter_part(span, k, v, k_rim, v_rim, before, coefficients, bands):
    width, rows = k.shape
    groups, reach, taps = bands.shape
    tile, part = min(128, width), rows // 2
    cell = lambda size: pl.BlockSpec((tile, size), lambda i, t: (i, t))
    return pl.pallas_call(
        functools.partial(filter_kernel, span),
        out_shape=jax.ShapeDtypeStruct((width, rows), F32),
        grid=(width // tile, 2),
        in_specs=[cell(part), cell(part), cell(taps), cell(taps), cell(taps)]
        + [
            pl.BlockSpec((tile, coefficients.shape[1]), lambda i, t: (i, 0)),
            pl.BlockSpec((groups * tile // width, reach, taps), lambda i, t: (i, 0, 0)),
        ],
        out_specs=cell(part),
        compiler_params=pltpu.CompilerParams(vmem_limit_bytes=VMEM_LIMIT),
        cost_estimate=pl.CostEstimate(
            flops=2 * width * rows * (reach + 4 * span),
            bytes_accessed=8 * width * rows + 2 * groups * reach * taps,
            transcendentals=0,
        ),
    )(k, v, k_rim, v_rim, before, coefficients, bands)


def mix_kernel(span, q, q_rim, filtered, coefficients, out):
    features = featurize(q_rim[...], q[...], coefficients[...], 0, span)
    out[...] = (features * filtered[...]).T.astype(BF16)


def mix(span, q, q_rim, filtered, coefficients):
    width, rows = q.shape
    tile, part = min(128, width), rows // 2
    cell = lambda size: pl.BlockSpec((tile, size), lambda i, t: (i, t))
    return pl.pallas_call(
        functools.partial(mix_kernel, span),
        out_shape=jax.ShapeDtypeStruct((rows, width), BF16),
        grid=(width // tile, 2),
        in_specs=[
            cell(part),
            cell(q_rim.shape[1] // 2),
            cell(part),
            pl.BlockSpec((tile, coefficients.shape[1]), lambda i, t: (i, 0)),
        ],
        out_specs=pl.BlockSpec((part, tile), lambda i, t: (t, i)),
        compiler_params=pltpu.CompilerParams(vmem_limit_bytes=VMEM_LIMIT),
        cost_estimate=pl.CostEstimate(
            flops=2 * width * rows * span, bytes_accessed=8 * width * rows, transcendentals=0
        ),
    )(q, q_rim, filtered, coefficients)


def output_kernel(count, chunks, order, *refs):
    mixed, stacks, outs = refs[:count], refs[count:-chunks], refs[-chunks:]
    left = jnp.concatenate([ref[...] for ref in mixed], axis=1)
    pieces = [stack[index] for stack in stacks for index in range(stack.shape[0])]
    width = outs[0].shape[2]
    for place, piece in enumerate(pieces):
        sums = jnp.dot(left, piece, preferred_element_type=F32)
        for c, out in enumerate(outs):
            out[order[place]] = sums[:, c * width : (c + 1) * width].astype(out.dtype)


def output_sums(order, mixed, stacks, chunks):
    rows, part = mixed[0].shape
    depth, share = stacks[0].shape[1:]
    width = share // chunks
    blocks = sum(stack.shape[0] for stack in stacks)
    tile = min(256, rows)
    return pl.pallas_call(
        functools.partial(output_kernel, len(mixed), chunks),
        out_shape=[jax.ShapeDtypeStruct((blocks, rows, width), BF16)] * chunks,
        grid_spec=pltpu.PrefetchScalarGridSpec(
            num_scalar_prefetch=1,
            grid=(rows // tile,),
            in_specs=[pl.BlockSpec((tile, part), lambda i, o: (i, 0))] * len(mixed)
            + [pl.BlockSpec(stack.shape, lambda i, o: (0, 0, 0)) for stack in stacks],
            out_specs=[pl.BlockSpec((blocks, tile, width), lambda i, o: (0, i, 0))] * chunks,
        ),
        compiler_params=pltpu.CompilerParams(vmem_limit_bytes=VMEM_LIMIT),
        cost_estimate=pl.CostEstimate(
            flops=2 * rows * depth * blocks * share,
            bytes_accessed=2 * (rows * depth + depth * blocks * share + rows * blocks * share),
            transcendentals=0,
        ),
    )(order, *mixed, *stacks)


def bands_of(filters):
    taps = filters.shape[1]
    source = jnp.arange(taps)[:, None]
    target = jnp.arange(taps)[None, :]
    distance = (target - source) % taps
    picker = (distance[None] == jnp.arange(taps)[:, None, None]).astype(BF16)
    full = jnp.einsum("gk,kji->gji", filters, picker, preferred_element_type=F32)
    same = target >= source
    before, current = jnp.where(same, 0.0, full), jnp.where(same, full, 0.0)
    return jnp.concatenate([before, current], axis=1).astype(BF16)


def tail_gate(k, v, taps_k, taps_v, reach, end):
    span = taps_k.shape[0]

    def features(value, taps):
        wide = value[:, end - reach - span + 1 : end].astype(F32)
        total = taps[0][:, None] * wide[:, span - 1 :]
        for offset in range(1, span):
            start = span - 1 - offset
            total = total + taps[offset][:, None] * wide[:, start : start + reach]
        return total

    return (features(k, taps_k) * features(v, taps_v)).astype(BF16)


def pick(value, index, axis):
    return lax.dynamic_index_in_dim(value, index, axis, keepdims=False)


def per_device(
    places, tokens, qkv_weight, short_filter, long_filter, decay_rate, skip_gain, out_weight
):
    rows, in_features = tokens.shape
    depth, width = qkv_weight.shape[1:]
    features = out_weight.shape[1]
    groups, taps = long_filter.shape
    span = short_filter.shape[1]
    ny, nx, nz = places.ny, places.nx, places.nz
    i, j = lax.axis_index("ctx"), lax.axis_index("tp")
    x, zl = i % nx, (i // nx) % 2
    y, core = j // 2, j % 2
    half = width // 2
    share = features // 2
    chunks = 2 if share >= 256 else 1
    chunk = share // chunks
    order = [i ^ step for step in range(nx)]
    order += [(i - x + step) ^ m for step in range(nx) for m in places.masks()]
    order = jnp.stack(order).astype(jnp.int32)
    flags = jnp.stack([zl, j]).astype(jnp.int32)
    line = Line(places)

    def halves(s):
        return [
            lax.dynamic_slice_in_dim(qkv_weight[s], part * half, half, 1).T
            for part in (zl, 1 - zl)
        ]

    q_parts, k_parts, v_parts = (halves(s) for s in range(3))
    own = jnp.stack([q_parts[0], k_parts[0], v_parts[0]])
    beside = line.beside(own)

    size = in_features // places.tp
    parts = [
        {
            0: places.flip(
                lax.dynamic_slice_in_dim(tokens, j * size + h * (size // 2), size // 2, 1), ctx=nx
            )
        }
        for h in range(2)
    ]
    out_halves = out_weight.reshape(width, 2, share)
    rows_of = [pick(out_halves, core, 1), places.flip(pick(out_halves, 1 - core, 1), tp=1)]
    both = jnp.stack(rows_of).reshape(2, 2, half, share)
    out_own, out_other = (pick(both, part, 1).reshape(width, share) for part in (zl, 1 - zl))
    k_held = line.gather(*k_parts, parts[0][0], *beside, rows_of[1])
    for part in parts:
        for step in range(1, ny):
            part[2 * step] = places.flip(part[0], tp=2 * step)
    k_cross = line.cross(k_held)

    v_held = line.gather(*v_parts, parts[1][0], *parts[0].values())
    v_cross = line.cross(v_held)
    q_held = line.begin(*q_parts)
    for part, done in zip(parts, ((), (q_held[nz - 1],))):
        for mask in list(part):
            part[mask ^ 1] = places.flip(after(part[mask], *done), tp=1)
    tokens = prepare(
        order,
        flags,
        tokens,
        [part[mask] for mask in range(places.tp) for part in parts],
        depth,
    )
    q_held = line.finish(q_held, *q_parts, tokens)
    q_cross = line.cross(q_held)
    out_beside = line.beside(out_own)

    def entries(s, crossed):
        return [(stack, s, 1) for stack in [own] + beside] + [(crossed, 0, crossed.shape[0])]

    k = project(tokens, entries(1, k_cross))
    u = project(tokens, entries(2, v_cross))
    out_held = line.gather(out_own, out_other, k, u, *out_beside)
    outs = [stack[None] for stack in [out_own] + out_beside]
    outs.append(line.cross(out_held, u))

    tap_index = jnp.arange(taps, dtype=F32)
    filters = (long_filter * jnp.exp(-decay_rate[:, None] * tap_index[None, :])).astype(BF16)
    bands = bands_of(lax.dynamic_slice_in_dim(filters, zl * (groups // 2), groups // 2))
    short = lax.dynamic_slice_in_dim(short_filter, zl * half, half, 2)
    gain = lax.dynamic_slice_in_dim(skip_gain, zl * half, half)
    coefficients = jnp.concatenate([short.reshape(3 * span, half), gain[None, :]]).T
    coefficients = jnp.pad(coefficients, ((0, 0), (0, (-3 * span - 1) % 8)))

    def halos(tails, *done):
        beside = places.send(tails, lambda i, j: (i - i % nx + (i + 1) % nx, j))
        below = places.send(
            tails[1],
            lambda i, j: (i + 2 * nx - nx + 1, j)
            if i % nx == nx - 1 and i + 2 * nx < places.ctx
            else None,
        )
        beside, below = after(beside, *done), after(below, *done)
        start = x == 0
        return [jnp.where(start, below, beside[0]), jnp.where(start, beside[0], beside[1])]

    def rim_of(value):
        return jnp.pad(value.T, ((0, 0), (taps - value.shape[0], 0)))

    def rims(values):
        return jnp.concatenate([rim_of(value) for value in values], axis=1)

    edge = 8 * -(-(span - 1) // 8)
    ends = (rows, 2 * rows)
    tails = [
        jnp.concatenate(
            [
                tail_gate(k, u, short[1], short[2], taps, end).T,
                k[:, end - edge : end].T,
                u[:, end - edge : end].T,
            ]
        )
        for end in ends
    ]
    before = halos(jnp.stack(tails))
    q = project(tokens, entries(0, after(q_cross, *out_held.values(), *before)))
    edges = halos(jnp.stack([q[:, end - edge : end].T for end in ends]))
    filtered = long_filter_part(
        span,
        k,
        u,
        rims([value[taps : taps + edge] for value in before]),
        rims([value[taps + edge :] for value in before]),
        rims([value[:taps] for value in before]),
        after(coefficients, q),
        bands,
    )
    mixed = mix(span, q, rims(edges), filtered, coefficients)
    mixed = [mixed, places.flip(mixed, tp=1)]

    def over_y(value):
        total = pick(value, y, 1).astype(F32)
        for step in range(1, ny):
            total = total + places.flip(pick(value, y ^ step, 1), tp=2 * step).astype(F32)
        return total.astype(BF16)

    def over_z(value):
        other = places.flip(pick(value, 1 - zl, 1), ctx=nx)
        return (pick(value, zl, 1).astype(F32) + other.astype(F32)).astype(BF16)

    results = []
    blocks = places.ctx
    part = rows // ny
    for c, sums in enumerate(output_sums(order, mixed, outs, chunks)):
        if c + 1 < chunks or chunks == 1:
            value = sums.reshape(blocks * 2, ny, part, chunk)
            value = over_z(over_y(value).reshape(blocks, 2, part, chunk))
        else:
            value = over_z(sums.reshape(blocks, 2, rows, chunk))
            value = over_y(value.reshape(blocks, ny, part, chunk))
        value = value.reshape(blocks, 2, part // 2, chunk)
        mine = pick(value, core, 1)
        yours = places.flip(pick(value, 1 - core, 1), tp=1)
        pair = jnp.stack(
            [jnp.where(core == 0, mine, yours), jnp.where(core == 0, yours, mine)], axis=1
        )
        results.append(pair)
    result = jnp.stack(results, axis=2)
    return result.transpose(3, 0, 1, 2, 4).reshape(part // 2, -1)


def solution(mesh):
    in_specs = (
        P("ctx", None),
        P(None, "ctx", "tp"),
        P(None, None, "tp"),
        P("tp", None),
        P("tp"),
        P("tp"),
        P("tp", "ctx"),
    )
    places = Places(mesh.shape["ctx"], mesh.shape["tp"])
    return jax.shard_map(
        functools.partial(per_device, places),
        mesh=mesh,
        in_specs=in_specs,
        out_specs=P(AXES, None),
        check_vma=False,
    )
```

```python
import functools

import jax
import jax.numpy as jnp
from jax import lax
from jax.experimental import pallas as pl
from jax.experimental.pallas import tpu as pltpu
from jax.sharding import PartitionSpec as P

AXES = ("ctx", "tp")
BF16, F32 = jnp.bfloat16, jnp.float32
VMEM_LIMIT = 56 << 20


class Places:
    def __init__(self, ctx, tp):
        self.ctx, self.tp = ctx, tp
        self.nx = 1 << ((ctx.bit_length() - 1) // 2)
        self.nz = ctx // self.nx
        self.ny = tp // 2

    def send(self, value, target):
        pairs = []
        for i in range(self.ctx):
            for j in range(self.tp):
                to = target(i, j)
                if to is not None:
                    pairs.append((i * self.tp + j, to[0] * self.tp + to[1]))
        return lax.ppermute(value, AXES, pairs)

    def flip(self, value, ctx=0, tp=0):
        return self.send(value, lambda i, j: (i ^ ctx, j ^ tp))

    def masks(self):
        return [m * self.nx for m in range(1, self.nz)]


def after(value, *done):
    done = [entry for entry in done if entry is not None]
    return lax.optimization_barrier((value, *done))[0] if done else value


class Line:
    def __init__(self, places):
        self.places, self.far = places, []

    def step(self, value, mask, *done):
        result = self.places.flip(
            after(value, self.far[-3] if len(self.far) >= 3 else None, *done), ctx=mask
        )
        self.far.append(result)
        return result

    def gather(self, own, other, *last):
        return self.finish(self.begin(own, other), own, other, *last)

    def begin(self, own, other):
        masks = sorted(range(2, self.places.nz))
        return {m: self.step(other if m % 2 else own, m * self.places.nx) for m in masks}

    def finish(self, held, own, other, *last):
        return {**held, 1: self.step(other, self.places.nx, *last)}

    def beside(self, own):
        return [self.places.flip(own, ctx=step) for step in range(1, self.places.nx)]

    def cross(self, held, *done):
        nx, nz = self.places.nx, self.places.nz
        stack = after(jnp.stack([held[m] for m in range(1, nz)]), *done)
        groups = [[z * nx + x for x in range(nx)] for z in range(nz)]
        return lax.all_gather(stack, "ctx", axis_index_groups=groups, tiled=True)


def prepare_kernel(per_part, order, flags, own, *refs):
    parts, out = refs[:-1], refs[-1]
    part = order[pl.program_id(0)] // per_part
    quarter, which = part // 2, part % 2
    rows = own.shape[0]
    out[:, pl.ds(pl.multiple_of(flags[0] * rows, rows), rows)] = own[...].T
    for index, ref in enumerate(parts):

        @pl.when((quarter == flags[1] ^ (index // 2)) & (which == index % 2))
        def _():
            out[:, pl.ds(pl.multiple_of((1 - flags[0]) * rows, rows), rows)] = ref[...].T


def prepare(order, flags, own, parts, depth):
    rows, features = own.shape
    count = features // depth
    per_part = count // len(parts)
    return pl.pallas_call(
        functools.partial(prepare_kernel, per_part),
        out_shape=jax.ShapeDtypeStruct((features, 2 * rows), BF16),
        grid_spec=pltpu.PrefetchScalarGridSpec(
            num_scalar_prefetch=2,
            grid=(count,),
            in_specs=[pl.BlockSpec((rows, depth), lambda i, o, f: (0, o[i]))]
            + [pl.BlockSpec((rows, depth), lambda i, o, f: (0, o[i] % per_part))] * len(parts),
            out_specs=pl.BlockSpec((depth, 2 * rows), lambda i, o, f: (i, 0)),
        ),
        compiler_params=pltpu.CompilerParams(vmem_limit_bytes=VMEM_LIMIT),
        cost_estimate=pl.CostEstimate(
            flops=0, bytes_accessed=8 * rows * features, transcendentals=0
        ),
    )(order, flags, own, *parts)


def project_kernel(tokens, *refs):
    stacks, out = refs[:-1], refs[-1]
    pieces = [stack[index] for stack in stacks for index in range(stack.shape[0])]
    out[...] = jnp.dot(
        jnp.concatenate(pieces, axis=1), tokens[...], preferred_element_type=F32
    ).astype(out.dtype)


def project(tokens, entries):
    features, rows = tokens.shape
    width, depth = entries[0][0].shape[1:]
    tile, part = min(256, width), rows // 2
    cell = lambda block, count: pl.BlockSpec((count, tile, depth), lambda t, i: (block, i, 0))
    return pl.pallas_call(
        project_kernel,
        out_shape=jax.ShapeDtypeStruct((width, rows), BF16),
        grid=(2, width // tile),
        in_specs=[pl.BlockSpec((features, part), lambda t, i: (0, t))]
        + [cell(block, count) for _, block, count in entries],
        out_specs=pl.BlockSpec((tile, part), lambda t, i: (i, t)),
        compiler_params=pltpu.CompilerParams(vmem_limit_bytes=VMEM_LIMIT),
        cost_estimate=pl.CostEstimate(
            flops=2 * width * rows * features,
            bytes_accessed=2 * ((2 * width + rows) * features + width * rows),
            transcendentals=0,
        ),
    )(tokens, *[stack for stack, _, _ in entries])


def featurize(rim, value, coefficients, first, span):
    wide = jnp.concatenate([rim, value], axis=1).astype(F32)
    total = coefficients[:, first : first + 1] * wide
    for offset in range(1, span):
        total = total + coefficients[:, first + offset : first + offset + 1] * pltpu.roll(
            wide, offset, 1
        )
    return total[:, rim.shape[1] :]


def filter_kernel(span, k, v, k_rim, v_rim, before, coefficients, bands, out):
    coef = coefficients[...]
    first = featurize(k_rim[...], k[...], coef, span, span)
    second = featurize(v_rim[...], v[...], coef, 2 * span, span)
    gated = (first * second).astype(BF16)
    wide = jnp.concatenate([before[...], gated], axis=1)
    groups, reach, taps = bands.shape
    size = wide.shape[0] // groups
    blocks = gated.shape[1] // taps
    for group in range(groups):
        rows = slice(group * size, (group + 1) * size)
        windows = jnp.concatenate(
            [wide[rows, block * taps : block * taps + reach] for block in range(blocks)], axis=0
        )
        sums = jnp.dot(windows, bands[group], preferred_element_type=F32)
        gain = coef[rows, 3 * span : 3 * span + 1]
        for block in range(blocks):
            lanes = slice(block * taps, (block + 1) * taps)
            out[rows, lanes] = sums[block * size : (block + 1) * size] + gain * gated[
                rows, lanes
            ].astype(F32)


def long_filter_part(span, k, v, k_rim, v_rim, before, coefficients, bands):
    width, rows = k.shape
    groups, reach, taps = bands.shape
    tile, part = min(128, width), rows // 2
    cell = lambda size: pl.BlockSpec((tile, size), lambda i, t: (i, t))
    return pl.pallas_call(
        functools.partial(filter_kernel, span),
        out_shape=jax.ShapeDtypeStruct((width, rows), F32),
        grid=(width // tile, 2),
        in_specs=[cell(part), cell(part), cell(taps), cell(taps), cell(taps)]
        + [
            pl.BlockSpec((tile, coefficients.shape[1]), lambda i, t: (i, 0)),
            pl.BlockSpec((groups * tile // width, reach, taps), lambda i, t: (i, 0, 0)),
        ],
        out_specs=cell(part),
        compiler_params=pltpu.CompilerParams(vmem_limit_bytes=VMEM_LIMIT),
        cost_estimate=pl.CostEstimate(
            flops=2 * width * rows * (reach + 4 * span),
            bytes_accessed=8 * width * rows + 2 * groups * reach * taps,
            transcendentals=0,
        ),
    )(k, v, k_rim, v_rim, before, coefficients, bands)


def mix_kernel(span, q, q_rim, filtered, coefficients, out):
    features = featurize(q_rim[...], q[...], coefficients[...], 0, span)
    out[...] = (features * filtered[...]).T.astype(BF16)


def mix(span, q, q_rim, filtered, coefficients):
    width, rows = q.shape
    tile, part = min(128, width), rows // 2
    cell = lambda size: pl.BlockSpec((tile, size), lambda i, t: (i, t))
    return pl.pallas_call(
        functools.partial(mix_kernel, span),
        out_shape=jax.ShapeDtypeStruct((rows, width), BF16),
        grid=(width // tile, 2),
        in_specs=[
            cell(part),
            cell(q_rim.shape[1] // 2),
            cell(part),
            pl.BlockSpec((tile, coefficients.shape[1]), lambda i, t: (i, 0)),
        ],
        out_specs=pl.BlockSpec((part, tile), lambda i, t: (t, i)),
        compiler_params=pltpu.CompilerParams(vmem_limit_bytes=VMEM_LIMIT),
        cost_estimate=pl.CostEstimate(
            flops=2 * width * rows * span, bytes_accessed=8 * width * rows, transcendentals=0
        ),
    )(q, q_rim, filtered, coefficients)


def output_kernel(count, chunks, order, *refs):
    mixed, stacks, outs = refs[:count], refs[count:-chunks], refs[-chunks:]
    left = jnp.concatenate([ref[...] for ref in mixed], axis=1)
    pieces = [stack[index] for stack in stacks for index in range(stack.shape[0])]
    width = outs[0].shape[2]
    for place, piece in enumerate(pieces):
        sums = jnp.dot(left, piece, preferred_element_type=F32)
        for c, out in enumerate(outs):
            out[order[place]] = sums[:, c * width : (c + 1) * width].astype(out.dtype)


def output_sums(order, mixed, stacks, chunks):
    rows, part = mixed[0].shape
    depth, share = stacks[0].shape[1:]
    width = share // chunks
    blocks = sum(stack.shape[0] for stack in stacks)
    tile = min(256, rows)
    return pl.pallas_call(
        functools.partial(output_kernel, len(mixed), chunks),
        out_shape=[jax.ShapeDtypeStruct((blocks, rows, width), BF16)] * chunks,
        grid_spec=pltpu.PrefetchScalarGridSpec(
            num_scalar_prefetch=1,
            grid=(rows // tile,),
            in_specs=[pl.BlockSpec((tile, part), lambda i, o: (i, 0))] * len(mixed)
            + [pl.BlockSpec(stack.shape, lambda i, o: (0, 0, 0)) for stack in stacks],
            out_specs=[pl.BlockSpec((blocks, tile, width), lambda i, o: (0, i, 0))] * chunks,
        ),
        compiler_params=pltpu.CompilerParams(vmem_limit_bytes=VMEM_LIMIT),
        cost_estimate=pl.CostEstimate(
            flops=2 * rows * depth * blocks * share,
            bytes_accessed=2 * (rows * depth + depth * blocks * share + rows * blocks * share),
            transcendentals=0,
        ),
    )(order, *mixed, *stacks)


def bands_of(filters):
    taps = filters.shape[1]
    source = jnp.arange(taps)[:, None]
    target = jnp.arange(taps)[None, :]
    distance = (target - source) % taps
    picker = (distance[None] == jnp.arange(taps)[:, None, None]).astype(BF16)
    full = jnp.einsum("gk,kji->gji", filters, picker, preferred_element_type=F32)
    same = target >= source
    before, current = jnp.where(same, 0.0, full), jnp.where(same, full, 0.0)
    return jnp.concatenate([before, current], axis=1).astype(BF16)


def tail_gate(k, v, taps_k, taps_v, reach, end):
    span = taps_k.shape[0]

    def features(value, taps):
        wide = value[:, end - reach - span + 1 : end].astype(F32)
        total = taps[0][:, None] * wide[:, span - 1 :]
        for offset in range(1, span):
            start = span - 1 - offset
            total = total + taps[offset][:, None] * wide[:, start : start + reach]
        return total

    return (features(k, taps_k) * features(v, taps_v)).astype(BF16)


def pick(value, index, axis):
    return lax.dynamic_index_in_dim(value, index, axis, keepdims=False)


def per_device(
    places, tokens, qkv_weight, short_filter, long_filter, decay_rate, skip_gain, out_weight
):
    rows, in_features = tokens.shape
    depth, width = qkv_weight.shape[1:]
    features = out_weight.shape[1]
    groups, taps = long_filter.shape
    span = short_filter.shape[1]
    ny, nx, nz = places.ny, places.nx, places.nz
    i, j = lax.axis_index("ctx"), lax.axis_index("tp")
    x, zl = i % nx, (i // nx) % 2
    y, core = j // 2, j % 2
    half = width // 2
    share = features // 2
    chunks = 2 if share >= 256 else 1
    chunk = share // chunks
    order = [i ^ step for step in range(nx)]
    order += [(i - x + step) ^ m for step in range(nx) for m in places.masks()]
    order = jnp.stack(order).astype(jnp.int32)
    flags = jnp.stack([zl, j]).astype(jnp.int32)
    line = Line(places)

    def halves(s):
        return [
            lax.dynamic_slice_in_dim(qkv_weight[s], part * half, half, 1).T
            for part in (zl, 1 - zl)
        ]

    q_parts, k_parts, v_parts = (halves(s) for s in range(3))
    own = jnp.stack([q_parts[0], k_parts[0], v_parts[0]])
    beside = line.beside(own)

    size = in_features // places.tp
    parts = [
        {
            0: places.flip(
                lax.dynamic_slice_in_dim(tokens, j * size + h * (size // 2), size // 2, 1), ctx=nx
            )
        }
        for h in range(2)
    ]
    out_halves = out_weight.reshape(width, 2, share)
    rows_of = [pick(out_halves, core, 1), places.flip(pick(out_halves, 1 - core, 1), tp=1)]
    both = jnp.stack(rows_of).reshape(2, 2, half, share)
    out_own, out_other = (pick(both, part, 1).reshape(width, share) for part in (zl, 1 - zl))
    k_held = line.gather(*k_parts, parts[0][0], *beside, rows_of[1])
    for part in parts:
        for step in range(1, ny):
            part[2 * step] = places.flip(part[0], tp=2 * step)
    k_cross = line.cross(k_held)

    v_held = line.gather(*v_parts, parts[1][0], *parts[0].values())
    v_cross = line.cross(v_held)
    q_held = line.begin(*q_parts)
    for part, done in zip(parts, ((), (q_held[nz - 1],))):
        for mask in list(part):
            part[mask ^ 1] = places.flip(after(part[mask], *done), tp=1)
    tokens = prepare(
        order,
        flags,
        tokens,
        [part[mask] for mask in range(places.tp) for part in parts],
        depth,
    )
    q_held = line.finish(q_held, *q_parts, tokens)
    q_cross = line.cross(q_held)
    out_beside = line.beside(out_own)

    def entries(s, crossed):
        return [(stack, s, 1) for stack in [own] + beside] + [(crossed, 0, crossed.shape[0])]

    k = project(tokens, entries(1, k_cross))
    u = project(tokens, entries(2, v_cross))
    out_held = line.gather(out_own, out_other, k, u, *out_beside)
    outs = [stack[None] for stack in [out_own] + out_beside]
    outs.append(line.cross(out_held, u))

    tap_index = jnp.arange(taps, dtype=F32)
    filters = (long_filter * jnp.exp(-decay_rate[:, None] * tap_index[None, :])).astype(BF16)
    bands = bands_of(lax.dynamic_slice_in_dim(filters, zl * (groups // 2), groups // 2))
    short = lax.dynamic_slice_in_dim(short_filter, zl * half, half, 2)
    gain = lax.dynamic_slice_in_dim(skip_gain, zl * half, half)
    coefficients = jnp.concatenate([short.reshape(3 * span, half), gain[None, :]]).T
    coefficients = jnp.pad(coefficients, ((0, 0), (0, (-3 * span - 1) % 8)))

    def halos(tails, *done):
        beside = places.send(tails, lambda i, j: (i - i % nx + (i + 1) % nx, j))
        below = places.send(
            tails[1],
            lambda i, j: (i + 2 * nx - nx + 1, j)
            if i % nx == nx - 1 and i + 2 * nx < places.ctx
            else None,
        )
        beside, below = after(beside, *done), after(below, *done)
        start = x == 0
        return [jnp.where(start, below, beside[0]), jnp.where(start, beside[0], beside[1])]

    def rim_of(value):
        return jnp.pad(value.T, ((0, 0), (taps - value.shape[0], 0)))

    def rims(values):
        return jnp.concatenate([rim_of(value) for value in values], axis=1)

    edge = 8 * -(-(span - 1) // 8)
    ends = (rows, 2 * rows)
    tails = [
        jnp.concatenate(
            [
                tail_gate(k, u, short[1], short[2], taps, end).T,
                k[:, end - edge : end].T,
                u[:, end - edge : end].T,
            ]
        )
        for end in ends
    ]
    q = project(tokens, entries(0, after(q_cross, *out_held.values())))
    before = halos(jnp.stack(tails), q)
    edges = halos(jnp.stack([q[:, end - edge : end].T for end in ends]))
    filtered = long_filter_part(
        span,
        k,
        u,
        rims([value[taps : taps + edge] for value in before]),
        rims([value[taps + edge :] for value in before]),
        rims([value[:taps] for value in before]),
        after(coefficients, q),
        bands,
    )
    mixed = mix(span, q, rims(edges), filtered, after(coefficients, outs[-1]))
    mixed = [mixed, places.flip(mixed, tp=1)]

    def over_y(value):
        total = pick(value, y, 1).astype(F32)
        for step in range(1, ny):
            total = total + places.flip(pick(value, y ^ step, 1), tp=2 * step).astype(F32)
        return total.astype(BF16)

    def over_z(value):
        other = places.flip(pick(value, 1 - zl, 1), ctx=nx)
        return (pick(value, zl, 1).astype(F32) + other.astype(F32)).astype(BF16)

    results = []
    blocks = places.ctx
    part = rows // ny
    for c, sums in enumerate(output_sums(order, mixed, outs, chunks)):
        if c + 1 < chunks or chunks == 1:
            value = sums.reshape(blocks * 2, ny, part, chunk)
            value = over_z(over_y(value).reshape(blocks, 2, part, chunk))
        else:
            value = over_z(sums.reshape(blocks, 2, rows, chunk))
            value = over_y(value.reshape(blocks, ny, part, chunk))
        value = value.reshape(blocks, 2, part // 2, chunk)
        mine = pick(value, core, 1)
        yours = places.flip(pick(value, 1 - core, 1), tp=1)
        pair = jnp.stack(
            [jnp.where(core == 0, mine, yours), jnp.where(core == 0, yours, mine)], axis=1
        )
        results.append(pair)
    result = jnp.stack(results, axis=2)
    return result.transpose(3, 0, 1, 2, 4).reshape(part // 2, -1)


def solution(mesh):
    in_specs = (
        P("ctx", None),
        P(None, "ctx", "tp"),
        P(None, None, "tp"),
        P("tp", None),
        P("tp"),
        P("tp"),
        P("tp", "ctx"),
    )
    places = Places(mesh.shape["ctx"], mesh.shape["tp"])
    return jax.shard_map(
        functools.partial(per_device, places),
        mesh=mesh,
        in_specs=in_specs,
        out_specs=P(AXES, None),
        check_vma=False,
    )
```
